128 devices in a mesh: gx: 8 (over z, core), gy: 16 (over y, x).
Axes of the slice: x: 4, y: 4, z: 4, core: 2. Of those that a mesh axis runs over, the one named last changes fastest.
Arguments:
- src_embed: bfloat16 [4096, 384, 128], P(('gx', 'gy')), may hold values from -3 to 3
- tgt_embed: bfloat16 [4096, 384, 128], P(('gx', 'gy')), may hold values from -3 to 3
- src_potential: bfloat16 [4096, 384], P(('gx', 'gy')), may hold values from -0.29882812 to 0.69921875
- tgt_potential: bfloat16 [4096, 384], P(('gx', 'gy')), may hold values from -0.29882812 to 0.69921875
- src_sizes: int32 [4096], P(('gx', 'gy')), may hold values from 1 to 384, 786432 in all
- tgt_sizes: int32 [4096], replicated, may hold values from 1 to 384, 786432 in all
- pair_counts: int32 [4096], replicated, may hold values from 2 to 4, as said below
- pairs: int32 [4096, 4], replicated, may hold values from 0 to 4095, as said below
Outputs:
- src_grad: float32 [4096, 384, 128], P(('gx', 'gy'))
- tgt_grad: float32 [4096, 384, 128], P(('gx', 'gy'))
The draws below stay inside these ranges and needn't reach their ends.
Inputs may be any that keep to these rules, and one draw needn't show every extreme that they name: `pairs`: source cluster c and target cluster t belong to the device of index c // 32 and t // 32 of gx+gy. Among the 128 entries of the source clusters of one device, used or not, at most 1 name target clusters of one device, and some device is named exactly 1 times. Among the used entries (k < pair_counts[c]) of one device, at most 1 name target clusters of one device, and some device is named exactly 1 times. `pair_counts`: the counts of the 32 source clusters of one device sum to exactly 96.
All inputs are finite; a program needn't handle non-finite values. No bound on the sum of `src_sizes` on one device may be relied on, other than what follows from the above.
Results may differ from the reference program's by a relative error of at most 0.0038.
Values may be sent and summed in bfloat16 or wider, within the bound.
No kernel may reach another device: no remote copies, remote signals or barrier semaphores. Data moves between devices by JAX's collectives and lax.ppermute only.
A program may use at most 192 MiB of HBM per device.

```python
import math
import jax
import jax.numpy as jnp
import numpy as np
from jax import lax

E = 128
CAP = 384
PAIRS = 4
SC_DEV = 32
SRC_CL = 4096
TGT_CL = 4096
DEVICES = 128


def common_counts(key):
    count_key = jax.random.fold_in(key, 5)
    delta_key, perm_key = jax.random.split(count_key)
    half = SC_DEV // 2
    delta = jax.random.randint(delta_key, (DEVICES, half), -1, 2)
    paired = jnp.concatenate([3 + delta, 3 - delta], axis=1)
    perm_keys = jax.random.split(perm_key, DEVICES)
    shuffled = jax.vmap(lambda one_key, row: jax.random.permutation(one_key, row))(perm_keys, paired)
    return shuffled.astype(jnp.int32)


def draw_pair_counts(key, part):
    counts = common_counts(key)
    return counts.reshape(SRC_CL).astype(jnp.int32)


def draw_pairs(key, part):
    counts = common_counts(key)
    key = jax.random.fold_in(key, 11)
    key_owner, key_local = jax.random.split(key)
    listed = SC_DEV * PAIRS
    fan_ids = jnp.arange(PAIRS, dtype=jnp.int32)
    unused = (fan_ids[None, None, :] >= counts[:, :, None]).astype(jnp.int32)
    entry_ids = jnp.arange(listed, dtype=jnp.int32).reshape(1, SC_DEV, PAIRS)
    order_key = (unused * listed + entry_ids).reshape(DEVICES, listed)
    order = jnp.argsort(order_key, axis=1, stable=True)
    rank = jnp.argsort(order, axis=1, stable=True).astype(jnp.int32)
    owner_keys = jax.random.split(key_owner, DEVICES)
    devices_perm = jax.vmap(lambda one_key: jax.random.permutation(one_key, DEVICES))(owner_keys)
    owners = jnp.take_along_axis(devices_perm, rank % DEVICES, axis=1)
    local = jax.random.randint(key_local, (DEVICES, listed), 0, SC_DEV)
    return (owners * SC_DEV + local).reshape(SRC_CL, PAIRS).astype(jnp.int32)


def levels(rng, extent, cuts, low, top_value):
    level, own = 1.0, jax.random.fold_in(rng, 6)
    for axis_at, blocks in cuts:
        draws = jnp.exp(jax.random.uniform(jax.random.fold_in(own, axis_at), (blocks,), jnp.float32, low / len(cuts), top_value / len(cuts)))
        level = level * jnp.repeat(draws, extent[axis_at] // blocks).reshape([-1 if axis == axis_at else 1 for axis in range(len(extent))])
    return level


def profile(count, total, limit, skew):
    weights = [(1 << 20) // math.isqrt(standing ** skew) + 1 for standing in range(2, count + 1)]
    surplus, given = total - limit - (count - 1), [1] * (count - 1)
    while surplus > 0:
        movable = [i for i in range(count - 1) if given[i] < limit]
        mass, left = sum([weights[i] for i in movable]), surplus
        for i in movable:
            more = min(limit - given[i], max(1, left * weights[i] // mass), surplus)
            given[i] = given[i] + more
            surplus = surplus - more
    return np.array([limit] + given)


def uneven(stream_key, count, total, bound, slope):
    if count == 2:
        one = jax.random.randint(stream_key, (), max(1, total - bound), min(bound, total - 1) + 1)
        return jnp.stack([one, total - one])
    lengths = jnp.asarray(profile(count, total, bound, slope), jnp.int32)
    twos = (count - 1) // 2
    source_of, sink = lengths[1:1 + 2 * twos:2], lengths[2:2 + 2 * twos:2]
    margin = jnp.minimum(source_of - 1, bound - sink)
    shifted = jax.random.randint(jax.random.fold_in(stream_key, 1), (twos,), 0, 1 << 20) % (margin + 1)
    lengths = lengths.at[1:1 + 2 * twos:2].set(source_of - shifted).at[2:2 + 2 * twos:2].set(sink + shifted)
    return lengths[jax.random.permutation(jax.random.fold_in(stream_key, 2), count)]


def bell_draw(own_key, extent, deviation, bound, cuts=(), kind=jnp.bfloat16):
    drawn = deviation * jax.random.normal(own_key, extent, jnp.float32)
    if cuts:
        drawn = drawn * levels(own_key, extent, cuts, -0.22, 0.18)
    return jnp.clip(drawn, -bound, bound).astype(kind)


def setup_inputs(seed: int = 0) -> dict:
    arg_keys = jax.random.split(jax.random.key(seed), 9)
    src_embed = bell_draw(arg_keys[0], (SRC_CL, CAP, E), 0.5, 3.0, ((0, 128),))
    tgt_embed = bell_draw(arg_keys[1], (TGT_CL, CAP, E), 0.5, 3.0, ((0, 128),))
    src_potential = jnp.clip(-0.29882812 + 0.9980469 * jax.random.uniform(arg_keys[2], (SRC_CL, CAP), jnp.float32) ** levels(arg_keys[2], (SRC_CL, CAP), ((0, 128),), -0.2, 0.2), -0.29882812, 0.69921875).astype(jnp.bfloat16)
    tgt_potential = jnp.clip(-0.29882812 + 0.9980469 * jax.random.uniform(arg_keys[3], (TGT_CL, CAP), jnp.float32) ** levels(arg_keys[3], (TGT_CL, CAP), ((0, 128),), -0.2, 0.2), -0.29882812, 0.69921875).astype(jnp.bfloat16)
    src_sizes = uneven(arg_keys[4], SRC_CL, SRC_CL * CAP // 2, CAP, 2).astype(jnp.int32)
    tgt_sizes = uneven(arg_keys[5], TGT_CL, TGT_CL * CAP // 2, CAP, 2).astype(jnp.int32)
    pair_counts = draw_pair_counts(jax.random.fold_in(arg_keys[8], 71), 0)
    pairs = draw_pairs(jax.random.fold_in(arg_keys[8], 71), 0)
    return dict(src_embed=src_embed, tgt_embed=tgt_embed, src_potential=src_potential, tgt_potential=tgt_potential, src_sizes=src_sizes, tgt_sizes=tgt_sizes, pair_counts=pair_counts, pairs=pairs)


smoothing_epsilon = 0.5


def reference(src_embed, tgt_embed, src_potential, tgt_potential, src_sizes, tgt_sizes, pair_counts, pairs):
    scale = E ** -0.5
    row_ids = jnp.arange(CAP, dtype=jnp.int32)
    slot_ids = jnp.arange(PAIRS, dtype=jnp.int32)

    def one_cluster(carry, items):
        src_block, left_kantorovich_potential, src_size, count, target_ids = items
        tgt_block = tgt_embed[target_ids].reshape(PAIRS * CAP, E)
        right_kantorovich_potential = tgt_potential[target_ids].reshape(PAIRS * CAP).astype(jnp.float32)
        tgt_size = tgt_sizes[target_ids]
        valid_right_entity = ((row_ids[None, :] < tgt_size[:, None]) & (slot_ids[:, None] < count)).reshape(PAIRS * CAP)
        valid_left_entity = row_ids < src_size
        similarity_grid = jnp.dot(src_block, tgt_block.T, preferred_element_type=jnp.float32) * scale
        coupling_probabilities = jnp.exp((left_kantorovich_potential.astype(jnp.float32)[:, None] + right_kantorovich_potential[None, :] - (1.0 - similarity_grid)) / smoothing_epsilon)
        objective_factor = jnp.where(valid_left_entity[:, None] & valid_right_entity[None, :], coupling_probabilities * (1.0 - (1.0 - similarity_grid) / smoothing_epsilon), 0.0).astype(jnp.bfloat16)
        grad_src = -jnp.dot(objective_factor, tgt_block, preferred_element_type=jnp.float32) * scale
        grad_part = (-jnp.dot(objective_factor.T, src_block, preferred_element_type=jnp.float32) * scale).astype(jnp.bfloat16)
        carry = carry.at[target_ids].add(grad_part.reshape(PAIRS, CAP, E).astype(jnp.float32))
        return carry, grad_src

    start = jnp.zeros((TGT_CL, CAP, E), jnp.float32)
    tgt_grad, src_grad = lax.scan(one_cluster, start, (src_embed, src_potential, src_sizes, pair_counts, pairs))
    return src_grad, tgt_grad
```

```python
import functools
import math

import jax
import jax.numpy as jnp
from jax import lax
from jax.experimental import pallas as pl
from jax.experimental.pallas import tpu as pltpu
from jax.sharding import PartitionSpec as P

AXES = ("gx", "gy")
CHUNK = 16
TILE = 128
VMEM_BYTES = 60 * 1024 * 1024
DEAD = -1e30
epsilon = 0.5


def _params():
    return pltpu.CompilerParams(vmem_limit_bytes=VMEM_BYTES)


def _any():
    return pl.BlockSpec(memory_space=pl.ANY)


def _vmem():
    return pl.BlockSpec(memory_space=pltpu.VMEM)


def _smem():
    return pl.BlockSpec(memory_space=pltpu.SMEM)


def _rows(chunk):
    return pl.ds(pl.multiple_of(chunk * CHUNK, CHUNK), CHUNK)


def pack_kernel(slot_chunks, table, tgt_any, src_any, out, home, sems):
    half = tgt_any.shape[0]
    first = pltpu.make_async_copy(tgt_any, home.at[pl.ds(0, half)], sems.at[0])
    second = pltpu.make_async_copy(src_any, home.at[pl.ds(half, half)], sems.at[1])
    first.start()
    second.start()
    home[pl.ds(2 * half, CHUNK), :] = jnp.zeros((CHUNK, home.shape[1]), home.dtype)
    first.wait()
    second.wait()

    def slot(peer, carry):
        for p in range(slot_chunks):
            out[_rows(peer * slot_chunks + p), :] = home[_rows(table[p, peer]), :]
        return carry

    lax.fori_loop(0, table.shape[1], slot, 0)


def pack(table, tgt_rows, src_rows, slot_chunks):
    peers = table.shape[1]
    width = tgt_rows.shape[1]
    total = peers * slot_chunks * CHUNK
    return pl.pallas_call(
        functools.partial(pack_kernel, slot_chunks),
        out_shape=jax.ShapeDtypeStruct((total, width), tgt_rows.dtype),
        in_specs=[_smem(), _any(), _any()],
        out_specs=_vmem(),
        scratch_shapes=[
            pltpu.VMEM((2 * tgt_rows.shape[0] + CHUNK, width), tgt_rows.dtype),
            pltpu.SemaphoreType.DMA((2,)),
        ],
        compiler_params=_params(),
        name="pack",
    )(table, tgt_rows, src_rows)


def side_rows(potential, live, first):
    shape = (CHUNK, potential.shape[1])
    row = lax.broadcasted_iota(jnp.int32, shape, 0)
    lane = lax.broadcasted_iota(jnp.int32, shape, 1)
    dead = jnp.where(lane < live, 0.0, DEAD)
    pot = jnp.broadcast_to(potential, shape)
    own = 0 if first else 1
    other = 1 - own
    mine = 2 if first else 3
    rows = jnp.where(row == own, pot, jnp.where(row == mine, dead, 1.0))
    rows = jnp.where(row < 4, rows, 0.0)
    return rows.astype(jnp.bfloat16)


def compute_kernel(
    capacity,
    scale,
    desc,
    table,
    pots_in,
    pots_home,
    recv_any,
    tgt_any,
    src_any,
    ret_any,
    acc,
    recv,
    ret,
    home,
    moved,
    part,
    sems,
):
    width = home.shape[1]
    half = tgt_any.shape[0]
    total = recv_any.shape[0]
    copies = [
        pltpu.make_async_copy(tgt_any, home.at[pl.ds(0, half)], sems.at[0]),
        pltpu.make_async_copy(src_any, home.at[pl.ds(half, half)], sems.at[1]),
        pltpu.make_async_copy(recv_any, recv.at[pl.ds(0, total)], sems.at[2]),
    ]
    for copy in copies:
        copy.start()
    recv[pl.ds(total, CHUNK), :] = jnp.zeros((CHUNK, width), recv.dtype)
    moved[...] = jnp.zeros_like(moved)

    def clear(i, carry):
        at = pl.multiple_of(i * capacity, capacity)
        acc[pl.ds(at, capacity), :] = jnp.zeros((capacity, width), jnp.float32)
        return carry

    lax.fori_loop(0, acc.shape[0] // capacity, clear, 0)
    for copy in copies:
        copy.wait()
    log2e = math.log2(math.e)
    to_exp = log2e / epsilon

    def tiles(blocks, pair):
        home_id, live_moved, live_home, pot_at = pair
        count = (live_home + TILE - 1) // TILE
        right_pots = pots_in[pl.ds(pl.multiple_of(pot_at, 8), 8), :]
        left_pots = pots_home[pl.ds(pl.multiple_of(home_id * 8, 8), 8), :]
        span = blocks * TILE
        right = moved[0:span, :]
        right_side = jnp.concatenate(
            [
                side_rows(right_pots[b : b + 1, :], live_moved - b * TILE, False)
                for b in range(blocks)
            ],
            axis=1,
        )
        for i in range(capacity // TILE):

            @pl.when(i < count)
            def _():
                at = pl.multiple_of(home_id * capacity + i * TILE, TILE)
                left = home[pl.ds(at, TILE), :]
                left_side = side_rows(left_pots[i : i + 1, :], live_home - i * TILE, True)
                dots = lax.dot_general(
                    left, right, (((1,), (1,)), ((), ())), preferred_element_type=jnp.float32
                )
                sums = lax.dot_general(
                    left_side,
                    right_side,
                    (((0,), (0,)), ((), ())),
                    preferred_element_type=jnp.float32,
                )
                plan = jnp.exp2(dots * (scale * to_exp) + (sums * to_exp - to_exp))
                weight = (plan * (dots * (scale / epsilon) + (1.0 - 1.0 / epsilon))).astype(
                    jnp.bfloat16
                )
                acc[pl.ds(at, TILE), :] += (-scale) * jnp.dot(
                    weight, right, preferred_element_type=jnp.float32
                )
                piece = lax.dot_general(
                    weight, left, (((0,), (0,)), ((), ())), preferred_element_type=jnp.float32
                )
                if i == 0:
                    part[0:span, :] = piece
                else:
                    part[0:span, :] += piece

    def one(peer, kind):
        home_id = desc[4 * kind, peer]
        live_moved = desc[4 * kind + 1, peer]
        live_home = desc[4 * kind + 2, peer]
        start = desc[4 * kind + 3, peer]

        @pl.when(home_id >= 0)
        def _():
            pair = (home_id, live_moved, live_home, (peer * 2 + kind) * 8)
            blocks = (live_moved + TILE - 1) // TILE
            for b in range(capacity // TILE):

                @pl.when(b < blocks)
                def _():
                    for j in range(TILE // CHUNK):
                        at = b * (TILE // CHUNK) + j
                        moved[at * CHUNK : (at + 1) * CHUNK, :] = recv[
                            _rows(table[start + at, peer]), :
                        ]

            for b in range(1, capacity // TILE + 1):
                pl.when(blocks == b)(functools.partial(tiles, b, pair))
            for b in range(capacity // TILE):

                @pl.when(b < blocks)
                def _():
                    for j in range(TILE // CHUNK):
                        at = b * (TILE // CHUNK) + j
                        ret[_rows(table[start + at, peer]), :] = (
                            part[at * CHUNK : (at + 1) * CHUNK, :] * (-scale)
                        ).astype(ret.dtype)

    def peers(peer, carry):
        one(peer, 0)
        one(peer, 1)
        return carry

    lax.fori_loop(0, desc.shape[1], peers, 0)
    back = pltpu.make_async_copy(ret.at[pl.ds(0, total)], ret_any, sems.at[3])
    back.start()
    back.wait()


def compute(desc, table, pots_in, pots_home, recv, tgt_rows, src_rows, capacity):
    width = tgt_rows.shape[1]
    scale = width ** (-0.5)
    homes = 2 * tgt_rows.shape[0]
    return pl.pallas_call(
        functools.partial(compute_kernel, capacity, scale),
        out_shape=(
            jax.ShapeDtypeStruct(recv.shape, recv.dtype),
            jax.ShapeDtypeStruct((homes, width), jnp.float32),
        ),
        in_specs=[_smem(), _smem(), _vmem(), _vmem(), _any(), _any(), _any()],
        out_specs=(_any(), _vmem()),
        scratch_shapes=[
            pltpu.VMEM((recv.shape[0] + CHUNK, width), recv.dtype),
            pltpu.VMEM((recv.shape[0] + CHUNK, width), recv.dtype),
            pltpu.VMEM((homes, width), tgt_rows.dtype),
            pltpu.VMEM((capacity, width), tgt_rows.dtype),
            pltpu.VMEM((capacity, width), jnp.float32),
            pltpu.SemaphoreType.DMA((4,)),
        ],
        compiler_params=_params(),
        name="pairs",
    )(desc, table, pots_in, pots_home, recv, tgt_rows, src_rows)


def fold_kernel(slot_chunks, table, got, acc_any, tgt_any, src_any, acc, sems):
    homes = acc_any.shape[0]
    half = homes // 2
    first = pltpu.make_async_copy(acc_any, acc.at[pl.ds(0, homes)], sems.at[0])
    first.start()
    acc[pl.ds(homes, CHUNK), :] = jnp.zeros((CHUNK, acc.shape[1]), jnp.float32)
    first.wait()

    def slot(peer, carry):
        for p in range(slot_chunks):
            at = _rows(table[p, peer])
            acc[at, :] += got[_rows(peer * slot_chunks + p), :].astype(jnp.float32)
        return carry

    lax.fori_loop(0, table.shape[1], slot, 0)
    out = [
        pltpu.make_async_copy(acc.at[pl.ds(0, half)], tgt_any, sems.at[1]),
        pltpu.make_async_copy(acc.at[pl.ds(half, half)], src_any, sems.at[2]),
    ]
    for copy in out:
        copy.start()
    for copy in out:
        copy.wait()


def fold(table, got, acc, slot_chunks):
    homes, width = acc.shape
    result = jax.ShapeDtypeStruct((homes // 2, width), jnp.float32)
    return pl.pallas_call(
        functools.partial(fold_kernel, slot_chunks),
        out_shape=(result, result),
        in_specs=[_smem(), _vmem(), _any()],
        out_specs=(_any(), _any()),
        scratch_shapes=[
            pltpu.VMEM((homes + CHUNK, width), jnp.float32),
            pltpu.SemaphoreType.DMA((3,)),
        ],
        compiler_params=_params(),
        name="fold",
    )(table, got, acc)


def exchange(blocks, devices):
    shaped = blocks.reshape(devices, -1, blocks.shape[-1])
    got = lax.all_to_all(shaped, AXES, split_axis=0, concat_axis=0, tiled=True)
    return got.reshape(blocks.shape)


def shards(
    src_embed, tgt_embed, src_potential, tgt_potential, src_sizes, tgt_sizes, pair_counts, pairs
):
    devices = lax.axis_size(AXES)
    me = lax.axis_index(AXES)
    clusters, capacity, width = src_embed.shape
    fanout = pairs.shape[1]
    listed = pairs.reshape(devices, clusters * fanout)
    entry = jnp.arange(clusters * fanout, dtype=jnp.int32)
    used = (
        jnp.arange(fanout, dtype=jnp.int32)[None, None, :]
        < pair_counts.reshape(devices, clusters)[:, :, None]
    ).reshape(devices, clusters * fanout)
    peer_ids = jnp.arange(devices, dtype=jnp.int32)
    code = used.astype(jnp.int32) * (
        1 + 2 * (entry[None, :] // fanout) + 2 * clusters * (listed % clusters)
    )
    matrix = jnp.sum(
        jnp.where((listed // clusters)[:, :, None] == peer_ids[None, None, :], code[:, :, None], 0),
        axis=1,
    )
    mine = lax.dynamic_index_in_dim(matrix, me, 0, keepdims=False)
    theirs = lax.dynamic_index_in_dim(matrix, me, 1, keepdims=False)
    sizes = tgt_sizes.reshape(devices, clusters)
    own_sizes = lax.dynamic_index_in_dim(sizes, me, 0, keepdims=False)

    def split(value):
        return value % 2, (value // 2) % clusters, value // (2 * clusters)

    out_used, _, out_local = split(theirs)
    in_used, in_home, in_local = split(mine)
    cluster_ids = jnp.arange(clusters, dtype=jnp.int32)

    def pick(rows, at):
        return jnp.sum(jnp.where(at[:, None] == cluster_ids[None, :], rows, 0), axis=1)

    out_size = pick(own_sizes[None, :], out_local) * out_used
    in_size = pick(sizes, in_local) * in_used
    home_size = pick(src_sizes[None, :], in_home)

    chunks = capacity // CHUNK
    homes = 2 * clusters
    p = jnp.arange(chunks, dtype=jnp.int32)[:, None]
    out_table = jnp.where(
        p * CHUNK < out_size[None, :], out_local[None, :] * chunks + p, homes * chunks
    )
    q = jnp.arange(2 * chunks, dtype=jnp.int32)[:, None]
    in_table = jnp.where(
        q * CHUNK < in_size[None, :], peer_ids[None, :] * chunks + q, devices * chunks
    )
    none = jnp.full((devices,), -1, jnp.int32)
    zero = jnp.zeros((devices,), jnp.int32)
    desc = jnp.stack(
        [jnp.where(in_used > 0, clusters + in_home, -1), in_size, home_size, zero, none, zero, zero, zero]
    )
    tgt_rows = tgt_embed.reshape(clusters * capacity, width)
    src_rows = src_embed.reshape(clusters * capacity, width)
    header = jnp.take(tgt_potential, out_local, axis=0).reshape(devices, capacity // TILE, TILE)
    header = jnp.pad(header, ((0, 0), (0, 8 - capacity // TILE), (0, 0)))
    got_header = lax.all_to_all(header, AXES, split_axis=0, concat_axis=0, tiled=True)
    got_header = got_header.astype(jnp.float32)
    pots_in = jnp.stack([got_header, got_header], axis=1).reshape(devices * 16, TILE)
    pots_home = jnp.concatenate([tgt_potential, src_potential], axis=0).reshape(
        homes, capacity // TILE, TILE
    )
    pots_home = (
        jnp.pad(pots_home, ((0, 0), (0, 8 - capacity // TILE), (0, 0)))
        .astype(jnp.float32)
        .reshape(homes * 8, TILE)
    )
    sent = pack(out_table, tgt_rows, src_rows, chunks)
    recv = exchange(sent, devices)
    ret, acc = compute(desc, in_table, pots_in, pots_home, recv, tgt_rows, src_rows, capacity)
    back = exchange(ret, devices)
    tgt_grad, src_grad = fold(out_table, back, acc, chunks)
    return src_grad.reshape(src_embed.shape), tgt_grad.reshape(tgt_embed.shape)


def solution(mesh):
    placed = (
        P(AXES, None, None),
        P(AXES, None, None),
        P(AXES, None),
        P(AXES, None),
        P(AXES),
        P(),
        P(),
        P(),
    )
    return jax.shard_map(
        shards,
        mesh=mesh,
        in_specs=placed,
        out_specs=(P(AXES, None, None), P(AXES, None, None)),
        check_vma=False,
    )
```

```python
import functools
import math

import jax
import jax.numpy as jnp
from jax import lax
from jax.experimental import pallas as pl
from jax.experimental.pallas import tpu as pltpu
from jax.sharding import PartitionSpec as P

AXES = ("gx", "gy")
CHUNK = 16
TILE = 128
VMEM_BYTES = 60 * 1024 * 1024
DEAD = -1e30
NEAR = 8
FAR = 5
PLANES = 96
GROUP = 4
epsilon = 0.5


def _params():
    return pltpu.CompilerParams(vmem_limit_bytes=VMEM_BYTES)


def _any():
    return pl.BlockSpec(memory_space=pl.ANY)


def _vmem():
    return pl.BlockSpec(memory_space=pltpu.VMEM)


def _smem():
    return pl.BlockSpec(memory_space=pltpu.SMEM)


def _rows(chunk):
    return pl.ds(pl.multiple_of(chunk * CHUNK, CHUNK), CHUNK)


def pack_kernel(slot_chunks, table, tgt_any, src_any, out, home, sems):
    half = tgt_any.shape[0]
    first = pltpu.make_async_copy(tgt_any, home.at[pl.ds(0, half)], sems.at[0])
    second = pltpu.make_async_copy(src_any, home.at[pl.ds(half, half)], sems.at[1])
    first.start()
    second.start()
    home[pl.ds(2 * half, CHUNK), :] = jnp.zeros((CHUNK, home.shape[1]), home.dtype)
    first.wait()
    second.wait()

    def slot(peer, carry):
        for p in range(slot_chunks):
            out[_rows(peer * slot_chunks + p), :] = home[_rows(table[p, peer]), :]
        return carry

    lax.fori_loop(0, table.shape[1], slot, 0)


def pack(table, tgt_rows, src_rows, slot_chunks):
    peers = table.shape[1]
    width = tgt_rows.shape[1]
    total = peers * slot_chunks * CHUNK
    return pl.pallas_call(
        functools.partial(pack_kernel, slot_chunks),
        out_shape=jax.ShapeDtypeStruct((total, width), tgt_rows.dtype),
        in_specs=[_smem(), _any(), _any()],
        out_specs=_vmem(),
        scratch_shapes=[
            pltpu.VMEM((2 * tgt_rows.shape[0] + CHUNK, width), tgt_rows.dtype),
            pltpu.SemaphoreType.DMA((2,)),
        ],
        compiler_params=_params(),
        name="pack",
    )(table, tgt_rows, src_rows)


def side_rows(potential, live, first):
    shape = (CHUNK, potential.shape[1])
    row = lax.broadcasted_iota(jnp.int32, shape, 0)
    lane = lax.broadcasted_iota(jnp.int32, shape, 1)
    dead = jnp.where(lane < live, 0.0, DEAD)
    pot = jnp.broadcast_to(potential, shape)
    own = 0 if first else 1
    other = 1 - own
    mine = 2 if first else 3
    rows = jnp.where(row == own, pot, jnp.where(row == mine, dead, 1.0))
    rows = jnp.where(row < 4, rows, 0.0)
    return rows.astype(jnp.bfloat16)


def compute_kernel(
    capacity,
    scale,
    desc,
    table,
    pots_in,
    pots_home,
    near_any,
    far_any,
    tgt_any,
    src_any,
    ret_near,
    ret_far,
    acc,
    recv,
    ret,
    home,
    moved,
    part,
    sems,
):
    width = home.shape[1]
    half = tgt_any.shape[0]
    near = near_any.shape[0]
    total = near + far_any.shape[0]
    copies = [
        pltpu.make_async_copy(tgt_any, home.at[pl.ds(0, half)], sems.at[0]),
        pltpu.make_async_copy(src_any, home.at[pl.ds(half, half)], sems.at[1]),
        pltpu.make_async_copy(near_any, recv.at[pl.ds(0, near)], sems.at[2]),
        pltpu.make_async_copy(far_any, recv.at[pl.ds(near, total - near)], sems.at[3]),
    ]
    for copy in copies:
        copy.start()
    recv[pl.ds(total, CHUNK), :] = jnp.zeros((CHUNK, width), recv.dtype)
    moved[...] = jnp.zeros_like(moved)

    def clear(i, carry):
        at = pl.multiple_of(i * capacity, capacity)
        acc[pl.ds(at, capacity), :] = jnp.zeros((capacity, width), jnp.float32)
        return carry

    lax.fori_loop(0, acc.shape[0] // capacity, clear, 0)
    for copy in copies:
        copy.wait()
    log2e = math.log2(math.e)
    to_exp = log2e / epsilon

    def tiles(blocks, pair):
        home_id, live_moved, live_home, pot_at, pot_row = pair
        count = (live_home + TILE - 1) // TILE
        right_pots = pots_in[pl.ds(pl.multiple_of(pot_at, 8), 8), :]
        left_pots = pots_home[pl.ds(pl.multiple_of(home_id * 8, 8), 8), :]
        span = blocks * TILE
        right = moved[0:span, :]
        right_side = jnp.concatenate(
            [
                side_rows(right_pots[pot_row + b : pot_row + b + 1, :], live_moved - b * TILE, False)
                for b in range(blocks)
            ],
            axis=1,
        )
        for i in range(capacity // TILE):

            @pl.when(i < count)
            def _():
                at = pl.multiple_of(home_id * capacity + i * TILE, TILE)
                left = home[pl.ds(at, TILE), :]
                left_side = side_rows(left_pots[i : i + 1, :], live_home - i * TILE, True)
                dots = lax.dot_general(
                    left, right, (((1,), (1,)), ((), ())), preferred_element_type=jnp.float32
                )
                sums = lax.dot_general(
                    left_side,
                    right_side,
                    (((0,), (0,)), ((), ())),
                    preferred_element_type=jnp.float32,
                )
                plan = jnp.exp2(dots * (scale * to_exp) + (sums * to_exp - to_exp))
                weight = (plan * (dots * (scale / epsilon) + (1.0 - 1.0 / epsilon))).astype(
                    jnp.bfloat16
                )
                acc[pl.ds(at, TILE), :] += (-scale) * jnp.dot(
                    weight, right, preferred_element_type=jnp.float32
                )
                piece = lax.dot_general(
                    weight, left, (((0,), (0,)), ((), ())), preferred_element_type=jnp.float32
                )
                if i == 0:
                    part[0:span, :] = piece
                else:
                    part[0:span, :] += piece

    def one(peer, kind):
        home_id = desc[4 * kind, peer]
        live_moved = desc[4 * kind + 1, peer]
        live_home = desc[4 * kind + 2, peer]
        start = desc[4 * kind + 3, peer]

        @pl.when(home_id >= 0)
        def _():
            pair = (home_id, live_moved, live_home, peer * 8, kind * (capacity // TILE))
            blocks = (live_moved + TILE - 1) // TILE
            for b in range(capacity // TILE):

                @pl.when(b < blocks)
                def _():
                    for j in range(TILE // CHUNK):
                        at = b * (TILE // CHUNK) + j
                        moved[at * CHUNK : (at + 1) * CHUNK, :] = recv[
                            _rows(table[start + at, peer]), :
                        ]

            for b in range(1, capacity // TILE + 1):
                pl.when(blocks == b)(functools.partial(tiles, b, pair))
            for b in range(capacity // TILE):

                @pl.when(b < blocks)
                def _():
                    for j in range(TILE // CHUNK):
                        at = b * (TILE // CHUNK) + j
                        ret[_rows(table[start + at, peer]), :] = (
                            part[at * CHUNK : (at + 1) * CHUNK, :] * (-scale)
                        ).astype(ret.dtype)

    def peers(peer, carry):
        one(peer, 0)
        one(peer, 1)
        return carry

    lax.fori_loop(0, desc.shape[1], peers, 0)
    back = [
        pltpu.make_async_copy(ret.at[pl.ds(0, near)], ret_near, sems.at[4]),
        pltpu.make_async_copy(ret.at[pl.ds(near, total - near)], ret_far, sems.at[5]),
    ]
    for copy in back:
        copy.start()
    for copy in back:
        copy.wait()


def compute(desc, table, pots_in, pots_home, near, far, tgt_rows, src_rows, capacity):
    width = tgt_rows.shape[1]
    scale = width ** (-0.5)
    homes = 2 * tgt_rows.shape[0]
    return pl.pallas_call(
        functools.partial(compute_kernel, capacity, scale),
        out_shape=(
            jax.ShapeDtypeStruct(near.shape, near.dtype),
            jax.ShapeDtypeStruct(far.shape, far.dtype),
            jax.ShapeDtypeStruct((homes, width), jnp.float32),
        ),
        in_specs=[_smem(), _smem(), _vmem(), _vmem(), _any(), _any(), _any(), _any()],
        out_specs=(_any(), _any(), _vmem()),
        scratch_shapes=[
            pltpu.VMEM((near.shape[0] + far.shape[0] + CHUNK, width), near.dtype),
            pltpu.VMEM((near.shape[0] + far.shape[0] + CHUNK, width), near.dtype),
            pltpu.VMEM((homes, width), tgt_rows.dtype),
            pltpu.VMEM((capacity, width), tgt_rows.dtype),
            pltpu.VMEM((capacity, width), jnp.float32),
            pltpu.SemaphoreType.DMA((6,)),
        ],
        compiler_params=_params(),
        name="pairs",
    )(desc, table, pots_in, pots_home, near, far, tgt_rows, src_rows)


def pass_on_kernel(slot_chunks, table, tgt_any, src_any, got_any, out, pool, sems):
    half = tgt_any.shape[0]
    homes = 2 * half + CHUNK
    copies = [
        pltpu.make_async_copy(tgt_any, pool.at[pl.ds(0, half)], sems.at[0]),
        pltpu.make_async_copy(src_any, pool.at[pl.ds(half, half)], sems.at[1]),
        pltpu.make_async_copy(got_any, pool.at[pl.ds(homes, got_any.shape[0])], sems.at[2]),
    ]
    for copy in copies:
        copy.start()
    pool[pl.ds(2 * half, CHUNK), :] = jnp.zeros((CHUNK, pool.shape[1]), pool.dtype)
    for copy in copies:
        copy.wait()

    def slot(peer, carry):
        for p in range(slot_chunks):
            out[_rows(peer * slot_chunks + p), :] = pool[_rows(table[p, peer]), :]
        return carry

    lax.fori_loop(0, table.shape[1], slot, 0)


def pass_on(table, tgt_rows, src_rows, got, slot_chunks):
    peers = table.shape[1]
    width = tgt_rows.shape[1]
    return pl.pallas_call(
        functools.partial(pass_on_kernel, slot_chunks),
        out_shape=jax.ShapeDtypeStruct((peers * slot_chunks * CHUNK, width), tgt_rows.dtype),
        in_specs=[_smem(), _any(), _any(), _any()],
        out_specs=_vmem(),
        scratch_shapes=[
            pltpu.VMEM((2 * tgt_rows.shape[0] + CHUNK + got.shape[0], width), tgt_rows.dtype),
            pltpu.SemaphoreType.DMA((3,)),
        ],
        compiler_params=_params(),
        name="pass_on",
    )(table, tgt_rows, src_rows, got)


def pass_back_kernel(slot_chunks, homes, table, got, ret_any, out_any, out, sems):
    rows = ret_any.shape[0]
    first = pltpu.make_async_copy(ret_any, out.at[pl.ds(0, rows)], sems.at[0])
    first.start()
    first.wait()

    def slot(peer, carry):
        for p in range(slot_chunks):
            at = table[p, peer] - (homes + 1)
            at = jnp.where(at < 0, rows // CHUNK, at)
            out[_rows(at), :] = got[_rows(peer * slot_chunks + p), :]
        return carry

    lax.fori_loop(0, table.shape[1], slot, 0)
    second = pltpu.make_async_copy(out.at[pl.ds(0, rows)], out_any, sems.at[1])
    second.start()
    second.wait()


def pass_back(table, got, ret, homes, slot_chunks):
    rows, width = ret.shape
    return pl.pallas_call(
        functools.partial(pass_back_kernel, slot_chunks, homes),
        out_shape=jax.ShapeDtypeStruct(ret.shape, ret.dtype),
        in_specs=[_smem(), _vmem(), _any()],
        out_specs=_any(),
        scratch_shapes=[
            pltpu.VMEM((rows + CHUNK, width), ret.dtype),
            pltpu.SemaphoreType.DMA((2,)),
        ],
        compiler_params=_params(),
        name="pass_back",
    )(table, got, ret)


def fold_kernel(
    r1, r2, near_table, far_table, near, far, acc_any, tgt_any, src_any, acc, sems
):
    homes = acc_any.shape[0]
    half = homes // 2
    first = pltpu.make_async_copy(acc_any, acc.at[pl.ds(0, homes)], sems.at[0])
    first.start()
    acc[pl.ds(homes, CHUNK), :] = jnp.zeros((CHUNK, acc.shape[1]), jnp.float32)
    first.wait()

    def slot(peer, carry):
        for p in range(r1):
            at = _rows(near_table[p, peer])
            acc[at, :] += near[_rows(peer * r1 + p), :].astype(jnp.float32)
        for p in range(r2):
            at = _rows(jnp.minimum(far_table[p, peer], homes // CHUNK))
            acc[at, :] += far[_rows(peer * r2 + p), :].astype(jnp.float32)
        return carry

    lax.fori_loop(0, near_table.shape[1], slot, 0)
    out = [
        pltpu.make_async_copy(acc.at[pl.ds(0, half)], tgt_any, sems.at[1]),
        pltpu.make_async_copy(acc.at[pl.ds(half, half)], src_any, sems.at[2]),
    ]
    for copy in out:
        copy.start()
    for copy in out:
        copy.wait()


def fold(near_table, far_table, near, far, acc, r1, r2):
    homes, width = acc.shape
    result = jax.ShapeDtypeStruct((homes // 2, width), jnp.float32)
    return pl.pallas_call(
        functools.partial(fold_kernel, r1, r2),
        out_shape=(result, result),
        in_specs=[_smem(), _smem(), _vmem(), _vmem(), _any()],
        out_specs=(_any(), _any()),
        scratch_shapes=[
            pltpu.VMEM((homes + CHUNK, width), jnp.float32),
            pltpu.SemaphoreType.DMA((3,)),
        ],
        compiler_params=_params(),
        name="fold",
    )(near_table, far_table, near, far, acc)


def exchange(blocks, devices):
    shaped = blocks.reshape(devices, -1, blocks.shape[-1])
    got = lax.all_to_all(shaped, AXES, split_axis=0, concat_axis=0, tiled=True)
    return got.reshape(blocks.shape)


def sched_kernel(
    r1, r2, planes, chunks, me_ref, tc_ref, sc_ref, base_ref, t1, t2, t3, info, moves
):
    n = tc_ref.shape[0]
    me = me_ref[0]
    last = n - 1
    tc = tc_ref[...]
    sc = sc_ref[...]
    row = lax.broadcasted_iota(jnp.int32, (n, n), 0)
    col = lax.broadcasted_iota(jnp.int32, (n, n), 1)
    direct = float(r1 + r2)

    def price(load):
        return load + jnp.maximum(load - r1, 0.0) + jnp.maximum(load - direct, 0.0)

    tct, sct = tc.T, sc.T
    none = price(jnp.zeros_like(tc))
    src_tgt = price(sc + tct) + none
    src_src = price(sc) + price(sct)
    tgt_tgt = price(tct) + price(tc)
    tgt_src = price(tc + sct) + none
    best = jnp.minimum(jnp.minimum(src_tgt, src_src), jnp.minimum(tgt_tgt, tgt_src))
    first = jnp.where((src_tgt == best) | (src_src == best), 0.0, 1.0)
    second = jnp.where(
        src_tgt == best,
        1.0,
        jnp.where(src_src == best, 0.0, jnp.where(tgt_tgt == best, 1.0, 0.0)),
    )
    tgt_moves = jnp.where(row < col, first, second.T)
    tm = tc * tgt_moves
    sm = sc * (1.0 - tgt_moves)
    tmt = tm.T
    load = tmt + sm
    d1 = jnp.minimum(load, float(r1))
    d2 = jnp.minimum(load - d1, float(r2))
    d12 = d1 + d2
    slack1 = r1 - d1
    slack2 = r2 - d2
    bit = 1
    while bit < n:
        slack1 = jnp.where((row & bit) > 0, pltpu.roll(slack1, n - bit, 1), slack1)
        slack2 = jnp.where((col & bit) > 0, pltpu.roll(slack2, n - bit, 0), slack2)
        bit *= 2
    excess = load - d12
    group = 8

    def more(state):
        return (state[0] < planes) & (state[1] > 0.0)

    def step(state):
        at, _, excess, slack1, slack2 = state
        for k in range(group):
            x = jnp.minimum(jnp.minimum(excess, slack1), slack2)
            moves[at + k] = x
            excess = excess - x
            slack1 = pltpu.roll(slack1 - x, n - 1, 1)
            slack2 = pltpu.roll(slack2 - x, n - 1, 0)
        return at + group, jnp.sum(excess), excess, slack1, slack2

    count, left, _, _, _ = lax.while_loop(
        more, step, (jnp.int32(0), jnp.sum(excess), excess, slack1, slack2)
    )

    def mine(value):
        return jnp.sum(jnp.where(row == me, value, 0.0), axis=0, keepdims=True)

    d1r, d2r, d12r = mine(d1), mine(d2), mine(d12)
    d1c, d2c, d12c = mine(d1.T), mine(d2.T), mine(d12.T)
    tn = mine(tmt)
    tb = base_ref[0:1, :]
    sb = base_ref[1:2, :] - tn
    negate = jnp.where(row == ((n - col) & last), 1.0, 0.0).astype(jnp.bfloat16)
    p1n = jnp.dot(
        jnp.broadcast_to(d1c, (16, n)).astype(jnp.bfloat16),
        negate,
        preferred_element_type=jnp.float32,
    )[0:1, :]
    homes = 2.0 * chunks
    first_n = float(n * r1)
    total = float(n * (r1 + r2))
    lane = lax.broadcasted_iota(jnp.int32, (1, n), 1)
    lane_f = lane.astype(jnp.float32)

    def iota_f(rows):
        return lax.broadcasted_iota(jnp.int32, (rows, n), 0).astype(jnp.float32)

    p1, p2, p3 = iota_f(t1.shape[0]), iota_f(t2.shape[0]), iota_f(t3.shape[0])

    def home_of(q, tn, tb, sb):
        return jnp.where(q < tn, tb + q, sb + q)

    v1 = jnp.where(p1 < d1r, home_of(p1, tn, tb, sb), homes)
    v2 = jnp.where(p2 < d2r, home_of(p2 + d1r, tn, tb, sb), homes)
    v3 = jnp.where(
        p3 < d1c,
        lane_f * r1 + p3,
        jnp.where(p3 < d12c, first_n + lane_f * r2 + p3 - d1c, total),
    )
    pick = jnp.where(
        lax.broadcasted_iota(jnp.int32, (16, n), 1) == me, 1.0, 0.0
    ).astype(jnp.bfloat16)

    def extract(r, state):
        v1, v2, v3, qa, p1a, qb, p2b, p1n, p2c = state
        x = moves[r]
        xa = jnp.sum(jnp.where(row == me, x, 0.0), axis=0, keepdims=True)
        xb = lax.dot_general(
            pick, x.astype(jnp.bfloat16), (((1,), (1,)), ((), ())),
            preferred_element_type=jnp.float32,
        )[0:1, :]
        xc = jnp.sum(
            jnp.where(((row + col + r - me) & last) == 0, x, 0.0), axis=0, keepdims=True
        )
        ahead = (me + r) & last
        back = (n - ahead) & last
        stacked = jnp.concatenate([xa, qa, tn, tb, sb, xa, xa, xa], axis=0)
        turned = pltpu.roll(stacked, ahead, 1)
        xa_c, qa_c = turned[0:1, :], turned[1:2, :]
        at = p1 - p1a
        v1 = jnp.where(
            (at >= 0.0) & (at < xa_c),
            home_of(qa_c + at, turned[2:3, :], turned[3:4, :], turned[4:5, :]),
            v1,
        )
        p1a = p1a + xa_c
        qa = qa + xa
        forth = (me - r) & last
        p1b = pltpu.roll(jnp.broadcast_to(p1n, (8, n)), forth, 1)[0:1, :]
        at = p2 - p2c
        origin = ((me - lane - r) & last).astype(jnp.float32)
        v2 = jnp.where((at >= 0.0) & (at < xc), homes + 1.0 + origin * r1 + p1b + at, v2)
        p2c = p2c + xc
        p1n = p1n + pltpu.roll(jnp.broadcast_to(xc, (8, n)), (n - forth) & last, 1)[0:1, :]
        p2a = pltpu.roll(jnp.broadcast_to(p2b, (8, n)), back, 1)[0:1, :]
        via = ((lane + me + r) & last).astype(jnp.float32)
        at = p3 - qb
        v3 = jnp.where((at >= 0.0) & (at < xb), first_n + via * r2 + p2a + at, v3)
        p2b = p2b + pltpu.roll(jnp.broadcast_to(xb, (8, n)), ahead, 1)[0:1, :]
        qb = qb + xb
        return v1, v2, v3, qa, p1a, qb, p2b, p1n, p2c

    v1, v2, v3 = lax.fori_loop(
        0, count, extract, (v1, v2, v3, d12r, d1r, d12c, d2c, p1n, d2r)
    )[:3]
    t1[...] = v1.astype(jnp.int32)
    t2[...] = v2.astype(jnp.int32)
    t3[...] = v3.astype(jnp.int32)
    info[...] = jnp.zeros_like(info)
    info[0:1, :] = mine(tgt_moves)
    info[1:2, :] = mine(tgt_moves.T)
    info[2:3, :] = mine(tm)
    info[3:4, :] = jnp.broadcast_to(left, (1, n))
    info[4:5, :] = jnp.broadcast_to(count.astype(jnp.float32), (1, n))


def schedule(me, tc, sc, base, r1, r2, planes, chunks, deep):
    n = tc.shape[0]

    def ints(rows):
        return jax.ShapeDtypeStruct((rows, n), jnp.int32)

    return pl.pallas_call(
        functools.partial(sched_kernel, r1, r2, planes, chunks),
        out_shape=(
            ints((r1 + 7) // 8 * 8),
            ints((r2 + 7) // 8 * 8),
            ints(deep),
            jax.ShapeDtypeStruct((8, n), jnp.float32),
        ),
        in_specs=[_smem(), _vmem(), _vmem(), _vmem()],
        out_specs=(_vmem(), _vmem(), _vmem(), _vmem()),
        scratch_shapes=[pltpu.VMEM((planes, n, n), jnp.float32)],
        compiler_params=_params(),
        name="plan",
    )(me, tc, sc, base)


def whole_blocks(
    src_embed, tgt_embed, src_potential, tgt_potential, src_sizes, tgt_sizes, pair_counts, pairs
):
    devices = lax.axis_size(("gx", "gy"))
    own_index = lax.axis_index(("gx", "gy"))
    clusters, capacity, feature_width = src_embed.shape
    fanout = pairs.shape[1]
    listed_count = clusters * fanout
    scale = feature_width ** (-0.5)
    listed = pairs.reshape(devices, listed_count)
    fan_ids = jnp.arange(fanout, dtype=jnp.int32)
    used_all = (
        fan_ids[None, None, :] < pair_counts.reshape(devices, clusters)[:, :, None]
    ).reshape(devices, listed_count)
    slot_count = (listed_count + devices - 1) // devices
    counted = jnp.ones_like(used_all)
    owner_all = listed // clusters
    local_all = listed % clusters
    is_mine = (owner_all == own_index) & counted
    rank_all = jnp.cumsum(is_mine.astype(jnp.int32), axis=1) - 1
    slot_ids = jnp.arange(slot_count, dtype=jnp.int32)
    matched = is_mine[:, :, None] & (rank_all[:, :, None] == slot_ids[None, None, :])
    send_local = jnp.sum(jnp.where(matched, local_all[:, :, None], 0), axis=1)
    filled = jnp.any(matched, axis=1)
    out_blocks = jnp.take(tgt_embed, send_local, axis=0)
    out_pots = jnp.take(tgt_potential, send_local, axis=0)
    got_blocks, got_pots = (
        lax.all_to_all(out_blocks, ("gx", "gy"), split_axis=0, concat_axis=0, tiled=True),
        lax.all_to_all(out_pots, ("gx", "gy"), split_axis=0, concat_axis=0, tiled=True),
    )
    my_ids = lax.dynamic_index_in_dim(listed, own_index, 0, keepdims=False)
    my_counted = lax.dynamic_index_in_dim(counted, own_index, 0, keepdims=False)
    my_owner = my_ids // clusters
    order_ids = jnp.arange(listed_count, dtype=jnp.int32)
    same_owner = (my_owner[:, None] == my_owner[None, :]) & my_counted[None, :]
    earlier = order_ids[None, :] < order_ids[:, None]
    my_rank = jnp.sum((same_owner & earlier).astype(jnp.int32), axis=1)
    position = jnp.where(my_counted, my_owner * slot_count + my_rank, devices * slot_count)
    fetch_at = jnp.minimum(position, devices * slot_count - 1)
    tgt_blocks = jnp.take(
        got_blocks.reshape(devices * slot_count, capacity, feature_width), fetch_at, axis=0
    )
    tgt_blocks = tgt_blocks.reshape(clusters, fanout * capacity, feature_width)
    tgt_pots = jnp.take(got_pots.reshape(devices * slot_count, capacity), fetch_at, axis=0).reshape(
        clusters, fanout * capacity
    )
    tgt_size = jnp.take(tgt_sizes, my_ids).reshape(clusters, fanout)
    my_counts = lax.dynamic_slice_in_dim(pair_counts, own_index * clusters, clusters)
    row_ids = jnp.arange(capacity, dtype=jnp.int32)
    valid_right_entity = (row_ids[None, None, :] < tgt_size[:, :, None]) & (
        fan_ids[None, :, None] < my_counts[:, None, None]
    )
    valid_right_entity = valid_right_entity.reshape(clusters, fanout * capacity)
    valid_left_entity = row_ids[None, :] < src_sizes[:, None]

    def per_group(items):
        (
            src_block,
            left_kantorovich_potential,
            row_mask,
            tgt_block,
            right_kantorovich_potential,
            col_mask,
        ) = items
        similarity_grid = (
            jnp.einsum("gic,gjc->gij", src_block, tgt_block, preferred_element_type=jnp.float32)
            * scale
        )
        coupling_probabilities = jnp.exp(
            (
                left_kantorovich_potential.astype(jnp.float32)[:, :, None]
                + right_kantorovich_potential.astype(jnp.float32)[:, None, :]
                - (1.0 - similarity_grid)
            )
            / epsilon
        )
        objective_factor = jnp.where(
            row_mask[:, :, None] & col_mask[:, None, :],
            coupling_probabilities * (1.0 - (1.0 - similarity_grid) / epsilon),
            0.0,
        ).astype(jnp.bfloat16)
        grad_src = (
            -jnp.einsum(
                "gij,gjc->gic", objective_factor, tgt_block, preferred_element_type=jnp.float32
            )
            * scale
        )
        grad_part = (
            -jnp.einsum(
                "gij,gic->gjc", objective_factor, src_block, preferred_element_type=jnp.float32
            )
            * scale
        ).astype(jnp.bfloat16)
        return (grad_src, grad_part)

    batches = clusters // GROUP
    grad_src, grad_part = lax.map(
        per_group,
        (
            src_embed.reshape(batches, GROUP, capacity, feature_width),
            src_potential.reshape(batches, GROUP, capacity),
            valid_left_entity.reshape(batches, GROUP, capacity),
            tgt_blocks.reshape(batches, GROUP, fanout * capacity, feature_width),
            tgt_pots.reshape(batches, GROUP, fanout * capacity),
            valid_right_entity.reshape(batches, GROUP, fanout * capacity),
        ),
    )
    src_grad = grad_src.reshape(clusters, capacity, feature_width)
    part_rows = grad_part.reshape(listed_count, capacity, feature_width)
    outgoing = (
        jnp.zeros((devices * slot_count, capacity, feature_width), jnp.bfloat16)
        .at[position]
        .set(part_rows, mode="drop")
    )
    returned = lax.all_to_all(
        outgoing.reshape(devices, slot_count, capacity, feature_width),
        ("gx", "gy"),
        split_axis=0,
        concat_axis=0,
        tiled=True,
    )
    cluster_ids = jnp.arange(clusters, dtype=jnp.int32)
    selector = (
        (send_local.reshape(-1)[None, :] == cluster_ids[:, None]) & filled.reshape(-1)[None, :]
    ).astype(jnp.bfloat16)
    tgt_grad = jnp.dot(
        selector,
        returned.reshape(devices * slot_count, capacity * feature_width),
        preferred_element_type=jnp.float32,
    )
    return (src_grad, tgt_grad.reshape(clusters, capacity, feature_width))


def shards(
    src_embed, tgt_embed, src_potential, tgt_potential, src_sizes, tgt_sizes, pair_counts, pairs
):
    devices = lax.axis_size(AXES)
    me = lax.axis_index(AXES)
    clusters, capacity, width = src_embed.shape
    fanout = pairs.shape[1]
    listed = pairs.reshape(devices, clusters * fanout)
    entry = jnp.arange(clusters * fanout, dtype=jnp.int32)
    used = (
        jnp.arange(fanout, dtype=jnp.int32)[None, None, :]
        < pair_counts.reshape(devices, clusters)[:, :, None]
    ).reshape(devices, clusters * fanout)
    peer_ids = jnp.arange(devices, dtype=jnp.int32)
    code = used.astype(jnp.int32) * (
        1 + 2 * (entry[None, :] // fanout) + 2 * clusters * (listed % clusters)
    )
    matrix = jnp.sum(
        jnp.where((listed // clusters)[:, :, None] == peer_ids[None, None, :], code[:, :, None], 0),
        axis=1,
    )
    mine = lax.dynamic_index_in_dim(matrix, me, 0, keepdims=False)
    theirs = lax.dynamic_index_in_dim(matrix, me, 1, keepdims=False)
    sizes = tgt_sizes.reshape(devices, clusters)
    own_sizes = lax.dynamic_index_in_dim(sizes, me, 0, keepdims=False)

    def split(value):
        return value % 2, (value // 2) % clusters, value // (2 * clusters)

    out_used, out_peer, out_local = split(theirs)
    in_used, in_home, in_local = split(mine)
    cluster_ids = jnp.arange(clusters, dtype=jnp.int32)

    def pick(rows, at):
        return jnp.sum(jnp.where(at[:, None] == cluster_ids[None, :], rows, 0), axis=1)

    out_size = pick(own_sizes[None, :], out_local)
    in_size = pick(sizes, in_local)
    home_size = pick(src_sizes[None, :], in_home)
    chunks = capacity // CHUNK
    blocks = capacity // TILE
    used_m, home_m, local_m = split(matrix)

    def ceil_chunks(value):
        return (value + CHUNK - 1) // CHUNK

    tgt_chunks = used_m * jnp.sum(
        jnp.where(
            local_m[None] == cluster_ids[:, None, None], ceil_chunks(sizes).T[:, None, :], 0
        ),
        axis=0,
    )
    sizes_row = jnp.stack([src_sizes // CHUNK, src_sizes % CHUNK]).astype(jnp.bfloat16)
    sizes_row = jnp.pad(sizes_row, ((0, 0), (0, TILE - clusters)))
    header = jnp.concatenate(
        [
            jnp.take(tgt_potential, out_local, axis=0).reshape(devices, blocks, TILE),
            jnp.take(src_potential, in_home, axis=0).reshape(devices, blocks, TILE),
            jnp.broadcast_to(sizes_row[None], (devices, 2, TILE)),
        ],
        axis=1,
    )
    header = lax.all_to_all(header, AXES, split_axis=0, concat_axis=0, tiled=True)
    header = header.astype(jnp.float32)
    all_src = (header[:, 6, :clusters] * CHUNK + header[:, 7, :clusters]).astype(jnp.int32)
    src_chunks = used_m * jnp.sum(
        jnp.where(
            home_m[None] == cluster_ids[:, None, None], ceil_chunks(all_src).T[:, :, None], 0
        ),
        axis=0,
    )
    base = jnp.stack([out_local * chunks, (clusters + in_home) * chunks])
    base = jnp.pad(base, ((0, 6), (0, 0))).astype(jnp.float32)
    first, second, third, info = schedule(
        me.reshape(1).astype(jnp.int32),
        tgt_chunks.astype(jnp.float32),
        src_chunks.astype(jnp.float32),
        base,
        NEAR,
        FAR,
        PLANES,
        clusters * chunks,
        2 * chunks,
    )
    tgt_in = (in_used > 0) & (info[0] > 0)
    src_in = (out_used > 0) & (info[1] == 0)
    desc = jnp.stack(
        [
            jnp.where(tgt_in, clusters + in_home, -1),
            in_size,
            home_size,
            jnp.zeros_like(in_size),
            jnp.where(src_in, out_local, -1),
            pick(all_src, out_peer),
            out_size,
            info[2].astype(jnp.int32),
        ]
    )
    homes = 2 * clusters
    pots_home = jnp.concatenate([tgt_potential, src_potential], axis=0).reshape(
        homes, blocks, TILE
    )
    pots_home = (
        jnp.pad(pots_home, ((0, 0), (0, 8 - blocks), (0, 0)))
        .astype(jnp.float32)
        .reshape(homes * 8, TILE)
    )

    def packed(_):
        tgt_rows = tgt_embed.reshape(clusters * capacity, width)
        src_rows = src_embed.reshape(clusters * capacity, width)
        near = exchange(pack(first, tgt_rows, src_rows, NEAR), devices)
        far = exchange(pass_on(second, tgt_rows, src_rows, near, FAR), devices)
        ret_near, ret_far, acc = compute(
            desc,
            third,
            header.reshape(devices * 8, TILE),
            pots_home,
            near,
            far,
            tgt_rows,
            src_rows,
            capacity,
        )
        back_far = exchange(ret_far, devices)
        ret_near = pass_back(second, back_far, ret_near, homes * chunks, FAR)
        back_near = exchange(ret_near, devices)
        tgt_grad, src_grad = fold(first, second, back_near, back_far, acc, NEAR, FAR)
        return src_grad.reshape(src_embed.shape), tgt_grad.reshape(tgt_embed.shape)

    def unpacked(_):
        return whole_blocks(
            src_embed,
            tgt_embed,
            src_potential,
            tgt_potential,
            src_sizes,
            tgt_sizes,
            pair_counts,
            pairs,
        )

    return lax.cond(info[3, 0] == 0.0, packed, unpacked, 0)


def solution(mesh):
    placed = (
        P(AXES, None, None),
        P(AXES, None, None),
        P(AXES, None),
        P(AXES, None),
        P(AXES),
        P(),
        P(),
        P(),
    )
    return jax.shard_map(
        shards,
        mesh=mesh,
        in_specs=placed,
        out_specs=(P(AXES, None, None), P(AXES, None, None)),
        check_vma=False,
    )
```

```python
import functools
import math

import jax
import jax.numpy as jnp
from jax import lax
from jax.experimental import pallas as pl
from jax.experimental.pallas import tpu as pltpu
from jax.sharding import PartitionSpec as P

AXES = ("gx", "gy")
CHUNK = 16
TILE = 128
VMEM_BYTES = 60 * 1024 * 1024
DEAD = -1e30
NEAR = 8
FAR = 5
PLANES = 96
GROUP = 4
epsilon = 0.5


def _params():
    return pltpu.CompilerParams(vmem_limit_bytes=VMEM_BYTES)


def _any():
    return pl.BlockSpec(memory_space=pl.ANY)


def _vmem():
    return pl.BlockSpec(memory_space=pltpu.VMEM)


def _smem():
    return pl.BlockSpec(memory_space=pltpu.SMEM)


def _rows(chunk):
    return pl.ds(pl.multiple_of(chunk * CHUNK, CHUNK), CHUNK)


def pack_kernel(slot_chunks, table, tgt_any, src_any, out, home, sems):
    half = tgt_any.shape[0]
    first = pltpu.make_async_copy(tgt_any, home.at[pl.ds(0, half)], sems.at[0])
    second = pltpu.make_async_copy(src_any, home.at[pl.ds(half, half)], sems.at[1])
    first.start()
    second.start()
    home[pl.ds(2 * half, CHUNK), :] = jnp.zeros((CHUNK, home.shape[1]), home.dtype)
    first.wait()
    second.wait()

    def slot(peer, carry):
        for p in range(slot_chunks):
            out[_rows(peer * slot_chunks + p), :] = home[_rows(table[p, peer]), :]
        return carry

    lax.fori_loop(0, table.shape[1], slot, 0)


def pack(table, tgt_rows, src_rows, slot_chunks):
    peers = table.shape[1]
    width = tgt_rows.shape[1]
    total = peers * slot_chunks * CHUNK
    return pl.pallas_call(
        functools.partial(pack_kernel, slot_chunks),
        out_shape=jax.ShapeDtypeStruct((total, width), tgt_rows.dtype),
        in_specs=[_smem(), _any(), _any()],
        out_specs=_vmem(),
        scratch_shapes=[
            pltpu.VMEM((2 * tgt_rows.shape[0] + CHUNK, width), tgt_rows.dtype),
            pltpu.SemaphoreType.DMA((2,)),
        ],
        compiler_params=_params(),
        name="pack",
    )(table, tgt_rows, src_rows)


def side_rows(potential, live, first):
    shape = (CHUNK, potential.shape[1])
    row = lax.broadcasted_iota(jnp.int32, shape, 0)
    lane = lax.broadcasted_iota(jnp.int32, shape, 1)
    dead = jnp.where(lane < live, 0.0, DEAD)
    pot = jnp.broadcast_to(potential, shape)
    own = 0 if first else 1
    other = 1 - own
    mine = 2 if first else 3
    rows = jnp.where(row == own, pot, jnp.where(row == mine, dead, 1.0))
    rows = jnp.where(row < 4, rows, 0.0)
    return rows.astype(jnp.bfloat16)


def compute_kernel(capacity, scale, phase, far_rows, refs_in, *refs):
    desc, table, pots_in, pots_home, near_any, tgt_any, src_any = refs[:7]
    extra = refs[7:refs_in]
    if phase == 1:
        far_any, ret_before = extra
        ret_near, ret_far, acc = refs[refs_in : refs_in + 3]
    else:
        ret_near, acc = refs[refs_in : refs_in + 2]
    recv, ret, home, items, fill, sems = refs[-6:]
    width = home.shape[1]
    half = tgt_any.shape[0]
    near = near_any.shape[0]
    total = near + far_rows
    copies = [
        pltpu.make_async_copy(tgt_any, home.at[pl.ds(0, half)], sems.at[0]),
        pltpu.make_async_copy(src_any, home.at[pl.ds(half, half)], sems.at[1]),
        pltpu.make_async_copy(near_any, recv.at[pl.ds(0, near)], sems.at[2]),
    ]
    if phase == 1:
        copies += [
            pltpu.make_async_copy(far_any, recv.at[pl.ds(near, far_rows)], sems.at[3]),
            pltpu.make_async_copy(ret_before, ret.at[pl.ds(0, near)], sems.at[4]),
        ]
    if phase == 2:
        ret_before, acc_first, acc_second = extra
        more = refs[-7]
        copies += [
            pltpu.make_async_copy(ret_before, ret.at[pl.ds(0, near)], sems.at[4]),
            pltpu.make_async_copy(acc_first, acc, sems.at[5]),
            pltpu.make_async_copy(acc_second, more, sems.at[6]),
        ]
    for copy in copies:
        copy.start()
    recv[pl.ds(total, CHUNK), :] = jnp.zeros((CHUNK, width), recv.dtype)

    if phase < 2:

        def clear(i, carry):
            at = pl.multiple_of(i * capacity, capacity)
            acc[pl.ds(at, capacity), :] = jnp.zeros((capacity, width), jnp.float32)
            return carry

        lax.fori_loop(0, acc.shape[0] // capacity, clear, 0)
    log2e = math.log2(math.e)
    to_exp = log2e / epsilon

    each = TILE // CHUNK

    def pair_of(item):
        peer, kind = item // 2, item % 2
        field = kind * 4
        return (
            peer,
            kind,
            desc[field, peer],
            desc[field + 1, peer],
            desc[field + 2, peer],
            desc[field + 3, peer],
        )

    def some(blocks, count, pairs):
        rights, sides, lefts = [], [], []
        for peer, kind, home_id, live_moved, live_home, start in pairs:
            rights.append(
                jnp.concatenate(
                    [recv[_rows(table[start + j, peer]), :] for j in range(blocks * each)], axis=0
                )
            )
            right_pots = pots_in[pl.ds(pl.multiple_of(peer * 8, 8), 8), :]
            deep = capacity // TILE
            right_pots = jnp.where(kind == 0, right_pots[0:deep, :], right_pots[deep : 2 * deep, :])
            left_pots = pots_home[pl.ds(pl.multiple_of(home_id * 8, 8), 8), :]
            right_side = jnp.concatenate(
                [
                    side_rows(right_pots[b : b + 1, :], live_moved - b * TILE, False)
                    for b in range(blocks)
                ],
                axis=1,
            )
            left_side = [
                side_rows(left_pots[i : i + 1, :], live_home - i * TILE, True)
                for i in range(count)
            ]
            sides.append((left_side, right_side))
            at = pl.multiple_of(home_id * capacity, TILE)
            lefts.append([home[pl.ds(at + i * TILE, TILE), :] for i in range(count)])
        work = [(k, i) for i in range(count) for k in range(len(pairs))]
        sums = [
            lax.dot_general(
                sides[k][0][i],
                sides[k][1],
                (((0,), (0,)), ((), ())),
                preferred_element_type=jnp.float32,
            )
            for k, i in work
        ]
        dots = [
            lax.dot_general(
                lefts[k][i], rights[k], (((1,), (1,)), ((), ())), preferred_element_type=jnp.float32
            )
            for k, i in work
        ]
        weights = []
        for dot, total_pot in zip(dots, sums):
            plan = jnp.exp2(dot * (scale * to_exp) + (total_pot * to_exp - to_exp))
            weights.append(
                (plan * (dot * (scale / epsilon) + (1.0 - 1.0 / epsilon))).astype(jnp.bfloat16)
            )
        pieces = [
            lax.dot_general(
                weight, lefts[k][i], (((0,), (0,)), ((), ())), preferred_element_type=jnp.float32
            )
            for weight, (k, i) in zip(weights, work)
        ]
        grads = [
            jnp.dot(weight, rights[k], preferred_element_type=jnp.float32)
            for weight, (k, i) in zip(weights, work)
        ]
        for k, pair in enumerate(pairs):
            at = pl.multiple_of(pair[2] * capacity, TILE)
            for i in range(count):
                acc[pl.ds(at + i * TILE, TILE), :] += (-scale) * grads[work.index((k, i))]
            piece = functools.reduce(
                jnp.add, [pieces[work.index((k, i))] for i in range(count)]
            ) * (-scale)
            for j in range(blocks * each):
                into = table[pair[5] + j, pair[0]]
                if j > (blocks - 1) * each:
                    into = jnp.where(j * CHUNK < pair[3], into, total // CHUNK)
                ret[_rows(into), :] = piece[j * CHUNK : (j + 1) * CHUNK, :].astype(ret.dtype)

    deep = capacity // TILE
    for c in range(deep * deep):
        fill[c] = 0

    def sort(peer, carry):
        for kind in range(2):
            home_id = desc[4 * kind, peer]

            @pl.when((home_id >= 0) & (desc[8 + kind, peer] == phase))
            def _():
                blocks = (desc[4 * kind + 1, peer] + TILE - 1) // TILE
                count = (desc[4 * kind + 2, peer] + TILE - 1) // TILE
                group = (blocks - 1) * deep + count - 1
                at = fill[group]
                items[group, at] = peer * 2 + kind
                fill[group] = at + 1

        return carry

    lax.fori_loop(0, desc.shape[1], sort, 0)
    for copy in copies:
        copy.wait()
    if phase == 2:

        def join(i, carry):
            at = pl.ds(pl.multiple_of(i * capacity, capacity), capacity)
            acc[at, :] += more[at, :]
            return carry

        lax.fori_loop(0, acc.shape[0] // capacity, join, 0)
    for b in range(1, deep + 1):
        for c in range(1, deep + 1):
            group = (b - 1) * deep + c - 1
            size = fill[group]

            def two(k, carry, b=b, c=c, group=group):
                some(b, c, [pair_of(items[group, 2 * k]), pair_of(items[group, 2 * k + 1])])
                return carry

            lax.fori_loop(0, size // 2, two, 0)

            @pl.when(size % 2 == 1)
            def _(b=b, c=c, group=group, size=size):
                some(b, c, [pair_of(items[group, size - 1])])

    back = [pltpu.make_async_copy(ret.at[pl.ds(0, near)], ret_near, sems.at[7])]
    if phase == 1:
        back.append(
            pltpu.make_async_copy(ret.at[pl.ds(near, far_rows)], ret_far, sems.at[8])
        )
    for copy in back:
        copy.start()
    for copy in back:
        copy.wait()


def compute(phase, desc, table, pots_in, pots_home, near, tgt_rows, src_rows, capacity, far_rows, extra):
    width = tgt_rows.shape[1]
    scale = width ** (-0.5)
    homes = 2 * tgt_rows.shape[0]
    shapes = [jax.ShapeDtypeStruct(near.shape, near.dtype)]
    if phase == 1:
        shapes.append(jax.ShapeDtypeStruct((far_rows, width), near.dtype))
    shapes.append(jax.ShapeDtypeStruct((homes, width), jnp.float32))
    rows = near.shape[0] + far_rows + CHUNK
    groups = (capacity // TILE) ** 2
    scratch = [
        pltpu.VMEM((rows, width), near.dtype),
        pltpu.VMEM((rows, width), near.dtype),
        pltpu.VMEM((homes, width), tgt_rows.dtype),
        pltpu.SMEM((groups, 2 * desc.shape[1]), jnp.int32),
        pltpu.SMEM((groups,), jnp.int32),
        pltpu.SemaphoreType.DMA((9,)),
    ]
    if phase == 2:
        scratch = [pltpu.VMEM((homes, width), jnp.float32)] + scratch
    work = 4 * desc.shape[1] * capacity * capacity
    return pl.pallas_call(
        functools.partial(compute_kernel, capacity, scale, phase, far_rows, 7 + len(extra)),
        out_shape=tuple(shapes),
        in_specs=[_smem(), _smem(), _vmem(), _vmem()] + [_any()] * (3 + len(extra)),
        out_specs=tuple([_any()] * (len(shapes) - 1) + [_vmem()]),
        scratch_shapes=scratch,
        compiler_params=_params(),
        cost_estimate=pl.CostEstimate(
            flops=work * width, bytes_accessed=8 * homes * width, transcendentals=work // 8
        ),
        name="pairs%d" % phase,
    )(desc, table, pots_in, pots_home, near, tgt_rows, src_rows, *extra)


def pass_on_kernel(slot_chunks, table, tgt_any, src_any, got_any, out, pool, sems):
    half = tgt_any.shape[0]
    homes = 2 * half + CHUNK
    copies = [
        pltpu.make_async_copy(tgt_any, pool.at[pl.ds(0, half)], sems.at[0]),
        pltpu.make_async_copy(src_any, pool.at[pl.ds(half, half)], sems.at[1]),
        pltpu.make_async_copy(got_any, pool.at[pl.ds(homes, got_any.shape[0])], sems.at[2]),
    ]
    for copy in copies:
        copy.start()
    pool[pl.ds(2 * half, CHUNK), :] = jnp.zeros((CHUNK, pool.shape[1]), pool.dtype)
    for copy in copies:
        copy.wait()

    def slot(peer, carry):
        for p in range(slot_chunks):
            out[_rows(peer * slot_chunks + p), :] = pool[_rows(table[p, peer]), :]
        return carry

    lax.fori_loop(0, table.shape[1], slot, 0)


def pass_on(table, tgt_rows, src_rows, got, slot_chunks):
    peers = table.shape[1]
    width = tgt_rows.shape[1]
    return pl.pallas_call(
        functools.partial(pass_on_kernel, slot_chunks),
        out_shape=jax.ShapeDtypeStruct((peers * slot_chunks * CHUNK, width), tgt_rows.dtype),
        in_specs=[_smem(), _any(), _any(), _any()],
        out_specs=_vmem(),
        scratch_shapes=[
            pltpu.VMEM((2 * tgt_rows.shape[0] + CHUNK + got.shape[0], width), tgt_rows.dtype),
            pltpu.SemaphoreType.DMA((3,)),
        ],
        compiler_params=_params(),
        name="pass_on",
    )(table, tgt_rows, src_rows, got)


def pass_back_kernel(slot_chunks, homes, table, got, ret_any, out_any, out, sems):
    rows = ret_any.shape[0]
    first = pltpu.make_async_copy(ret_any, out.at[pl.ds(0, rows)], sems.at[0])
    first.start()
    first.wait()

    def slot(peer, carry):
        for p in range(slot_chunks):
            at = table[p, peer] - (homes + 1)
            at = jnp.where(at < 0, rows // CHUNK, at)
            out[_rows(at), :] = got[_rows(peer * slot_chunks + p), :]
        return carry

    lax.fori_loop(0, table.shape[1], slot, 0)
    second = pltpu.make_async_copy(out.at[pl.ds(0, rows)], out_any, sems.at[1])
    second.start()
    second.wait()


def pass_back(table, got, ret, homes, slot_chunks):
    rows, width = ret.shape
    return pl.pallas_call(
        functools.partial(pass_back_kernel, slot_chunks, homes),
        out_shape=jax.ShapeDtypeStruct(ret.shape, ret.dtype),
        in_specs=[_smem(), _vmem(), _any()],
        out_specs=_any(),
        scratch_shapes=[
            pltpu.VMEM((rows + CHUNK, width), ret.dtype),
            pltpu.SemaphoreType.DMA((2,)),
        ],
        compiler_params=_params(),
        name="pass_back",
    )(table, got, ret)


def fold_kernel(slot_chunks, table, got, acc_any, *refs):
    outs, acc, sems = refs[:-2], refs[-2], refs[-1]
    homes = acc_any.shape[0]
    first = pltpu.make_async_copy(acc_any, acc.at[pl.ds(0, homes)], sems.at[0])
    first.start()
    acc[pl.ds(homes, CHUNK), :] = jnp.zeros((CHUNK, acc.shape[1]), jnp.float32)
    first.wait()

    def slot(peer, carry):
        for p in range(slot_chunks):
            at = _rows(jnp.minimum(table[p, peer], homes // CHUNK))
            acc[at, :] += got[_rows(peer * slot_chunks + p), :].astype(jnp.float32)
        return carry

    lax.fori_loop(0, table.shape[1], slot, 0)
    share = homes // len(outs)
    copies = [
        pltpu.make_async_copy(acc.at[pl.ds(k * share, share)], out, sems.at[k + 1])
        for k, out in enumerate(outs)
    ]
    for copy in copies:
        copy.start()
    for copy in copies:
        copy.wait()


def fold(table, got, acc, slot_chunks, parts):
    homes, width = acc.shape
    result = jax.ShapeDtypeStruct((homes // parts, width), jnp.float32)
    return pl.pallas_call(
        functools.partial(fold_kernel, slot_chunks),
        out_shape=(result,) * parts,
        in_specs=[_smem(), _vmem(), _any()],
        out_specs=(_any(),) * parts,
        scratch_shapes=[
            pltpu.VMEM((homes + CHUNK, width), jnp.float32),
            pltpu.SemaphoreType.DMA((parts + 1,)),
        ],
        compiler_params=_params(),
        cost_estimate=pl.CostEstimate(
            flops=homes * width, bytes_accessed=8 * homes * width, transcendentals=0
        ),
        name="fold%d" % parts,
    )(table, got, acc)


def exchange(blocks, devices):
    shaped = blocks.reshape(devices, -1, blocks.shape[-1])
    got = lax.all_to_all(shaped, AXES, split_axis=0, concat_axis=0, tiled=True)
    return got.reshape(blocks.shape)


def sched_kernel(
    r1, r2, planes, chunks, me_ref, tc_ref, sc_ref, base_ref, t1, t2, t3, info, moves
):
    n = tc_ref.shape[0]
    me = me_ref[0]
    last = n - 1
    tc = tc_ref[...]
    sc = sc_ref[...]
    row = lax.broadcasted_iota(jnp.int32, (n, n), 0)
    col = lax.broadcasted_iota(jnp.int32, (n, n), 1)
    direct = float(r1 + r2)

    def price(load):
        return load + jnp.maximum(load - r1, 0.0) + jnp.maximum(load - direct, 0.0)

    tct, sct = tc.T, sc.T
    none = price(jnp.zeros_like(tc))
    src_tgt = price(sc + tct) + none
    src_src = price(sc) + price(sct)
    tgt_tgt = price(tct) + price(tc)
    tgt_src = price(tc + sct) + none
    best = jnp.minimum(jnp.minimum(src_tgt, src_src), jnp.minimum(tgt_tgt, tgt_src))
    first = jnp.where((src_tgt == best) | (src_src == best), 0.0, 1.0)
    second = jnp.where(
        src_tgt == best,
        1.0,
        jnp.where(src_src == best, 0.0, jnp.where(tgt_tgt == best, 1.0, 0.0)),
    )
    tgt_moves = jnp.where(row < col, first, second.T)
    tm = tc * tgt_moves
    sm = sc * (1.0 - tgt_moves)
    tmt = tm.T
    load = tmt + sm
    d1 = jnp.minimum(load, float(r1))
    d2 = jnp.minimum(load - d1, float(r2))
    d12 = d1 + d2
    slack1 = r1 - d1
    slack2 = r2 - d2
    bit = 1
    while bit < n:
        slack1 = jnp.where((row & bit) > 0, pltpu.roll(slack1, n - bit, 1), slack1)
        slack2 = jnp.where((col & bit) > 0, pltpu.roll(slack2, n - bit, 0), slack2)
        bit *= 2
    excess = load - d12
    group = 8

    def more(state):
        return (state[0] < planes) & (state[1] > 0.0)

    def step(state):
        at, _, excess, slack1, slack2 = state
        for k in range(group):
            x = jnp.minimum(jnp.minimum(excess, slack1), slack2)
            moves[at + k] = x
            excess = excess - x
            slack1 = pltpu.roll(slack1 - x, n - 1, 1)
            slack2 = pltpu.roll(slack2 - x, n - 1, 0)
        return at + group, jnp.sum(excess), excess, slack1, slack2

    count, left, _, _, _ = lax.while_loop(
        more, step, (jnp.int32(0), jnp.sum(excess), excess, slack1, slack2)
    )

    def mine(value):
        return jnp.sum(jnp.where(row == me, value, 0.0), axis=0, keepdims=True)

    d1r, d2r, d12r = mine(d1), mine(d2), mine(d12)
    d1c, d2c, d12c = mine(d1.T), mine(d2.T), mine(d12.T)
    tn = mine(tmt)
    tb = base_ref[0:1, :]
    sb = base_ref[1:2, :] - tn
    negate = jnp.where(row == ((n - col) & last), 1.0, 0.0).astype(jnp.bfloat16)
    p1n = jnp.dot(
        jnp.broadcast_to(d1c, (16, n)).astype(jnp.bfloat16),
        negate,
        preferred_element_type=jnp.float32,
    )[0:1, :]
    homes = 2.0 * chunks
    first_n = float(n * r1)
    total = float(n * (r1 + r2))
    lane = lax.broadcasted_iota(jnp.int32, (1, n), 1)
    lane_f = lane.astype(jnp.float32)

    def iota_f(rows):
        return lax.broadcasted_iota(jnp.int32, (rows, n), 0).astype(jnp.float32)

    p1, p2, p3 = iota_f(t1.shape[0]), iota_f(t2.shape[0]), iota_f(t3.shape[0])

    def home_of(q, tn, tb, sb):
        return jnp.where(q < tn, tb + q, sb + q)

    v1 = jnp.where(p1 < d1r, home_of(p1, tn, tb, sb), homes)
    v2 = jnp.where(p2 < d2r, home_of(p2 + d1r, tn, tb, sb), homes)
    v3 = jnp.where(
        p3 < d1c,
        lane_f * r1 + p3,
        jnp.where(p3 < d12c, first_n + lane_f * r2 + p3 - d1c, total),
    )
    pick = jnp.where(
        lax.broadcasted_iota(jnp.int32, (16, n), 1) == me, 1.0, 0.0
    ).astype(jnp.bfloat16)

    def extract(r, state):
        v1, v2, v3, qa, p1a, qb, p2b, p1n, p2c = state
        x = moves[r]
        xa = jnp.sum(jnp.where(row == me, x, 0.0), axis=0, keepdims=True)
        xb = lax.dot_general(
            pick, x.astype(jnp.bfloat16), (((1,), (1,)), ((), ())),
            preferred_element_type=jnp.float32,
        )[0:1, :]
        xc = jnp.sum(
            jnp.where(((row + col + r - me) & last) == 0, x, 0.0), axis=0, keepdims=True
        )
        ahead = (me + r) & last
        back = (n - ahead) & last
        stacked = jnp.concatenate([xa, qa, tn, tb, sb, xa, xa, xa], axis=0)
        turned = pltpu.roll(stacked, ahead, 1)
        xa_c, qa_c = turned[0:1, :], turned[1:2, :]
        at = p1 - p1a
        v1 = jnp.where(
            (at >= 0.0) & (at < xa_c),
            home_of(qa_c + at, turned[2:3, :], turned[3:4, :], turned[4:5, :]),
            v1,
        )
        p1a = p1a + xa_c
        qa = qa + xa
        forth = (me - r) & last
        p1b = pltpu.roll(jnp.broadcast_to(p1n, (8, n)), forth, 1)[0:1, :]
        at = p2 - p2c
        origin = ((me - lane - r) & last).astype(jnp.float32)
        v2 = jnp.where((at >= 0.0) & (at < xc), homes + 1.0 + origin * r1 + p1b + at, v2)
        p2c = p2c + xc
        p1n = p1n + pltpu.roll(jnp.broadcast_to(xc, (8, n)), (n - forth) & last, 1)[0:1, :]
        p2a = pltpu.roll(jnp.broadcast_to(p2b, (8, n)), back, 1)[0:1, :]
        via = ((lane + me + r) & last).astype(jnp.float32)
        at = p3 - qb
        v3 = jnp.where((at >= 0.0) & (at < xb), first_n + via * r2 + p2a + at, v3)
        p2b = p2b + pltpu.roll(jnp.broadcast_to(xb, (8, n)), ahead, 1)[0:1, :]
        qb = qb + xb
        return v1, v2, v3, qa, p1a, qb, p2b, p1n, p2c

    v1, v2, v3 = lax.fori_loop(
        0, count, extract, (v1, v2, v3, d12r, d1r, d12c, d2c, p1n, d2r)
    )[:3]
    t1[...] = v1.astype(jnp.int32)
    t2[...] = v2.astype(jnp.int32)
    t3[...] = v3.astype(jnp.int32)
    info[...] = jnp.zeros_like(info)
    info[0:1, :] = mine(tgt_moves)
    info[1:2, :] = mine(tgt_moves.T)
    info[2:3, :] = mine(tm)
    info[3:4, :] = jnp.broadcast_to(left, (1, n))
    info[4:5, :] = jnp.broadcast_to(count.astype(jnp.float32), (1, n))


def schedule(me, tc, sc, base, r1, r2, planes, chunks, deep):
    n = tc.shape[0]

    def ints(rows):
        return jax.ShapeDtypeStruct((rows, n), jnp.int32)

    return pl.pallas_call(
        functools.partial(sched_kernel, r1, r2, planes, chunks),
        out_shape=(
            ints((r1 + 7) // 8 * 8),
            ints((r2 + 7) // 8 * 8),
            ints(deep),
            jax.ShapeDtypeStruct((8, n), jnp.float32),
        ),
        in_specs=[_smem(), _vmem(), _vmem(), _vmem()],
        out_specs=(_vmem(), _vmem(), _vmem(), _vmem()),
        scratch_shapes=[pltpu.VMEM((planes, n, n), jnp.float32)],
        compiler_params=_params(),
        name="plan",
    )(me, tc, sc, base)


def whole_blocks(
    src_embed, tgt_embed, src_potential, tgt_potential, src_sizes, tgt_sizes, pair_counts, pairs
):
    devices = lax.axis_size(("gx", "gy"))
    own_index = lax.axis_index(("gx", "gy"))
    clusters, capacity, feature_width = src_embed.shape
    fanout = pairs.shape[1]
    listed_count = clusters * fanout
    scale = feature_width ** (-0.5)
    listed = pairs.reshape(devices, listed_count)
    fan_ids = jnp.arange(fanout, dtype=jnp.int32)
    used_all = (
        fan_ids[None, None, :] < pair_counts.reshape(devices, clusters)[:, :, None]
    ).reshape(devices, listed_count)
    slot_count = (listed_count + devices - 1) // devices
    counted = jnp.ones_like(used_all)
    owner_all = listed // clusters
    local_all = listed % clusters
    is_mine = (owner_all == own_index) & counted
    rank_all = jnp.cumsum(is_mine.astype(jnp.int32), axis=1) - 1
    slot_ids = jnp.arange(slot_count, dtype=jnp.int32)
    matched = is_mine[:, :, None] & (rank_all[:, :, None] == slot_ids[None, None, :])
    send_local = jnp.sum(jnp.where(matched, local_all[:, :, None], 0), axis=1)
    filled = jnp.any(matched, axis=1)
    out_blocks = jnp.take(tgt_embed, send_local, axis=0)
    out_pots = jnp.take(tgt_potential, send_local, axis=0)
    got_blocks, got_pots = (
        lax.all_to_all(out_blocks, ("gx", "gy"), split_axis=0, concat_axis=0, tiled=True),
        lax.all_to_all(out_pots, ("gx", "gy"), split_axis=0, concat_axis=0, tiled=True),
    )
    my_ids = lax.dynamic_index_in_dim(listed, own_index, 0, keepdims=False)
    my_counted = lax.dynamic_index_in_dim(counted, own_index, 0, keepdims=False)
    my_owner = my_ids // clusters
    order_ids = jnp.arange(listed_count, dtype=jnp.int32)
    same_owner = (my_owner[:, None] == my_owner[None, :]) & my_counted[None, :]
    earlier = order_ids[None, :] < order_ids[:, None]
    my_rank = jnp.sum((same_owner & earlier).astype(jnp.int32), axis=1)
    position = jnp.where(my_counted, my_owner * slot_count + my_rank, devices * slot_count)
    fetch_at = jnp.minimum(position, devices * slot_count - 1)
    tgt_blocks = jnp.take(
        got_blocks.reshape(devices * slot_count, capacity, feature_width), fetch_at, axis=0
    )
    tgt_blocks = tgt_blocks.reshape(clusters, fanout * capacity, feature_width)
    tgt_pots = jnp.take(got_pots.reshape(devices * slot_count, capacity), fetch_at, axis=0).reshape(
        clusters, fanout * capacity
    )
    tgt_size = jnp.take(tgt_sizes, my_ids).reshape(clusters, fanout)
    my_counts = lax.dynamic_slice_in_dim(pair_counts, own_index * clusters, clusters)
    row_ids = jnp.arange(capacity, dtype=jnp.int32)
    valid_right_entity = (row_ids[None, None, :] < tgt_size[:, :, None]) & (
        fan_ids[None, :, None] < my_counts[:, None, None]
    )
    valid_right_entity = valid_right_entity.reshape(clusters, fanout * capacity)
    valid_left_entity = row_ids[None, :] < src_sizes[:, None]

    def per_group(items):
        (
            src_block,
            left_kantorovich_potential,
            row_mask,
            tgt_block,
            right_kantorovich_potential,
            col_mask,
        ) = items
        similarity_grid = (
            jnp.einsum("gic,gjc->gij", src_block, tgt_block, preferred_element_type=jnp.float32)
            * scale
        )
        coupling_probabilities = jnp.exp(
            (
                left_kantorovich_potential.astype(jnp.float32)[:, :, None]
                + right_kantorovich_potential.astype(jnp.float32)[:, None, :]
                - (1.0 - similarity_grid)
            )
            / epsilon
        )
        objective_factor = jnp.where(
            row_mask[:, :, None] & col_mask[:, None, :],
            coupling_probabilities * (1.0 - (1.0 - similarity_grid) / epsilon),
            0.0,
        ).astype(jnp.bfloat16)
        grad_src = (
            -jnp.einsum(
                "gij,gjc->gic", objective_factor, tgt_block, preferred_element_type=jnp.float32
            )
            * scale
        )
        grad_part = (
            -jnp.einsum(
                "gij,gic->gjc", objective_factor, src_block, preferred_element_type=jnp.float32
            )
            * scale
        ).astype(jnp.bfloat16)
        return (grad_src, grad_part)

    batches = clusters // GROUP
    grad_src, grad_part = lax.map(
        per_group,
        (
            src_embed.reshape(batches, GROUP, capacity, feature_width),
            src_potential.reshape(batches, GROUP, capacity),
            valid_left_entity.reshape(batches, GROUP, capacity),
            tgt_blocks.reshape(batches, GROUP, fanout * capacity, feature_width),
            tgt_pots.reshape(batches, GROUP, fanout * capacity),
            valid_right_entity.reshape(batches, GROUP, fanout * capacity),
        ),
    )
    src_grad = grad_src.reshape(clusters, capacity, feature_width)
    part_rows = grad_part.reshape(listed_count, capacity, feature_width)
    outgoing = (
        jnp.zeros((devices * slot_count, capacity, feature_width), jnp.bfloat16)
        .at[position]
        .set(part_rows, mode="drop")
    )
    returned = lax.all_to_all(
        outgoing.reshape(devices, slot_count, capacity, feature_width),
        ("gx", "gy"),
        split_axis=0,
        concat_axis=0,
        tiled=True,
    )
    cluster_ids = jnp.arange(clusters, dtype=jnp.int32)
    selector = (
        (send_local.reshape(-1)[None, :] == cluster_ids[:, None]) & filled.reshape(-1)[None, :]
    ).astype(jnp.bfloat16)
    tgt_grad = jnp.dot(
        selector,
        returned.reshape(devices * slot_count, capacity * feature_width),
        preferred_element_type=jnp.float32,
    )
    return (src_grad, tgt_grad.reshape(clusters, capacity, feature_width))


def shards(
    src_embed, tgt_embed, src_potential, tgt_potential, src_sizes, tgt_sizes, pair_counts, pairs
):
    devices = lax.axis_size(AXES)
    me = lax.axis_index(AXES)
    clusters, capacity, width = src_embed.shape
    fanout = pairs.shape[1]
    listed = pairs.reshape(devices, clusters * fanout)
    entry = jnp.arange(clusters * fanout, dtype=jnp.int32)
    used = (
        jnp.arange(fanout, dtype=jnp.int32)[None, None, :]
        < pair_counts.reshape(devices, clusters)[:, :, None]
    ).reshape(devices, clusters * fanout)
    peer_ids = jnp.arange(devices, dtype=jnp.int32)
    code = used.astype(jnp.int32) * (
        1 + 2 * (entry[None, :] // fanout) + 2 * clusters * (listed % clusters)
    )
    matrix = jnp.sum(
        jnp.where((listed // clusters)[:, :, None] == peer_ids[None, None, :], code[:, :, None], 0),
        axis=1,
    )
    mine = lax.dynamic_index_in_dim(matrix, me, 0, keepdims=False)
    theirs = lax.dynamic_index_in_dim(matrix, me, 1, keepdims=False)
    sizes = tgt_sizes.reshape(devices, clusters)
    own_sizes = lax.dynamic_index_in_dim(sizes, me, 0, keepdims=False)

    def split(value):
        return value % 2, (value // 2) % clusters, value // (2 * clusters)

    out_used, out_peer, out_local = split(theirs)
    in_used, in_home, in_local = split(mine)
    cluster_ids = jnp.arange(clusters, dtype=jnp.int32)

    def pick(rows, at):
        return jnp.sum(jnp.where(at[:, None] == cluster_ids[None, :], rows, 0), axis=1)

    out_size = pick(own_sizes[None, :], out_local)
    in_size = pick(sizes, in_local)
    home_size = pick(src_sizes[None, :], in_home)
    chunks = capacity // CHUNK
    blocks = capacity // TILE
    used_m, home_m, local_m = split(matrix)

    def ceil_chunks(value):
        return (value + CHUNK - 1) // CHUNK

    tgt_chunks = used_m * jnp.sum(
        jnp.where(
            local_m[None] == cluster_ids[:, None, None], ceil_chunks(sizes).T[:, None, :], 0
        ),
        axis=0,
    )
    sizes_row = jnp.stack([src_sizes // CHUNK, src_sizes % CHUNK]).astype(jnp.bfloat16)
    sizes_row = jnp.pad(sizes_row, ((0, 0), (0, TILE - clusters)))
    header = jnp.concatenate(
        [
            jnp.take(tgt_potential, out_local, axis=0).reshape(devices, blocks, TILE),
            jnp.take(src_potential, in_home, axis=0).reshape(devices, blocks, TILE),
            jnp.broadcast_to(sizes_row[None], (devices, 2, TILE)),
        ],
        axis=1,
    )
    header = lax.all_to_all(header, AXES, split_axis=0, concat_axis=0, tiled=True)
    header = header.astype(jnp.float32)
    all_src = (header[:, 6, :clusters] * CHUNK + header[:, 7, :clusters]).astype(jnp.int32)
    src_chunks = used_m * jnp.sum(
        jnp.where(
            home_m[None] == cluster_ids[:, None, None], ceil_chunks(all_src).T[:, :, None], 0
        ),
        axis=0,
    )
    base = jnp.stack([out_local * chunks, (clusters + in_home) * chunks])
    base = jnp.pad(base, ((0, 6), (0, 0))).astype(jnp.float32)
    first, second, third, info = schedule(
        me.reshape(1).astype(jnp.int32),
        tgt_chunks.astype(jnp.float32),
        src_chunks.astype(jnp.float32),
        base,
        NEAR,
        FAR,
        PLANES,
        clusters * chunks,
        2 * chunks,
    )
    tgt_in = (in_used > 0) & (info[0] > 0)
    src_in = (out_used > 0) & (info[1] == 0)
    tgt_end = info[2].astype(jnp.int32)
    src_end = tgt_end + ceil_chunks(pick(all_src, out_peer))
    early = 2 * (peer_ids % 2)
    desc = jnp.stack(
        [
            jnp.where(tgt_in, clusters + in_home, -1),
            in_size,
            home_size,
            jnp.zeros_like(in_size),
            jnp.where(src_in, out_local, -1),
            pick(all_src, out_peer),
            out_size,
            info[2].astype(jnp.int32),
            jnp.where(tgt_end > NEAR, 1, early),
            jnp.where(src_end > NEAR, 1, early),
        ]
    )
    homes = 2 * clusters
    pots_home = jnp.concatenate([tgt_potential, src_potential], axis=0).reshape(
        homes, blocks, TILE
    )
    pots_home = (
        jnp.pad(pots_home, ((0, 0), (0, 8 - blocks), (0, 0)))
        .astype(jnp.float32)
        .reshape(homes * 8, TILE)
    )

    def packed(_):
        tgt_rows = tgt_embed.reshape(clusters * capacity, width)
        src_rows = src_embed.reshape(clusters * capacity, width)
        near = exchange(pack(first, tgt_rows, src_rows, NEAR), devices)
        far = exchange(pass_on(second, tgt_rows, src_rows, near, FAR), devices)

        def pairs_of(phase, *extra):
            return compute(
                phase,
                desc,
                third,
                header.reshape(devices * 8, TILE),
                pots_home,
                near,
                tgt_rows,
                src_rows,
                capacity,
                devices * FAR * CHUNK,
                extra,
            )

        ret, acc_first = pairs_of(0)
        ret, ret_far, acc_second = pairs_of(1, far, ret)
        back_far = exchange(ret_far, devices)
        ret, acc = pairs_of(2, ret, acc_first, acc_second)
        ret = pass_back(second, back_far, ret, homes * chunks, FAR)
        back_near = exchange(ret, devices)
        (acc,) = fold(second, back_far, acc, FAR, 1)
        tgt_grad, src_grad = fold(first, back_near, acc, NEAR, 2)
        return src_grad.reshape(src_embed.shape), tgt_grad.reshape(tgt_embed.shape)

    def unpacked(_):
        return whole_blocks(
            src_embed,
            tgt_embed,
            src_potential,
            tgt_potential,
            src_sizes,
            tgt_sizes,
            pair_counts,
            pairs,
        )

    return lax.cond(info[3, 0] == 0.0, packed, unpacked, 0)


def solution(mesh):
    placed = (
        P(AXES, None, None),
        P(AXES, None, None),
        P(AXES, None),
        P(AXES, None),
        P(AXES),
        P(),
        P(),
        P(),
    )
    return jax.shard_map(
        shards,
        mesh=mesh,
        in_specs=placed,
        out_specs=(P(AXES, None, None), P(AXES, None, None)),
        check_vma=False,
    )
```

```python
import functools
import math

import jax
import jax.numpy as jnp
from jax import lax
from jax.experimental import pallas as pl
from jax.experimental.pallas import tpu as pltpu
from jax.sharding import PartitionSpec as P

AXES = ("gx", "gy")
CHUNK = 16
TILE = 128
VMEM_BYTES = 60 * 1024 * 1024
DEAD = -1e30
NEAR = 8
FAR = 4
PLANES = 128
ROUNDS = 4
STEP = 0.3
GROUP = 4
epsilon = 0.5


def _params():
    return pltpu.CompilerParams(vmem_limit_bytes=VMEM_BYTES)


def _any():
    return pl.BlockSpec(memory_space=pl.ANY)


def _vmem():
    return pl.BlockSpec(memory_space=pltpu.VMEM)


def _smem():
    return pl.BlockSpec(memory_space=pltpu.SMEM)


def _rows(chunk):
    return pl.ds(pl.multiple_of(chunk * CHUNK, CHUNK), CHUNK)


def pack_kernel(slot_chunks, table, tgt_any, src_any, out, home, sems):
    half = tgt_any.shape[0]
    first = pltpu.make_async_copy(tgt_any, home.at[pl.ds(0, half)], sems.at[0])
    second = pltpu.make_async_copy(src_any, home.at[pl.ds(half, half)], sems.at[1])
    first.start()
    second.start()
    home[pl.ds(2 * half, CHUNK), :] = jnp.zeros((CHUNK, home.shape[1]), home.dtype)
    first.wait()
    second.wait()

    def slot(peer, carry):
        for p in range(slot_chunks):
            out[_rows(peer * slot_chunks + p), :] = home[_rows(table[p, peer]), :]
        return carry

    lax.fori_loop(0, table.shape[1], slot, 0)


def pack(table, tgt_rows, src_rows, slot_chunks):
    peers = table.shape[1]
    width = tgt_rows.shape[1]
    total = peers * slot_chunks * CHUNK
    return pl.pallas_call(
        functools.partial(pack_kernel, slot_chunks),
        out_shape=jax.ShapeDtypeStruct((total, width), tgt_rows.dtype),
        in_specs=[_smem(), _any(), _any()],
        out_specs=_vmem(),
        scratch_shapes=[
            pltpu.VMEM((2 * tgt_rows.shape[0] + CHUNK, width), tgt_rows.dtype),
            pltpu.SemaphoreType.DMA((2,)),
        ],
        compiler_params=_params(),
        name="pack",
    )(table, tgt_rows, src_rows)


def side_rows(potential, live, first):
    shape = (CHUNK, potential.shape[1])
    row = lax.broadcasted_iota(jnp.int32, shape, 0)
    lane = lax.broadcasted_iota(jnp.int32, shape, 1)
    dead = jnp.where(lane < live, 0.0, DEAD)
    pot = jnp.broadcast_to(potential, shape)
    own = 0 if first else 1
    other = 1 - own
    mine = 2 if first else 3
    rows = jnp.where(row == own, pot, jnp.where(row == mine, dead, 1.0))
    rows = jnp.where(row < 4, rows, 0.0)
    return rows.astype(jnp.bfloat16)


def compute_kernel(capacity, scale, phase, far_rows, refs_in, *refs):
    desc, table, pots_in, pots_home, near_any, tgt_any, src_any = refs[:7]
    extra = refs[7:refs_in]
    if phase == 1:
        far_any, ret_before = extra
        ret_near, ret_far, acc = refs[refs_in : refs_in + 3]
    else:
        ret_near, acc = refs[refs_in : refs_in + 2]
    recv, ret, home, items, fill, sems = refs[-6:]
    width = home.shape[1]
    half = tgt_any.shape[0]
    near = near_any.shape[0]
    total = near + far_rows
    copies = [
        pltpu.make_async_copy(tgt_any, home.at[pl.ds(0, half)], sems.at[0]),
        pltpu.make_async_copy(src_any, home.at[pl.ds(half, half)], sems.at[1]),
        pltpu.make_async_copy(near_any, recv.at[pl.ds(0, near)], sems.at[2]),
    ]
    if phase == 1:
        copies += [
            pltpu.make_async_copy(far_any, recv.at[pl.ds(near, far_rows)], sems.at[3]),
            pltpu.make_async_copy(ret_before, ret.at[pl.ds(0, near)], sems.at[4]),
        ]
    if phase == 2:
        ret_before, acc_first, acc_second = extra
        more = refs[-7]
        copies += [
            pltpu.make_async_copy(ret_before, ret.at[pl.ds(0, near)], sems.at[4]),
            pltpu.make_async_copy(acc_first, acc, sems.at[5]),
            pltpu.make_async_copy(acc_second, more, sems.at[6]),
        ]
    for copy in copies:
        copy.start()
    recv[pl.ds(total, CHUNK), :] = jnp.zeros((CHUNK, width), recv.dtype)

    if phase < 2:

        def clear(i, carry):
            at = pl.multiple_of(i * capacity, capacity)
            acc[pl.ds(at, capacity), :] = jnp.zeros((capacity, width), jnp.float32)
            return carry

        lax.fori_loop(0, acc.shape[0] // capacity, clear, 0)
    log2e = math.log2(math.e)
    to_exp = log2e / epsilon

    each = TILE // CHUNK

    def pair_of(group, at, size):
        item = items[group, jnp.minimum(at, size - 1)]
        real = at < size
        peer, kind = item // 2, item % 2
        field = kind * 4
        return (
            peer,
            kind,
            desc[field, peer],
            jnp.where(real, desc[field + 1, peer], 0),
            jnp.where(real, desc[field + 2, peer], 0),
            desc[field + 3, peer],
        )

    def some(blocks, count, pairs):
        rights, sides, lefts = [], [], []
        for peer, kind, home_id, live_moved, live_home, start in pairs:
            rights.append(
                jnp.concatenate(
                    [recv[_rows(table[start + j, peer]), :] for j in range(blocks * each)], axis=0
                )
            )
            right_pots = pots_in[pl.ds(pl.multiple_of(peer * 8, 8), 8), :]
            deep = capacity // TILE
            right_pots = jnp.where(kind == 0, right_pots[0:deep, :], right_pots[deep : 2 * deep, :])
            left_pots = pots_home[pl.ds(pl.multiple_of(home_id * 8, 8), 8), :]
            right_side = jnp.concatenate(
                [
                    side_rows(right_pots[b : b + 1, :], live_moved - b * TILE, False)
                    for b in range(blocks)
                ],
                axis=1,
            )
            left_side = [
                side_rows(left_pots[i : i + 1, :], live_home - i * TILE, True)
                for i in range(count)
            ]
            sides.append((left_side, right_side))
            at = pl.multiple_of(home_id * capacity, TILE)
            lefts.append([home[pl.ds(at + i * TILE, TILE), :] for i in range(count)])
        work = [(k, i) for i in range(count) for k in range(len(pairs))]
        sums = [
            lax.dot_general(
                sides[k][0][i],
                sides[k][1],
                (((0,), (0,)), ((), ())),
                preferred_element_type=jnp.float32,
            )
            for k, i in work
        ]
        dots = [
            lax.dot_general(
                lefts[k][i], rights[k], (((1,), (1,)), ((), ())), preferred_element_type=jnp.float32
            )
            for k, i in work
        ]
        weights = []
        for dot, total_pot in zip(dots, sums):
            plan = jnp.exp2(dot * (scale * to_exp) + (total_pot * to_exp - to_exp))
            weights.append(
                (plan * (dot * (scale / epsilon) + (1.0 - 1.0 / epsilon))).astype(jnp.bfloat16)
            )
        pieces = [
            lax.dot_general(
                weight, lefts[k][i], (((0,), (0,)), ((), ())), preferred_element_type=jnp.float32
            )
            for weight, (k, i) in zip(weights, work)
        ]
        grads = [
            jnp.dot(weight, rights[k], preferred_element_type=jnp.float32)
            for weight, (k, i) in zip(weights, work)
        ]
        for k, pair in enumerate(pairs):
            at = pl.multiple_of(pair[2] * capacity, TILE)
            for i in range(count):
                acc[pl.ds(at + i * TILE, TILE), :] += (-scale) * grads[work.index((k, i))]
            piece = functools.reduce(
                jnp.add, [pieces[work.index((k, i))] for i in range(count)]
            ) * (-scale)
            for j in range(blocks * each):
                into = table[pair[5] + j, pair[0]]
                into = jnp.where(j * CHUNK < pair[3], into, total // CHUNK)
                ret[_rows(into), :] = piece[j * CHUNK : (j + 1) * CHUNK, :].astype(ret.dtype)

    deep = capacity // TILE
    for c in range(deep * deep):
        fill[c] = 0

    def sort(peer, carry):
        for kind in range(2):
            home_id = desc[4 * kind, peer]

            @pl.when((home_id >= 0) & (desc[8 + kind, peer] == phase))
            def _():
                blocks = (desc[4 * kind + 1, peer] + TILE - 1) // TILE
                count = (desc[4 * kind + 2, peer] + TILE - 1) // TILE
                group = (blocks - 1) * deep + count - 1
                at = fill[group]
                items[group, at] = peer * 2 + kind
                fill[group] = at + 1

        return carry

    lax.fori_loop(0, desc.shape[1], sort, 0)
    for copy in copies:
        copy.wait()
    if phase == 2:

        def join(i, carry):
            at = pl.ds(pl.multiple_of(i * capacity, capacity), capacity)
            acc[at, :] += more[at, :]
            return carry

        lax.fori_loop(0, acc.shape[0] // capacity, join, 0)
    for b in range(1, deep + 1):
        for c in range(1, deep + 1):
            group = (b - 1) * deep + c - 1
            size = fill[group]

            def two(k, carry, b=b, c=c, group=group, size=size):
                some(b, c, [pair_of(group, 2 * k, size), pair_of(group, 2 * k + 1, size)])
                return carry

            lax.fori_loop(0, (size + 1) // 2, two, 0)

    back = [pltpu.make_async_copy(ret.at[pl.ds(0, near)], ret_near, sems.at[7])]
    if phase == 1:
        back.append(
            pltpu.make_async_copy(ret.at[pl.ds(near, far_rows)], ret_far, sems.at[8])
        )
    for copy in back:
        copy.start()
    for copy in back:
        copy.wait()


def compute(phase, desc, table, pots_in, pots_home, near, tgt_rows, src_rows, capacity, far_rows, extra):
    width = tgt_rows.shape[1]
    scale = width ** (-0.5)
    homes = 2 * tgt_rows.shape[0]
    shapes = [jax.ShapeDtypeStruct(near.shape, near.dtype)]
    if phase == 1:
        shapes.append(jax.ShapeDtypeStruct((far_rows, width), near.dtype))
    shapes.append(jax.ShapeDtypeStruct((homes, width), jnp.float32))
    rows = near.shape[0] + far_rows + CHUNK
    groups = (capacity // TILE) ** 2
    scratch = [
        pltpu.VMEM((rows, width), near.dtype),
        pltpu.VMEM((rows, width), near.dtype),
        pltpu.VMEM((homes, width), tgt_rows.dtype),
        pltpu.SMEM((groups, 2 * desc.shape[1]), jnp.int32),
        pltpu.SMEM((groups,), jnp.int32),
        pltpu.SemaphoreType.DMA((9,)),
    ]
    if phase == 2:
        scratch = [pltpu.VMEM((homes, width), jnp.float32)] + scratch
    work = 4 * desc.shape[1] * capacity * capacity
    return pl.pallas_call(
        functools.partial(compute_kernel, capacity, scale, phase, far_rows, 7 + len(extra)),
        out_shape=tuple(shapes),
        in_specs=[_smem(), _smem(), _vmem(), _vmem()] + [_any()] * (3 + len(extra)),
        out_specs=tuple([_any()] * (len(shapes) - 1) + [_vmem()]),
        scratch_shapes=scratch,
        compiler_params=_params(),
        cost_estimate=pl.CostEstimate(
            flops=work * width, bytes_accessed=8 * homes * width, transcendentals=work // 8
        ),
        name="pairs%d" % phase,
    )(desc, table, pots_in, pots_home, near, tgt_rows, src_rows, *extra)


def pass_on_kernel(slot_chunks, table, tgt_any, src_any, got_any, out, pool, sems):
    half = tgt_any.shape[0]
    homes = 2 * half + CHUNK
    copies = [
        pltpu.make_async_copy(tgt_any, pool.at[pl.ds(0, half)], sems.at[0]),
        pltpu.make_async_copy(src_any, pool.at[pl.ds(half, half)], sems.at[1]),
        pltpu.make_async_copy(got_any, pool.at[pl.ds(homes, got_any.shape[0])], sems.at[2]),
    ]
    for copy in copies:
        copy.start()
    pool[pl.ds(2 * half, CHUNK), :] = jnp.zeros((CHUNK, pool.shape[1]), pool.dtype)
    for copy in copies:
        copy.wait()

    def slot(peer, carry):
        for p in range(slot_chunks):
            out[_rows(peer * slot_chunks + p), :] = pool[_rows(table[p, peer]), :]
        return carry

    lax.fori_loop(0, table.shape[1], slot, 0)


def pass_on(table, tgt_rows, src_rows, got, slot_chunks):
    peers = table.shape[1]
    width = tgt_rows.shape[1]
    return pl.pallas_call(
        functools.partial(pass_on_kernel, slot_chunks),
        out_shape=jax.ShapeDtypeStruct((peers * slot_chunks * CHUNK, width), tgt_rows.dtype),
        in_specs=[_smem(), _any(), _any(), _any()],
        out_specs=_vmem(),
        scratch_shapes=[
            pltpu.VMEM((2 * tgt_rows.shape[0] + CHUNK + got.shape[0], width), tgt_rows.dtype),
            pltpu.SemaphoreType.DMA((3,)),
        ],
        compiler_params=_params(),
        name="pass_on",
    )(table, tgt_rows, src_rows, got)


def pass_back_kernel(slot_chunks, homes, table, got, ret_any, out_any, out, sems):
    rows = ret_any.shape[0]
    first = pltpu.make_async_copy(ret_any, out.at[pl.ds(0, rows)], sems.at[0])
    first.start()
    first.wait()

    def slot(peer, carry):
        for p in range(slot_chunks):
            at = table[p, peer] - (homes + 1)
            at = jnp.where(at < 0, rows // CHUNK, at)
            out[_rows(at), :] = got[_rows(peer * slot_chunks + p), :]
        return carry

    lax.fori_loop(0, table.shape[1], slot, 0)
    second = pltpu.make_async_copy(out.at[pl.ds(0, rows)], out_any, sems.at[1])
    second.start()
    second.wait()


def pass_back(table, got, ret, homes, slot_chunks):
    rows, width = ret.shape
    return pl.pallas_call(
        functools.partial(pass_back_kernel, slot_chunks, homes),
        out_shape=jax.ShapeDtypeStruct(ret.shape, ret.dtype),
        in_specs=[_smem(), _vmem(), _any()],
        out_specs=_any(),
        scratch_shapes=[
            pltpu.VMEM((rows + CHUNK, width), ret.dtype),
            pltpu.SemaphoreType.DMA((2,)),
        ],
        compiler_params=_params(),
        name="pass_back",
    )(table, got, ret)


def fold_kernel(slot_chunks, table, got, acc_any, *refs):
    outs, (even, odd, base, sems) = refs[:-4], refs[-4:]
    homes = acc_any.shape[0]
    first = pltpu.make_async_copy(acc_any, base, sems.at[0])
    first.start()

    def clear(i, carry):
        at = pl.ds(pl.multiple_of(i * 8 * CHUNK, 8 * CHUNK), 8 * CHUNK)
        even[at, :] = jnp.zeros((8 * CHUNK, even.shape[1]), jnp.float32)
        odd[at, :] = jnp.zeros((8 * CHUNK, odd.shape[1]), jnp.float32)
        return carry

    lax.fori_loop(0, homes // (8 * CHUNK), clear, 0)

    def slot(peer, carry):
        for p in range(slot_chunks):
            sums = odd if p % 2 else even
            at = _rows(jnp.minimum(table[p, peer], homes // CHUNK))
            sums[at, :] += got[_rows(peer * slot_chunks + p), :].astype(jnp.float32)
        return carry

    lax.fori_loop(0, table.shape[1], slot, 0)
    first.wait()
    pieces = sems.shape[0] - 1
    share = homes // pieces
    per_out = pieces // len(outs)
    copies = []
    for k in range(pieces):

        def join(i, carry, k=k):
            at = pl.ds(pl.multiple_of(k * share + i * 8 * CHUNK, 8 * CHUNK), 8 * CHUNK)
            base[at, :] = base[at, :] + (even[at, :] + odd[at, :])
            return carry

        lax.fori_loop(0, share // (8 * CHUNK), join, 0)
        out = outs[k // per_out]
        into = out.at[pl.ds((k % per_out) * share, share)]
        copies.append(
            pltpu.make_async_copy(base.at[pl.ds(k * share, share)], into, sems.at[k + 1])
        )
        copies[-1].start()
    for copy in copies:
        copy.wait()


def fold(table, got, acc, slot_chunks, parts):
    homes, width = acc.shape
    result = jax.ShapeDtypeStruct((homes // parts, width), jnp.float32)
    return pl.pallas_call(
        functools.partial(fold_kernel, slot_chunks),
        out_shape=(result,) * parts,
        in_specs=[_smem(), _vmem(), _any()],
        out_specs=(_any(),) * parts,
        scratch_shapes=[
            pltpu.VMEM((homes + CHUNK, width), jnp.float32),
            pltpu.VMEM((homes + CHUNK, width), jnp.float32),
            pltpu.VMEM((homes, width), jnp.float32),
            pltpu.SemaphoreType.DMA((8 + 1,)),
        ],
        compiler_params=_params(),
        cost_estimate=pl.CostEstimate(
            flops=homes * width, bytes_accessed=8 * homes * width, transcendentals=0
        ),
        name="fold%d" % parts,
    )(table, got, acc)


def exchange(blocks, devices):
    shaped = blocks.reshape(devices, -1, blocks.shape[-1])
    got = lax.all_to_all(shaped, AXES, split_axis=0, concat_axis=0, tiled=True)
    return got.reshape(blocks.shape)


def sched_kernel(
    r1, r2, planes, chunks, me_ref, tc_ref, sc_ref, base_ref, t1, t2, t3, info, moves
):
    n = tc_ref.shape[0]
    me = me_ref[0]
    last = n - 1
    tc = tc_ref[...]
    sc = sc_ref[...]
    row = lax.broadcasted_iota(jnp.int32, (n, n), 0)
    col = lax.broadcasted_iota(jnp.int32, (n, n), 1)
    direct = float(r1 + r2)

    tct, sct = tc.T, sc.T

    def cost(count, price):
        return price * (
            count + jnp.maximum(count - r1, 0.0) + jnp.maximum(count - direct, 0.0)
        )

    def choose(price):
        back = price.T
        src_tgt = cost(sc + tct, price)
        src_src = cost(sc, price) + cost(sct, back)
        tgt_tgt = cost(tct, price) + cost(tc, back)
        tgt_src = cost(tc + sct, back)
        best = jnp.minimum(jnp.minimum(src_tgt, src_src), jnp.minimum(tgt_tgt, tgt_src))
        src_first = (src_tgt == best) | (src_src == best)
        first = jnp.where(src_first, 0.0, 1.0)
        second = jnp.where(
            src_tgt == best,
            1.0,
            jnp.where(src_src == best, 0.0, jnp.where(tgt_tgt == best, 1.0, 0.0)),
        )
        tgt_moves = jnp.where(row < col, first, second.T)
        tm = tc * tgt_moves
        return tgt_moves, tm, tm.T + sc * (1.0 - tgt_moves)

    def update(_, price):
        load = choose(price)[2]
        sent = jnp.sum(load, axis=1, keepdims=True)
        got = jnp.sum(load, axis=0, keepdims=True)
        mean = jnp.maximum(jnp.sum(got, axis=1, keepdims=True) / n, 1.0)
        return price + STEP * (sent / mean - 1.0) + STEP * (got / mean - 1.0)

    prices = lax.fori_loop(0, ROUNDS, update, jnp.ones_like(tc))
    tgt_moves, tm, load = choose(prices)
    tmt = tm.T
    d1 = jnp.minimum(load, float(r1))
    d2 = jnp.minimum(load - d1, float(r2))
    d12 = d1 + d2
    slack1 = r1 - d1
    slack2 = r2 - d2
    bit = 1
    while bit < n:
        slack1 = jnp.where((row & bit) > 0, pltpu.roll(slack1, n - bit, 1), slack1)
        slack2 = jnp.where((col & bit) > 0, pltpu.roll(slack2, n - bit, 0), slack2)
        bit *= 2
    excess = load - d12
    group = 8

    def more(state):
        return (state[0] < planes) & (state[1] > 0.0)

    def step(state):
        at, _, excess, slack1, slack2 = state
        for k in range(group):
            x = jnp.minimum(jnp.minimum(excess, slack1), slack2)
            moves[at + k] = x
            excess = excess - x
            slack1 = pltpu.roll(slack1 - x, n - 1, 1)
            slack2 = pltpu.roll(slack2 - x, n - 1, 0)
        return at + group, jnp.sum(excess), excess, slack1, slack2

    count, left, _, _, _ = lax.while_loop(
        more, step, (jnp.int32(0), jnp.sum(excess), excess, slack1, slack2)
    )

    def mine(value):
        return jnp.sum(jnp.where(row == me, value, 0.0), axis=0, keepdims=True)

    d1r, d2r, d12r = mine(d1), mine(d2), mine(d12)
    d1c, d2c, d12c = mine(d1.T), mine(d2.T), mine(d12.T)
    tn = mine(tmt)
    tb = base_ref[0:1, :]
    sb = base_ref[1:2, :] - tn
    negate = jnp.where(row == ((n - col) & last), 1.0, 0.0).astype(jnp.bfloat16)
    p1n = jnp.dot(
        jnp.broadcast_to(d1c, (16, n)).astype(jnp.bfloat16),
        negate,
        preferred_element_type=jnp.float32,
    )[0:1, :]
    homes = 2.0 * chunks
    first_n = float(n * r1)
    total = float(n * (r1 + r2))
    lane = lax.broadcasted_iota(jnp.int32, (1, n), 1)
    lane_f = lane.astype(jnp.float32)

    def iota_f(rows):
        return lax.broadcasted_iota(jnp.int32, (rows, n), 0).astype(jnp.float32)

    p1, p2, p3 = iota_f(t1.shape[0]), iota_f(t2.shape[0]), iota_f(t3.shape[0])

    def home_of(q, tn, tb, sb):
        return jnp.where(q < tn, tb + q, sb + q)

    v1 = jnp.where(p1 < d1r, home_of(p1, tn, tb, sb), homes)
    v2 = jnp.where(p2 < d2r, home_of(p2 + d1r, tn, tb, sb), homes)
    v3 = jnp.where(
        p3 < d1c,
        lane_f * r1 + p3,
        jnp.where(p3 < d12c, first_n + lane_f * r2 + p3 - d1c, total),
    )
    pick = jnp.where(
        lax.broadcasted_iota(jnp.int32, (16, n), 1) == me, 1.0, 0.0
    ).astype(jnp.bfloat16)

    def extract(r, state):
        v1, v2, v3, qa, p1a, qb, p2b, p1n, p2c = state
        x = moves[r]
        xa = jnp.sum(jnp.where(row == me, x, 0.0), axis=0, keepdims=True)
        xb = lax.dot_general(
            pick, x.astype(jnp.bfloat16), (((1,), (1,)), ((), ())),
            preferred_element_type=jnp.float32,
        )[0:1, :]
        xc = jnp.sum(
            jnp.where(((row + col + r - me) & last) == 0, x, 0.0), axis=0, keepdims=True
        )
        ahead = (me + r) & last
        back = (n - ahead) & last
        stacked = jnp.concatenate([xa, qa, tn, tb, sb, xa, xa, xa], axis=0)
        turned = pltpu.roll(stacked, ahead, 1)
        xa_c, qa_c = turned[0:1, :], turned[1:2, :]
        at = p1 - p1a
        v1 = jnp.where(
            (at >= 0.0) & (at < xa_c),
            home_of(qa_c + at, turned[2:3, :], turned[3:4, :], turned[4:5, :]),
            v1,
        )
        p1a = p1a + xa_c
        qa = qa + xa
        forth = (me - r) & last
        p1b = pltpu.roll(jnp.broadcast_to(p1n, (8, n)), forth, 1)[0:1, :]
        at = p2 - p2c
        origin = ((me - lane - r) & last).astype(jnp.float32)
        v2 = jnp.where((at >= 0.0) & (at < xc), homes + 1.0 + origin * r1 + p1b + at, v2)
        p2c = p2c + xc
        p1n = p1n + pltpu.roll(jnp.broadcast_to(xc, (8, n)), (n - forth) & last, 1)[0:1, :]
        p2a = pltpu.roll(jnp.broadcast_to(p2b, (8, n)), back, 1)[0:1, :]
        via = ((lane + me + r) & last).astype(jnp.float32)
        at = p3 - qb
        v3 = jnp.where((at >= 0.0) & (at < xb), first_n + via * r2 + p2a + at, v3)
        p2b = p2b + pltpu.roll(jnp.broadcast_to(xb, (8, n)), ahead, 1)[0:1, :]
        qb = qb + xb
        return v1, v2, v3, qa, p1a, qb, p2b, p1n, p2c

    def several(k, state):
        for u in range(group // 2):
            state = extract(k * (group // 2) + u, state)
        return state

    v1, v2, v3 = lax.fori_loop(
        0, count // (group // 2), several, (v1, v2, v3, d12r, d1r, d12c, d2c, p1n, d2r)
    )[:3]
    t1[...] = v1.astype(jnp.int32)
    t2[...] = v2.astype(jnp.int32)
    t3[...] = v3.astype(jnp.int32)
    info[...] = jnp.zeros_like(info)
    info[0:1, :] = mine(tgt_moves)
    info[1:2, :] = mine(tgt_moves.T)
    info[2:3, :] = mine(tm)
    info[3:4, :] = jnp.broadcast_to(left, (1, n))
    info[4:5, :] = jnp.broadcast_to(count.astype(jnp.float32), (1, n))


def schedule(me, tc, sc, base, r1, r2, planes, chunks, deep):
    n = tc.shape[0]

    def ints(rows):
        return jax.ShapeDtypeStruct((rows, n), jnp.int32)

    return pl.pallas_call(
        functools.partial(sched_kernel, r1, r2, planes, chunks),
        out_shape=(
            ints((r1 + 7) // 8 * 8),
            ints((r2 + 7) // 8 * 8),
            ints(deep),
            jax.ShapeDtypeStruct((8, n), jnp.float32),
        ),
        in_specs=[_smem(), _vmem(), _vmem(), _vmem()],
        out_specs=(_vmem(), _vmem(), _vmem(), _vmem()),
        scratch_shapes=[pltpu.VMEM((planes, n, n), jnp.float32)],
        compiler_params=_params(),
        name="plan",
    )(me, tc, sc, base)


def whole_blocks(
    src_embed, tgt_embed, src_potential, tgt_potential, src_sizes, tgt_sizes, pair_counts, pairs
):
    devices = lax.axis_size(("gx", "gy"))
    own_index = lax.axis_index(("gx", "gy"))
    clusters, capacity, feature_width = src_embed.shape
    fanout = pairs.shape[1]
    listed_count = clusters * fanout
    scale = feature_width ** (-0.5)
    listed = pairs.reshape(devices, listed_count)
    fan_ids = jnp.arange(fanout, dtype=jnp.int32)
    used_all = (
        fan_ids[None, None, :] < pair_counts.reshape(devices, clusters)[:, :, None]
    ).reshape(devices, listed_count)
    slot_count = (listed_count + devices - 1) // devices
    counted = jnp.ones_like(used_all)
    owner_all = listed // clusters
    local_all = listed % clusters
    is_mine = (owner_all == own_index) & counted
    rank_all = jnp.cumsum(is_mine.astype(jnp.int32), axis=1) - 1
    slot_ids = jnp.arange(slot_count, dtype=jnp.int32)
    matched = is_mine[:, :, None] & (rank_all[:, :, None] == slot_ids[None, None, :])
    send_local = jnp.sum(jnp.where(matched, local_all[:, :, None], 0), axis=1)
    filled = jnp.any(matched, axis=1)
    out_blocks = jnp.take(tgt_embed, send_local, axis=0)
    out_pots = jnp.take(tgt_potential, send_local, axis=0)
    got_blocks, got_pots = (
        lax.all_to_all(out_blocks, ("gx", "gy"), split_axis=0, concat_axis=0, tiled=True),
        lax.all_to_all(out_pots, ("gx", "gy"), split_axis=0, concat_axis=0, tiled=True),
    )
    my_ids = lax.dynamic_index_in_dim(listed, own_index, 0, keepdims=False)
    my_counted = lax.dynamic_index_in_dim(counted, own_index, 0, keepdims=False)
    my_owner = my_ids // clusters
    order_ids = jnp.arange(listed_count, dtype=jnp.int32)
    same_owner = (my_owner[:, None] == my_owner[None, :]) & my_counted[None, :]
    earlier = order_ids[None, :] < order_ids[:, None]
    my_rank = jnp.sum((same_owner & earlier).astype(jnp.int32), axis=1)
    position = jnp.where(my_counted, my_owner * slot_count + my_rank, devices * slot_count)
    fetch_at = jnp.minimum(position, devices * slot_count - 1)
    tgt_blocks = jnp.take(
        got_blocks.reshape(devices * slot_count, capacity, feature_width), fetch_at, axis=0
    )
    tgt_blocks = tgt_blocks.reshape(clusters, fanout * capacity, feature_width)
    tgt_pots = jnp.take(got_pots.reshape(devices * slot_count, capacity), fetch_at, axis=0).reshape(
        clusters, fanout * capacity
    )
    tgt_size = jnp.take(tgt_sizes, my_ids).reshape(clusters, fanout)
    my_counts = lax.dynamic_slice_in_dim(pair_counts, own_index * clusters, clusters)
    row_ids = jnp.arange(capacity, dtype=jnp.int32)
    valid_right_entity = (row_ids[None, None, :] < tgt_size[:, :, None]) & (
        fan_ids[None, :, None] < my_counts[:, None, None]
    )
    valid_right_entity = valid_right_entity.reshape(clusters, fanout * capacity)
    valid_left_entity = row_ids[None, :] < src_sizes[:, None]

    def per_group(items):
        (
            src_block,
            left_kantorovich_potential,
            row_mask,
            tgt_block,
            right_kantorovich_potential,
            col_mask,
        ) = items
        similarity_grid = (
            jnp.einsum("gic,gjc->gij", src_block, tgt_block, preferred_element_type=jnp.float32)
            * scale
        )
        coupling_probabilities = jnp.exp(
            (
                left_kantorovich_potential.astype(jnp.float32)[:, :, None]
                + right_kantorovich_potential.astype(jnp.float32)[:, None, :]
                - (1.0 - similarity_grid)
            )
            / epsilon
        )
        objective_factor = jnp.where(
            row_mask[:, :, None] & col_mask[:, None, :],
            coupling_probabilities * (1.0 - (1.0 - similarity_grid) / epsilon),
            0.0,
        ).astype(jnp.bfloat16)
        grad_src = (
            -jnp.einsum(
                "gij,gjc->gic", objective_factor, tgt_block, preferred_element_type=jnp.float32
            )
            * scale
        )
        grad_part = (
            -jnp.einsum(
                "gij,gic->gjc", objective_factor, src_block, preferred_element_type=jnp.float32
            )
            * scale
        ).astype(jnp.bfloat16)
        return (grad_src, grad_part)

    batches = clusters // GROUP
    grad_src, grad_part = lax.map(
        per_group,
        (
            src_embed.reshape(batches, GROUP, capacity, feature_width),
            src_potential.reshape(batches, GROUP, capacity),
            valid_left_entity.reshape(batches, GROUP, capacity),
            tgt_blocks.reshape(batches, GROUP, fanout * capacity, feature_width),
            tgt_pots.reshape(batches, GROUP, fanout * capacity),
            valid_right_entity.reshape(batches, GROUP, fanout * capacity),
        ),
    )
    src_grad = grad_src.reshape(clusters, capacity, feature_width)
    part_rows = grad_part.reshape(listed_count, capacity, feature_width)
    outgoing = (
        jnp.zeros((devices * slot_count, capacity, feature_width), jnp.bfloat16)
        .at[position]
        .set(part_rows, mode="drop")
    )
    returned = lax.all_to_all(
        outgoing.reshape(devices, slot_count, capacity, feature_width),
        ("gx", "gy"),
        split_axis=0,
        concat_axis=0,
        tiled=True,
    )
    cluster_ids = jnp.arange(clusters, dtype=jnp.int32)
    selector = (
        (send_local.reshape(-1)[None, :] == cluster_ids[:, None]) & filled.reshape(-1)[None, :]
    ).astype(jnp.bfloat16)
    tgt_grad = jnp.dot(
        selector,
        returned.reshape(devices * slot_count, capacity * feature_width),
        preferred_element_type=jnp.float32,
    )
    return (src_grad, tgt_grad.reshape(clusters, capacity, feature_width))


def shards(
    src_embed, tgt_embed, src_potential, tgt_potential, src_sizes, tgt_sizes, pair_counts, pairs
):
    devices = lax.axis_size(AXES)
    me = lax.axis_index(AXES)
    clusters, capacity, width = src_embed.shape
    fanout = pairs.shape[1]
    listed = pairs.reshape(devices, clusters * fanout)
    entry = jnp.arange(clusters * fanout, dtype=jnp.int32)
    used = (
        jnp.arange(fanout, dtype=jnp.int32)[None, None, :]
        < pair_counts.reshape(devices, clusters)[:, :, None]
    ).reshape(devices, clusters * fanout)
    peer_ids = jnp.arange(devices, dtype=jnp.int32)
    code = used.astype(jnp.int32) * (
        1 + 2 * (entry[None, :] // fanout) + 2 * clusters * (listed % clusters)
    )
    matrix = jnp.sum(
        jnp.where((listed // clusters)[:, :, None] == peer_ids[None, None, :], code[:, :, None], 0),
        axis=1,
    )
    mine = lax.dynamic_index_in_dim(matrix, me, 0, keepdims=False)
    theirs = lax.dynamic_index_in_dim(matrix, me, 1, keepdims=False)
    sizes = tgt_sizes.reshape(devices, clusters)
    own_sizes = lax.dynamic_index_in_dim(sizes, me, 0, keepdims=False)

    def split(value):
        return value % 2, (value // 2) % clusters, value // (2 * clusters)

    out_used, out_peer, out_local = split(theirs)
    in_used, in_home, in_local = split(mine)
    cluster_ids = jnp.arange(clusters, dtype=jnp.int32)

    def pick(rows, at):
        return jnp.sum(jnp.where(at[:, None] == cluster_ids[None, :], rows, 0), axis=1)

    out_size = pick(own_sizes[None, :], out_local)
    in_size = pick(sizes, in_local)
    home_size = pick(src_sizes[None, :], in_home)
    chunks = capacity // CHUNK
    blocks = capacity // TILE
    used_m, home_m, local_m = split(matrix)

    def ceil_chunks(value):
        return (value + CHUNK - 1) // CHUNK

    tgt_chunks = used_m * jnp.sum(
        jnp.where(
            local_m[None] == cluster_ids[:, None, None], ceil_chunks(sizes).T[:, None, :], 0
        ),
        axis=0,
    )
    sizes_row = jnp.stack([src_sizes // CHUNK, src_sizes % CHUNK]).astype(jnp.bfloat16)
    sizes_row = jnp.pad(sizes_row, ((0, 0), (0, TILE - clusters)))
    header = jnp.concatenate(
        [
            jnp.take(tgt_potential, out_local, axis=0).reshape(devices, blocks, TILE),
            jnp.take(src_potential, in_home, axis=0).reshape(devices, blocks, TILE),
            jnp.broadcast_to(sizes_row[None], (devices, 2, TILE)),
        ],
        axis=1,
    )
    header = lax.all_to_all(header, AXES, split_axis=0, concat_axis=0, tiled=True)
    header = header.astype(jnp.float32)
    all_src = (header[:, 6, :clusters] * CHUNK + header[:, 7, :clusters]).astype(jnp.int32)
    src_chunks = used_m * jnp.sum(
        jnp.where(
            home_m[None] == cluster_ids[:, None, None], ceil_chunks(all_src).T[:, :, None], 0
        ),
        axis=0,
    )
    base = jnp.stack([out_local * chunks, (clusters + in_home) * chunks])
    base = jnp.pad(base, ((0, 6), (0, 0))).astype(jnp.float32)
    first, second, third, info = schedule(
        me.reshape(1).astype(jnp.int32),
        tgt_chunks.astype(jnp.float32),
        src_chunks.astype(jnp.float32),
        base,
        NEAR,
        FAR,
        PLANES,
        clusters * chunks,
        2 * chunks,
    )
    tgt_in = (in_used > 0) & (info[0] > 0)
    src_in = (out_used > 0) & (info[1] == 0)
    tgt_end = info[2].astype(jnp.int32)
    src_end = tgt_end + ceil_chunks(pick(all_src, out_peer))
    early = 2 * (peer_ids % 2)
    desc = jnp.stack(
        [
            jnp.where(tgt_in, clusters + in_home, -1),
            in_size,
            home_size,
            jnp.zeros_like(in_size),
            jnp.where(src_in, out_local, -1),
            pick(all_src, out_peer),
            out_size,
            info[2].astype(jnp.int32),
            jnp.where(tgt_end > NEAR, 1, early),
            jnp.where(src_end > NEAR, 1, early),
        ]
    )
    homes = 2 * clusters
    pots_home = jnp.concatenate([tgt_potential, src_potential], axis=0).reshape(
        homes, blocks, TILE
    )
    pots_home = (
        jnp.pad(pots_home, ((0, 0), (0, 8 - blocks), (0, 0)))
        .astype(jnp.float32)
        .reshape(homes * 8, TILE)
    )

    def packed(_):
        tgt_rows = tgt_embed.reshape(clusters * capacity, width)
        src_rows = src_embed.reshape(clusters * capacity, width)
        near = exchange(pack(first, tgt_rows, src_rows, NEAR), devices)
        far = exchange(pass_on(second, tgt_rows, src_rows, near, FAR), devices)

        def pairs_of(phase, *extra):
            return compute(
                phase,
                desc,
                third,
                header.reshape(devices * 8, TILE),
                pots_home,
                near,
                tgt_rows,
                src_rows,
                capacity,
                devices * FAR * CHUNK,
                extra,
            )

        ret, acc_first = pairs_of(0)
        ret, ret_far, acc_second = pairs_of(1, far, ret)
        back_far = exchange(ret_far, devices)
        ret, acc = pairs_of(2, ret, acc_first, acc_second)
        ret = pass_back(second, back_far, ret, homes * chunks, FAR)
        back_near = exchange(ret, devices)
        (acc,) = fold(second, back_far, acc, FAR, 1)
        tgt_grad, src_grad = fold(first, back_near, acc, NEAR, 2)
        return src_grad.reshape(src_embed.shape), tgt_grad.reshape(tgt_embed.shape)

    def unpacked(_):
        return whole_blocks(
            src_embed,
            tgt_embed,
            src_potential,
            tgt_potential,
            src_sizes,
            tgt_sizes,
            pair_counts,
            pairs,
        )

    return lax.cond(info[3, 0] == 0.0, packed, unpacked, 0)


def solution(mesh):
    placed = (
        P(AXES, None, None),
        P(AXES, None, None),
        P(AXES, None),
        P(AXES, None),
        P(AXES),
        P(),
        P(),
        P(),
    )
    return jax.shard_map(
        shards,
        mesh=mesh,
        in_specs=placed,
        out_specs=(P(AXES, None, None), P(AXES, None, None)),
        check_vma=False,
    )
```

```python
import functools
import math

import jax
import jax.numpy as jnp
from jax import lax
from jax.experimental import pallas as pl
from jax.experimental.pallas import tpu as pltpu
from jax.sharding import PartitionSpec as P

AXES = ("gx", "gy")
CHUNK = 16
TILE = 128
VMEM_BYTES = 60 * 1024 * 1024
DEAD = -1e30
NEAR = 8
FAR = 4
PLANES = 128
ROUNDS = 4
STEP = 0.3
epsilon = 0.5


def _params():
    return pltpu.CompilerParams(vmem_limit_bytes=VMEM_BYTES)


def _any():
    return pl.BlockSpec(memory_space=pl.ANY)


def _vmem():
    return pl.BlockSpec(memory_space=pltpu.VMEM)


def _smem():
    return pl.BlockSpec(memory_space=pltpu.SMEM)


def _rows(chunk):
    return pl.ds(pl.multiple_of(chunk * CHUNK, CHUNK), CHUNK)


def pack_kernel(slot_chunks, table, tgt_any, src_any, out, home, sems):
    half = tgt_any.shape[0]
    first = pltpu.make_async_copy(tgt_any, home.at[pl.ds(0, half)], sems.at[0])
    second = pltpu.make_async_copy(src_any, home.at[pl.ds(half, half)], sems.at[1])
    first.start()
    second.start()
    home[pl.ds(2 * half, CHUNK), :] = jnp.zeros((CHUNK, home.shape[1]), home.dtype)
    first.wait()
    second.wait()

    def slot(peer, carry):
        for p in range(slot_chunks):
            out[_rows(peer * slot_chunks + p), :] = home[_rows(table[p, peer]), :]
        return carry

    lax.fori_loop(0, table.shape[1], slot, 0)


def pack(table, tgt_rows, src_rows, slot_chunks):
    peers = table.shape[1]
    width = tgt_rows.shape[1]
    total = peers * slot_chunks * CHUNK
    return pl.pallas_call(
        functools.partial(pack_kernel, slot_chunks),
        out_shape=jax.ShapeDtypeStruct((total, width), tgt_rows.dtype),
        in_specs=[_smem(), _any(), _any()],
        out_specs=_vmem(),
        scratch_shapes=[
            pltpu.VMEM((2 * tgt_rows.shape[0] + CHUNK, width), tgt_rows.dtype),
            pltpu.SemaphoreType.DMA((2,)),
        ],
        compiler_params=_params(),
        name="pack",
    )(table, tgt_rows, src_rows)


def side_rows(potential, live, first):
    shape = (CHUNK, potential.shape[1])
    row = lax.broadcasted_iota(jnp.int32, shape, 0)
    lane = lax.broadcasted_iota(jnp.int32, shape, 1)
    dead = jnp.where(lane < live, 0.0, DEAD)
    pot = jnp.broadcast_to(potential, shape)
    own = 0 if first else 1
    other = 1 - own
    mine = 2 if first else 3
    rows = jnp.where(row == own, pot, jnp.where(row == mine, dead, 1.0))
    rows = jnp.where(row < 4, rows, 0.0)
    return rows.astype(jnp.bfloat16)


def compute_kernel(capacity, scale, phase, far_rows, refs_in, *refs):
    desc, table, pots_in, pots_home, near_any, tgt_any, src_any = refs[:7]
    extra = refs[7:refs_in]
    if phase == 1:
        far_any, ret_before = extra
        ret_near, ret_far, acc = refs[refs_in : refs_in + 3]
    else:
        ret_near, acc = refs[refs_in : refs_in + 2]
    recv, ret, home, items, fill, sems = refs[-6:]
    width = home.shape[1]
    half = tgt_any.shape[0]
    near = near_any.shape[0]
    total = near + far_rows
    copies = [
        pltpu.make_async_copy(tgt_any, home.at[pl.ds(0, half)], sems.at[0]),
        pltpu.make_async_copy(src_any, home.at[pl.ds(half, half)], sems.at[1]),
        pltpu.make_async_copy(near_any, recv.at[pl.ds(0, near)], sems.at[2]),
    ]
    if phase == 1:
        copies += [
            pltpu.make_async_copy(far_any, recv.at[pl.ds(near, far_rows)], sems.at[3]),
            pltpu.make_async_copy(ret_before, ret.at[pl.ds(0, near)], sems.at[4]),
        ]
    if phase == 2:
        (ret_before,) = extra
        copies += [pltpu.make_async_copy(ret_before, ret.at[pl.ds(0, near)], sems.at[4])]
    for copy in copies:
        copy.start()
    recv[pl.ds(total, CHUNK), :] = jnp.zeros((CHUNK, width), recv.dtype)


    def clear(i, carry):
        at = pl.multiple_of(i * capacity, capacity)
        acc[pl.ds(at, capacity), :] = jnp.zeros((capacity, width), jnp.float32)
        return carry

    lax.fori_loop(0, acc.shape[0] // capacity, clear, 0)
    log2e = math.log2(math.e)
    to_exp = log2e / epsilon

    each = TILE // CHUNK

    def pair_of(group, at, size):
        item = items[group, jnp.minimum(at, size - 1)]
        real = at < size
        peer, kind = item // 2, item % 2
        field = kind * 4
        return (
            peer,
            kind,
            desc[field, peer],
            jnp.where(real, desc[field + 1, peer], 0),
            jnp.where(real, desc[field + 2, peer], 0),
            desc[field + 3, peer],
        )

    def some(blocks, count, pairs):
        rights, sides, lefts = [], [], []
        for peer, kind, home_id, live_moved, live_home, start in pairs:
            rights.append(
                jnp.concatenate(
                    [recv[_rows(table[start + j, peer]), :] for j in range(blocks * each)], axis=0
                )
            )
            right_pots = pots_in[pl.ds(pl.multiple_of(peer * 8, 8), 8), :]
            deep = capacity // TILE
            right_pots = jnp.where(kind == 0, right_pots[0:deep, :], right_pots[deep : 2 * deep, :])
            left_pots = pots_home[pl.ds(pl.multiple_of(home_id * 8, 8), 8), :]
            right_side = jnp.concatenate(
                [
                    side_rows(right_pots[b : b + 1, :], live_moved - b * TILE, False)
                    for b in range(blocks)
                ],
                axis=1,
            )
            left_side = [
                side_rows(left_pots[i : i + 1, :], live_home - i * TILE, True)
                for i in range(count)
            ]
            sides.append((left_side, right_side))
            at = pl.multiple_of(home_id * capacity, TILE)
            lefts.append([home[pl.ds(at + i * TILE, TILE), :] for i in range(count)])
        work = [(k, i) for i in range(count) for k in range(len(pairs))]
        sums = [
            lax.dot_general(
                sides[k][0][i],
                sides[k][1],
                (((0,), (0,)), ((), ())),
                preferred_element_type=jnp.float32,
            )
            for k, i in work
        ]
        dots = [
            lax.dot_general(
                lefts[k][i], rights[k], (((1,), (1,)), ((), ())), preferred_element_type=jnp.float32
            )
            for k, i in work
        ]
        weights = []
        for dot, total_pot in zip(dots, sums):
            plan = jnp.exp2(dot * (scale * to_exp) + (total_pot * to_exp - to_exp))
            weights.append(
                (plan * (dot * (scale / epsilon) + (1.0 - 1.0 / epsilon))).astype(jnp.bfloat16)
            )
        pieces = [
            lax.dot_general(
                weight, lefts[k][i], (((0,), (0,)), ((), ())), preferred_element_type=jnp.float32
            )
            for weight, (k, i) in zip(weights, work)
        ]
        grads = [
            jnp.dot(weight, rights[k], preferred_element_type=jnp.float32)
            for weight, (k, i) in zip(weights, work)
        ]
        for k, pair in enumerate(pairs):
            at = pl.multiple_of(pair[2] * capacity, TILE)
            for i in range(count):
                acc[pl.ds(at + i * TILE, TILE), :] += (-scale) * grads[work.index((k, i))]
            piece = functools.reduce(
                jnp.add, [pieces[work.index((k, i))] for i in range(count)]
            ) * (-scale)
            for j in range(blocks * each):
                into = table[pair[5] + j, pair[0]]
                into = jnp.where(j * CHUNK < pair[3], into, total // CHUNK)
                ret[_rows(into), :] = piece[j * CHUNK : (j + 1) * CHUNK, :].astype(ret.dtype)

    deep = capacity // TILE
    for c in range(deep * deep):
        fill[c] = 0

    fill[deep * deep] = 0

    def sort(step, carry):
        for u in range(4):
            peer = step * 4 + u
            for kind in range(2):
                group = desc[8 + kind, peer] - phase * deep * deep
                ours = (group >= 0) & (group < deep * deep)
                group = jnp.where(ours, group, deep * deep)
                at = fill[group]
                items[group, at] = peer * 2 + kind
                fill[group] = at + 1
        return carry

    lax.fori_loop(0, desc.shape[1] // 4, sort, 0)
    for copy in copies:
        copy.wait()
    for b in range(1, deep + 1):
        for c in range(1, deep + 1):
            group = (b - 1) * deep + c - 1
            size = fill[group]

            def two(k, carry, b=b, c=c, group=group, size=size):
                some(b, c, [pair_of(group, 2 * k, size), pair_of(group, 2 * k + 1, size)])
                return carry

            lax.fori_loop(0, (size + 1) // 2, two, 0)

    back = [pltpu.make_async_copy(ret.at[pl.ds(0, near)], ret_near, sems.at[7])]
    if phase == 1:
        back.append(
            pltpu.make_async_copy(ret.at[pl.ds(near, far_rows)], ret_far, sems.at[8])
        )
    for copy in back:
        copy.start()
    for copy in back:
        copy.wait()


def compute(phase, desc, table, pots_in, pots_home, near, tgt_rows, src_rows, capacity, far_rows, extra):
    width = tgt_rows.shape[1]
    scale = width ** (-0.5)
    homes = 2 * tgt_rows.shape[0]
    shapes = [jax.ShapeDtypeStruct(near.shape, near.dtype)]
    if phase == 1:
        shapes.append(jax.ShapeDtypeStruct((far_rows, width), near.dtype))
    shapes.append(jax.ShapeDtypeStruct((homes, width), jnp.float32))
    rows = near.shape[0] + far_rows + CHUNK
    groups = (capacity // TILE) ** 2 + 1
    scratch = [
        pltpu.VMEM((rows, width), near.dtype),
        pltpu.VMEM((rows, width), near.dtype),
        pltpu.VMEM((homes, width), tgt_rows.dtype),
        pltpu.SMEM((groups, 2 * desc.shape[1]), jnp.int32),
        pltpu.SMEM((groups,), jnp.int32),
        pltpu.SemaphoreType.DMA((9,)),
    ]
    work = 4 * desc.shape[1] * capacity * capacity
    return pl.pallas_call(
        functools.partial(compute_kernel, capacity, scale, phase, far_rows, 7 + len(extra)),
        out_shape=tuple(shapes),
        in_specs=[_smem(), _smem(), _vmem(), _vmem()] + [_any()] * (3 + len(extra)),
        out_specs=tuple([_any()] * (len(shapes) - 1) + [_vmem()]),
        scratch_shapes=scratch,
        compiler_params=_params(),
        cost_estimate=pl.CostEstimate(
            flops=work * width, bytes_accessed=8 * homes * width, transcendentals=work // 8
        ),
        name="pairs%d" % phase,
    )(desc, table, pots_in, pots_home, near, tgt_rows, src_rows, *extra)


def pass_on_kernel(slot_chunks, table, tgt_any, src_any, got_any, out, pool, sems):
    half = tgt_any.shape[0]
    homes = 2 * half + CHUNK
    copies = [
        pltpu.make_async_copy(tgt_any, pool.at[pl.ds(0, half)], sems.at[0]),
        pltpu.make_async_copy(src_any, pool.at[pl.ds(half, half)], sems.at[1]),
        pltpu.make_async_copy(got_any, pool.at[pl.ds(homes, got_any.shape[0])], sems.at[2]),
    ]
    for copy in copies:
        copy.start()
    pool[pl.ds(2 * half, CHUNK), :] = jnp.zeros((CHUNK, pool.shape[1]), pool.dtype)
    for copy in copies:
        copy.wait()

    def slot(peer, carry):
        for p in range(slot_chunks):
            out[_rows(peer * slot_chunks + p), :] = pool[_rows(table[p, peer]), :]
        return carry

    lax.fori_loop(0, table.shape[1], slot, 0)


def pass_on(table, tgt_rows, src_rows, got, slot_chunks):
    peers = table.shape[1]
    width = tgt_rows.shape[1]
    return pl.pallas_call(
        functools.partial(pass_on_kernel, slot_chunks),
        out_shape=jax.ShapeDtypeStruct((peers * slot_chunks * CHUNK, width), tgt_rows.dtype),
        in_specs=[_smem(), _any(), _any(), _any()],
        out_specs=_vmem(),
        scratch_shapes=[
            pltpu.VMEM((2 * tgt_rows.shape[0] + CHUNK + got.shape[0], width), tgt_rows.dtype),
            pltpu.SemaphoreType.DMA((3,)),
        ],
        compiler_params=_params(),
        name="pass_on",
    )(table, tgt_rows, src_rows, got)


def pass_back_kernel(slot_chunks, homes, table, got, ret_any, out_any, out, sems):
    rows = ret_any.shape[0]
    first = pltpu.make_async_copy(ret_any, out.at[pl.ds(0, rows)], sems.at[0])
    first.start()
    first.wait()

    def slot(peer, carry):
        for p in range(slot_chunks):
            at = table[p, peer] - (homes + 1)
            at = jnp.where(at < 0, rows // CHUNK, at)
            out[_rows(at), :] = got[_rows(peer * slot_chunks + p), :]
        return carry

    lax.fori_loop(0, table.shape[1], slot, 0)
    second = pltpu.make_async_copy(out.at[pl.ds(0, rows)], out_any, sems.at[1])
    second.start()
    second.wait()


def pass_back(table, got, ret, homes, slot_chunks):
    rows, width = ret.shape
    return pl.pallas_call(
        functools.partial(pass_back_kernel, slot_chunks, homes),
        out_shape=jax.ShapeDtypeStruct(ret.shape, ret.dtype),
        in_specs=[_smem(), _vmem(), _any()],
        out_specs=_any(),
        scratch_shapes=[
            pltpu.VMEM((rows + CHUNK, width), ret.dtype),
            pltpu.SemaphoreType.DMA((2,)),
        ],
        compiler_params=_params(),
        name="pass_back",
    )(table, got, ret)


def fold_kernel(slot_chunks, bases, table, got, *refs):
    accs, outs, (even, odd, base, sems) = refs[:bases], refs[bases:-4], refs[-4:]
    homes = accs[0].shape[0]
    width = accs[0].shape[1]
    first = pltpu.make_async_copy(accs[0], base, sems.at[0])
    first.start()
    for k in range(1, bases):
        sums = (even, odd)[k - 1].at[pl.ds(0, homes)]
        pltpu.make_async_copy(accs[k], sums, sems.at[9 + k]).start()
    for sums in (even, odd):
        sums[pl.ds(homes, CHUNK), :] = jnp.zeros((CHUNK, width), jnp.float32)

    def clear(i, carry):
        at = pl.ds(pl.multiple_of(i * 8 * CHUNK, 8 * CHUNK), 8 * CHUNK)
        even[at, :] = jnp.zeros((8 * CHUNK, even.shape[1]), jnp.float32)
        odd[at, :] = jnp.zeros((8 * CHUNK, odd.shape[1]), jnp.float32)
        return carry

    if bases == 1:
        lax.fori_loop(0, homes // (8 * CHUNK), clear, 0)
    for k in range(1, bases):
        sums = (even, odd)[k - 1].at[pl.ds(0, homes)]
        pltpu.make_async_copy(accs[k], sums, sems.at[9 + k]).wait()

    def slot(peer, carry):
        for p in range(slot_chunks):
            sums = odd if p % 2 else even
            at = _rows(jnp.minimum(table[p, peer], homes // CHUNK))
            sums[at, :] += got[_rows(peer * slot_chunks + p), :].astype(jnp.float32)
        return carry

    lax.fori_loop(0, table.shape[1], slot, 0)
    first.wait()
    pieces = 8
    share = homes // pieces
    per_out = pieces // len(outs)
    copies = []
    for k in range(pieces):

        def join(i, carry, k=k):
            at = pl.ds(pl.multiple_of(k * share + i * 8 * CHUNK, 8 * CHUNK), 8 * CHUNK)
            base[at, :] = base[at, :] + (even[at, :] + odd[at, :])
            return carry

        lax.fori_loop(0, share // (8 * CHUNK), join, 0)
        out = outs[k // per_out]
        into = out.at[pl.ds((k % per_out) * share, share)]
        copies.append(
            pltpu.make_async_copy(base.at[pl.ds(k * share, share)], into, sems.at[k + 1])
        )
        copies[-1].start()
    for copy in copies:
        copy.wait()


def fold(table, got, accs, slot_chunks, parts):
    homes, width = accs[0].shape
    result = jax.ShapeDtypeStruct((homes // parts, width), jnp.float32)
    return pl.pallas_call(
        functools.partial(fold_kernel, slot_chunks, len(accs)),
        out_shape=(result,) * parts,
        in_specs=[_smem(), _vmem()] + [_any()] * len(accs),
        out_specs=(_any(),) * parts,
        scratch_shapes=[
            pltpu.VMEM((homes + CHUNK, width), jnp.float32),
            pltpu.VMEM((homes + CHUNK, width), jnp.float32),
            pltpu.VMEM((homes, width), jnp.float32),
            pltpu.SemaphoreType.DMA((12,)),
        ],
        compiler_params=_params(),
        cost_estimate=pl.CostEstimate(
            flops=homes * width, bytes_accessed=8 * homes * width, transcendentals=0
        ),
        name="fold%d" % parts,
    )(table, got, *accs)


def exchange(blocks, devices):
    shaped = blocks.reshape(devices, -1, blocks.shape[-1])
    got = lax.all_to_all(shaped, AXES, split_axis=0, concat_axis=0, tiled=True)
    return got.reshape(blocks.shape)


def sched_kernel(
    r1,
    r2,
    planes,
    clusters,
    depth,
    me_ref,
    code_ref,
    sizes_ref,
    header_ref,
    t1,
    t2,
    t3,
    desc,
    rest,
    moves,
):
    n = code_ref.shape[0]
    me = me_ref[0]
    last = n - 1
    chunks = clusters * depth
    row = lax.broadcasted_iota(jnp.int32, (n, n), 0)
    col = lax.broadcasted_iota(jnp.int32, (n, n), 1)
    direct = float(r1 + r2)
    code = code_ref[...]
    used = (code & 1).astype(jnp.float32)
    picked = (code // 2) & (clusters - 1)
    local = code // (2 * clusters)
    filler = jnp.zeros((n, n - clusters), jnp.float32)
    by_tgt = jnp.concatenate([sizes_ref[...], filler], axis=1).T
    every = header_ref[:, 6, :] * float(CHUNK) + header_ref[:, 7, :]
    by_src = every.T
    tgt_live = jnp.zeros((n, n), jnp.float32)
    src_live = jnp.zeros((n, n), jnp.float32)
    picked_t = picked.astype(jnp.float32).T
    for c in range(clusters):
        tgt_live = jnp.where(local == c, by_tgt[c : c + 1, :], tgt_live)
        src_live = jnp.where(picked_t == float(c), by_src[c : c + 1, :], src_live)
    src_live = src_live.T

    def ceil_chunks(rows):
        return jnp.floor((rows + (CHUNK - 1.0)) * (1.0 / CHUNK))

    tc = ceil_chunks(tgt_live) * used
    sc = ceil_chunks(src_live) * used
    tct, sct = tc.T, sc.T

    def cost(count, price):
        return price * (
            count + jnp.maximum(count - r1, 0.0) + jnp.maximum(count - direct, 0.0)
        )

    def choose(price):
        back = price.T
        src_tgt = cost(sc + tct, price)
        src_src = cost(sc, price) + cost(sct, back)
        tgt_tgt = cost(tct, price) + cost(tc, back)
        tgt_src = cost(tc + sct, back)
        best = jnp.minimum(jnp.minimum(src_tgt, src_src), jnp.minimum(tgt_tgt, tgt_src))
        src_first = (src_tgt == best) | (src_src == best)
        first = jnp.where(src_first, 0.0, 1.0)
        second = jnp.where(
            src_tgt == best,
            1.0,
            jnp.where(src_src == best, 0.0, jnp.where(tgt_tgt == best, 1.0, 0.0)),
        )
        tgt_moves = jnp.where(row < col, first, second.T)
        tm = tc * tgt_moves
        return tgt_moves, tm, tm.T + sc * (1.0 - tgt_moves)

    def update(_, price):
        load = choose(price)[2]
        sent = jnp.sum(load, axis=1, keepdims=True)
        got = jnp.sum(load, axis=0, keepdims=True)
        mean = jnp.maximum(jnp.sum(got, axis=1, keepdims=True) / n, 1.0)
        return price + STEP * (sent / mean - 1.0) + STEP * (got / mean - 1.0)

    prices = lax.fori_loop(0, ROUNDS, update, jnp.ones_like(tc))
    tgt_moves, tm, load = choose(prices)
    tmt = tm.T
    d1 = jnp.minimum(load, float(r1))
    d2 = jnp.minimum(load - d1, float(r2))
    d12 = d1 + d2
    slack1 = r1 - d1
    slack2 = r2 - d2
    bit = 1
    while bit < n:
        slack1 = jnp.where((row & bit) > 0, pltpu.roll(slack1, n - bit, 1), slack1)
        slack2 = jnp.where((col & bit) > 0, pltpu.roll(slack2, n - bit, 0), slack2)
        bit *= 2
    excess = load - d12
    group = 8

    def more(state):
        return (state[0] < planes) & (state[1] > 0.0)

    def step(state):
        at, _, excess, slack1, slack2 = state
        for k in range(group):
            x = jnp.minimum(jnp.minimum(excess, slack1), slack2)
            moves[at + k] = x
            excess = excess - x
            slack1 = pltpu.roll(slack1 - x, n - 1, 1)
            slack2 = pltpu.roll(slack2 - x, n - 1, 0)
        return at + group, jnp.sum(excess), excess, slack1, slack2

    count, left, _, _, _ = lax.while_loop(
        more, step, (jnp.int32(0), jnp.sum(excess), excess, slack1, slack2)
    )

    def mine(value):
        return jnp.sum(jnp.where(row == me, value, 0.0), axis=0, keepdims=True)

    d1r, d2r, d12r = mine(d1), mine(d2), mine(d12)
    d1c, d2c, d12c = mine(d1.T), mine(d2.T), mine(d12.T)
    tn = mine(tmt)
    local_t = local.astype(jnp.float32).T
    home_row = clusters + mine(picked.astype(jnp.float32))
    home_col = mine(local_t)
    tb = home_col * depth
    sb = home_row * depth - tn
    negate = jnp.where(row == ((n - col) & last), 1.0, 0.0).astype(jnp.bfloat16)
    p1n = jnp.dot(
        jnp.broadcast_to(d1c, (16, n)).astype(jnp.bfloat16),
        negate,
        preferred_element_type=jnp.float32,
    )[0:1, :]
    homes = 2.0 * chunks
    first_n = float(n * r1)
    total = float(n * (r1 + r2))
    lane = lax.broadcasted_iota(jnp.int32, (1, n), 1)
    lane_f = lane.astype(jnp.float32)

    def iota_f(rows):
        return lax.broadcasted_iota(jnp.int32, (rows, n), 0).astype(jnp.float32)

    p1, p2, p3 = iota_f(t1.shape[0]), iota_f(t2.shape[0]), iota_f(t3.shape[0])

    def home_of(q, tn, tb, sb):
        return jnp.where(q < tn, tb + q, sb + q)

    v1 = jnp.where(p1 < d1r, home_of(p1, tn, tb, sb), homes)
    v2 = jnp.where(p2 < d2r, home_of(p2 + d1r, tn, tb, sb), homes)
    v3 = jnp.where(
        p3 < d1c,
        lane_f * r1 + p3,
        jnp.where(p3 < d12c, first_n + lane_f * r2 + p3 - d1c, total),
    )
    pick = jnp.where(
        lax.broadcasted_iota(jnp.int32, (16, n), 1) == me, 1.0, 0.0
    ).astype(jnp.bfloat16)

    def extract(r, state):
        v1, v2, v3, qa, p1a, qb, p2b, p1n, p2c = state
        x = moves[r]
        xa = jnp.sum(jnp.where(row == me, x, 0.0), axis=0, keepdims=True)
        xb = lax.dot_general(
            pick, x.astype(jnp.bfloat16), (((1,), (1,)), ((), ())),
            preferred_element_type=jnp.float32,
        )[0:1, :]
        xc = jnp.sum(
            jnp.where(((row + col + r - me) & last) == 0, x, 0.0), axis=0, keepdims=True
        )
        ahead = (me + r) & last
        back = (n - ahead) & last
        stacked = jnp.concatenate([xa, qa, tn, tb, sb, xa, xa, xa], axis=0)
        turned = pltpu.roll(stacked, ahead, 1)
        xa_c, qa_c = turned[0:1, :], turned[1:2, :]
        at = p1 - p1a
        v1 = jnp.where(
            (at >= 0.0) & (at < xa_c),
            home_of(qa_c + at, turned[2:3, :], turned[3:4, :], turned[4:5, :]),
            v1,
        )
        p1a = p1a + xa_c
        qa = qa + xa
        forth = (me - r) & last
        p1b = pltpu.roll(jnp.broadcast_to(p1n, (8, n)), forth, 1)[0:1, :]
        at = p2 - p2c
        origin = ((me - lane - r) & last).astype(jnp.float32)
        v2 = jnp.where((at >= 0.0) & (at < xc), homes + 1.0 + origin * r1 + p1b + at, v2)
        p2c = p2c + xc
        p1n = p1n + pltpu.roll(jnp.broadcast_to(xc, (8, n)), (n - forth) & last, 1)[0:1, :]
        p2a = pltpu.roll(jnp.broadcast_to(p2b, (8, n)), back, 1)[0:1, :]
        via = ((lane + me + r) & last).astype(jnp.float32)
        at = p3 - qb
        v3 = jnp.where((at >= 0.0) & (at < xb), first_n + via * r2 + p2a + at, v3)
        p2b = p2b + pltpu.roll(jnp.broadcast_to(xb, (8, n)), ahead, 1)[0:1, :]
        qb = qb + xb
        return v1, v2, v3, qa, p1a, qb, p2b, p1n, p2c

    def several(k, state):
        for u in range(group // 2):
            state = extract(k * (group // 2) + u, state)
        return state

    v1, v2, v3 = lax.fori_loop(
        0, count // (group // 2), several, (v1, v2, v3, d12r, d1r, d12c, d2c, p1n, d2r)
    )[:3]
    t1[...] = v1.astype(jnp.int32)
    t2[...] = v2.astype(jnp.int32)
    t3[...] = v3.astype(jnp.int32)
    moves_here = mine(used * tgt_moves) > 0.0
    moves_there = mine((used * (1.0 - tgt_moves)).T) > 0.0
    tgt_end = mine(tm)
    src_rows = mine(src_live.T)
    src_end = tgt_end + ceil_chunks(src_rows)
    early = ((lane & 1) * 2).astype(jnp.float32)
    deep = depth * CHUNK // TILE

    def ceil_tiles(rows):
        return jnp.floor((rows + (TILE - 1.0)) * (1.0 / TILE))

    def group_of(active, end, moved, home):
        phase = jnp.where(end > r1, 1.0, early)
        group = (phase * deep + ceil_tiles(moved) - 1.0) * deep + ceil_tiles(home) - 1.0
        return jnp.where(active, group, -1.0)

    tgt_rows, own_rows, back_rows = mine(tgt_live), mine(src_live), mine(tgt_live.T)
    fields = [
        jnp.where(moves_here, home_row, -1.0),
        tgt_rows,
        own_rows,
        jnp.zeros_like(early),
        jnp.where(moves_there, home_col, -1.0),
        src_rows,
        back_rows,
        tgt_end,
        group_of(moves_here, tgt_end, tgt_rows, own_rows),
        group_of(moves_there, src_end, src_rows, back_rows),
    ]
    for k, field in enumerate(fields):
        desc[k : k + 1, :] = field.astype(jnp.int32)
    rest[...] = jnp.broadcast_to(left, rest.shape)


def schedule(me, code, sizes, header, r1, r2, planes, depth):
    n, clusters = sizes.shape

    def ints(rows):
        return jax.ShapeDtypeStruct((rows, n), jnp.int32)

    return pl.pallas_call(
        functools.partial(sched_kernel, r1, r2, planes, clusters, depth),
        out_shape=(
            ints((r1 + 7) // 8 * 8),
            ints((r2 + 7) // 8 * 8),
            ints(2 * depth),
            ints(10),
            jax.ShapeDtypeStruct((1, n), jnp.float32),
        ),
        in_specs=[_smem(), _vmem(), _vmem(), _vmem()],
        out_specs=(_vmem(),) * 5,
        scratch_shapes=[pltpu.VMEM((planes, n, n), jnp.float32)],
        compiler_params=_params(),
        name="plan",
    )(me, code, sizes, header)


def whole_blocks(
    src_embed, tgt_embed, src_potential, header, src_sizes, tgt_sizes, mine, theirs
):
    devices = mine.shape[0]
    clusters, capacity, width = src_embed.shape
    scale = width ** (-0.5)
    blocks = jnp.take(tgt_embed, theirs // (2 * clusters), axis=0)
    blocks = lax.all_to_all(blocks, AXES, split_axis=0, concat_axis=0, tiled=True)
    row_ids = jnp.arange(capacity, dtype=jnp.int32)

    def one(peer, carry):
        src_grad, parts = carry
        c = (mine[peer] // 2) % clusters
        t = peer * clusters + mine[peer] // (2 * clusters)
        src_block, tgt_block = src_embed[c], blocks[peer]
        right = header[peer, : capacity // TILE].reshape(capacity)
        dots = jnp.dot(src_block, tgt_block.T, preferred_element_type=jnp.float32) * scale
        plan = jnp.exp(
            (src_potential[c].astype(jnp.float32)[:, None] + right[None, :] - (1.0 - dots))
            / epsilon
        )
        live = (row_ids[:, None] < src_sizes[c]) & (row_ids[None, :] < tgt_sizes[t])
        live = live & (mine[peer] % 2 > 0)
        weight = jnp.where(live, plan * (1.0 - (1.0 - dots) / epsilon), 0.0).astype(jnp.bfloat16)
        grad = -jnp.dot(weight, tgt_block, preferred_element_type=jnp.float32) * scale
        part = -jnp.dot(weight.T, src_block, preferred_element_type=jnp.float32) * scale
        return src_grad.at[c].add(grad), parts.at[peer].set(part.astype(jnp.bfloat16))

    src_grad, parts = lax.fori_loop(
        0, devices, one, (jnp.zeros(src_embed.shape, jnp.float32), jnp.zeros_like(blocks))
    )
    parts = lax.all_to_all(parts, AXES, split_axis=0, concat_axis=0, tiled=True)

    def back(peer, tgt_grad):
        return tgt_grad.at[theirs[peer] // (2 * clusters)].add(
            jnp.where(theirs[peer] % 2 > 0, parts[peer].astype(jnp.float32), 0.0)
        )

    tgt_grad = lax.fori_loop(0, devices, back, jnp.zeros(tgt_embed.shape, jnp.float32))
    return src_grad, tgt_grad


def shards(
    src_embed, tgt_embed, src_potential, tgt_potential, src_sizes, tgt_sizes, pair_counts, pairs
):
    devices = lax.axis_size(AXES)
    me = lax.axis_index(AXES)
    clusters, capacity, width = src_embed.shape
    fanout = pairs.shape[1]
    chunks = capacity // CHUNK
    blocks = capacity // TILE
    peer_ids = jnp.arange(devices, dtype=jnp.int32)
    cluster_ids = jnp.arange(clusters, dtype=jnp.int32)
    fan_ids = jnp.arange(fanout, dtype=jnp.int32)
    listed = pairs.T.reshape(fanout, devices, clusters)
    counts = pair_counts.reshape(devices, clusters)
    code = (fan_ids[:, None, None] < counts[None]).astype(jnp.int32) * (
        1 + 2 * cluster_ids[None, None, :] + 2 * clusters * (listed % clusters)
    )
    matrix = jnp.sum(
        jnp.where((listed // clusters)[..., None] == peer_ids, code[..., None], 0), axis=(0, 2)
    )
    mine = lax.dynamic_index_in_dim(matrix, me, 0, keepdims=False)
    theirs = lax.dynamic_index_in_dim(matrix, me, 1, keepdims=False)
    in_home = (mine // 2) % clusters
    out_local = theirs // (2 * clusters)
    sizes_row = jnp.stack([src_sizes // CHUNK, src_sizes % CHUNK]).astype(jnp.bfloat16)
    sizes_row = jnp.pad(sizes_row, ((0, 0), (0, TILE - clusters)))
    header = jnp.concatenate(
        [
            jnp.take(tgt_potential, out_local, axis=0).reshape(devices, blocks, TILE),
            jnp.take(src_potential, in_home, axis=0).reshape(devices, blocks, TILE),
            jnp.broadcast_to(sizes_row[None], (devices, 2, TILE)),
        ],
        axis=1,
    )
    header = lax.all_to_all(header, AXES, split_axis=0, concat_axis=0, tiled=True)
    header = header.astype(jnp.float32)
    first, second, third, desc, rest = schedule(
        me.reshape(1).astype(jnp.int32),
        matrix,
        tgt_sizes.reshape(devices, clusters).astype(jnp.float32),
        header,
        NEAR,
        FAR,
        PLANES,
        chunks,
    )
    homes = 2 * clusters
    pots_home = jnp.concatenate([tgt_potential, src_potential], axis=0).reshape(
        homes, blocks, TILE
    )
    pots_home = (
        jnp.pad(pots_home, ((0, 0), (0, 8 - blocks), (0, 0)))
        .astype(jnp.float32)
        .reshape(homes * 8, TILE)
    )

    def packed(_):
        tgt_rows = tgt_embed.reshape(clusters * capacity, width)
        src_rows = src_embed.reshape(clusters * capacity, width)
        near = exchange(pack(first, tgt_rows, src_rows, NEAR), devices)
        far = exchange(pass_on(second, tgt_rows, src_rows, near, FAR), devices)

        def pairs_of(phase, *extra):
            return compute(
                phase,
                desc,
                third,
                header.reshape(devices * 8, TILE),
                pots_home,
                near,
                tgt_rows,
                src_rows,
                capacity,
                devices * FAR * CHUNK,
                extra,
            )

        ret, acc_first = pairs_of(0)
        ret, ret_far, acc_second = pairs_of(1, far, ret)
        back_far = exchange(ret_far, devices)
        ret, acc_third = pairs_of(2, ret)
        ret = pass_back(second, back_far, ret, homes * chunks, FAR)
        back_near = exchange(ret, devices)
        (acc,) = fold(second, back_far, (acc_first, acc_second, acc_third), FAR, 1)
        tgt_grad, src_grad = fold(first, back_near, (acc,), NEAR, 2)
        return src_grad.reshape(src_embed.shape), tgt_grad.reshape(tgt_embed.shape)

    def unpacked(_):
        return whole_blocks(
            src_embed, tgt_embed, src_potential, header, src_sizes, tgt_sizes, mine, theirs
        )

    return lax.cond(rest[0, 0] == 0.0, packed, unpacked, 0)


def solution(mesh):
    placed = (
        P(AXES, None, None),
        P(AXES, None, None),
        P(AXES, None),
        P(AXES, None),
        P(AXES),
        P(),
        P(),
        P(),
    )
    return jax.shard_map(
        shards,
        mesh=mesh,
        in_specs=placed,
        out_specs=(P(AXES, None, None), P(AXES, None, None)),
        check_vma=False,
    )
```

```python
import functools
import math

import jax
import jax.numpy as jnp
from jax import lax
from jax.experimental import pallas as pl
from jax.experimental.pallas import tpu as pltpu
from jax.sharding import PartitionSpec as P

AXES = ("gx", "gy")
CHUNK = 16
TILE = 128
VMEM_BYTES = 60 * 1024 * 1024
DEAD = -1e30
NEAR = 8
FAR = 4
PLANES = 128
ROUNDS = 4
STEP = 0.3
UNROLL = 1
epsilon = 0.5


def _params():
    return pltpu.CompilerParams(vmem_limit_bytes=VMEM_BYTES)


def _any():
    return pl.BlockSpec(memory_space=pl.ANY)


def _vmem():
    return pl.BlockSpec(memory_space=pltpu.VMEM)


def _smem():
    return pl.BlockSpec(memory_space=pltpu.SMEM)


def _rows(chunk):
    return pl.ds(pl.multiple_of(chunk * CHUNK, CHUNK), CHUNK)


def slots(one, step, carry):
    for u in range(UNROLL):
        carry = one(step * UNROLL + u, carry)
    return carry


def pack_kernel(slot_chunks, table, tgt_any, src_any, out, home, sems):
    half = tgt_any.shape[0]
    first = pltpu.make_async_copy(tgt_any, home.at[pl.ds(0, half)], sems.at[0])
    second = pltpu.make_async_copy(src_any, home.at[pl.ds(half, half)], sems.at[1])
    first.start()
    second.start()
    home[pl.ds(2 * half, CHUNK), :] = jnp.zeros((CHUNK, home.shape[1]), home.dtype)
    first.wait()
    second.wait()

    def slot(peer, carry):
        rows = [home[_rows(table[p, peer]), :] for p in range(slot_chunks)]
        for p in range(slot_chunks):
            out[_rows(peer * slot_chunks + p), :] = rows[p]
        return carry

    lax.fori_loop(0, table.shape[1] // UNROLL, functools.partial(slots, slot), 0)


def pack(table, tgt_rows, src_rows, slot_chunks):
    peers = table.shape[1]
    width = tgt_rows.shape[1]
    total = peers * slot_chunks * CHUNK
    return pl.pallas_call(
        functools.partial(pack_kernel, slot_chunks),
        out_shape=jax.ShapeDtypeStruct((total, width), tgt_rows.dtype),
        in_specs=[_smem(), _any(), _any()],
        out_specs=_vmem(),
        scratch_shapes=[
            pltpu.VMEM((2 * tgt_rows.shape[0] + CHUNK, width), tgt_rows.dtype),
            pltpu.SemaphoreType.DMA((2,)),
        ],
        compiler_params=_params(),
        name="pack",
    )(table, tgt_rows, src_rows)


def side_rows(potential, live, first):
    shape = (CHUNK, potential.shape[1])
    row = lax.broadcasted_iota(jnp.int32, shape, 0)
    lane = lax.broadcasted_iota(jnp.int32, shape, 1)
    dead = jnp.where(lane < live, 0.0, DEAD)
    pot = jnp.broadcast_to(potential, shape)
    own = 0 if first else 1
    other = 1 - own
    mine = 2 if first else 3
    rows = jnp.where(row == own, pot, jnp.where(row == mine, dead, 1.0))
    rows = jnp.where(row < 4, rows, 0.0)
    return rows.astype(jnp.bfloat16)


def compute_kernel(capacity, scale, phase, far_rows, refs_in, *refs):
    desc, table, pots_in, pots_home, near_any, tgt_any, src_any = refs[:7]
    extra = refs[7:refs_in]
    if phase == 1:
        far_any, ret_before = extra
        ret_near, ret_far, acc = refs[refs_in : refs_in + 3]
    else:
        ret_near, acc = refs[refs_in : refs_in + 2]
    recv, ret, home, items, fill, sems = refs[-6:]
    width = home.shape[1]
    half = tgt_any.shape[0]
    near = near_any.shape[0]
    total = near + far_rows
    copies = [
        pltpu.make_async_copy(tgt_any, home.at[pl.ds(0, half)], sems.at[0]),
        pltpu.make_async_copy(src_any, home.at[pl.ds(half, half)], sems.at[1]),
        pltpu.make_async_copy(near_any, recv.at[pl.ds(0, near)], sems.at[2]),
    ]
    if phase == 1:
        copies += [
            pltpu.make_async_copy(far_any, recv.at[pl.ds(near, far_rows)], sems.at[3]),
            pltpu.make_async_copy(ret_before, ret.at[pl.ds(0, near)], sems.at[4]),
        ]
    if phase == 2:
        (ret_before,) = extra
        copies += [pltpu.make_async_copy(ret_before, ret.at[pl.ds(0, near)], sems.at[4])]
    for copy in copies:
        copy.start()
    recv[pl.ds(total, CHUNK), :] = jnp.zeros((CHUNK, width), recv.dtype)


    def clear(i, carry):
        at = pl.multiple_of(i * capacity, capacity)
        acc[pl.ds(at, capacity), :] = jnp.zeros((capacity, width), jnp.float32)
        return carry

    lax.fori_loop(0, acc.shape[0] // capacity, clear, 0)
    log2e = math.log2(math.e)
    to_exp = log2e / epsilon

    each = TILE // CHUNK

    def pair_of(group, at, size):
        item = items[group, jnp.minimum(at, size - 1)]
        real = at < size
        peer, kind = item // 2, item % 2
        field = kind * 4
        return (
            peer,
            kind,
            desc[field, peer],
            jnp.where(real, desc[field + 1, peer], 0),
            jnp.where(real, desc[field + 2, peer], 0),
            desc[field + 3, peer],
        )

    def some(blocks, count, pairs):
        rights, sides, lefts = [], [], []
        for peer, kind, home_id, live_moved, live_home, start in pairs:
            rights.append(
                jnp.concatenate(
                    [recv[_rows(table[start + j, peer]), :] for j in range(blocks * each)], axis=0
                )
            )
            right_pots = pots_in[pl.ds(pl.multiple_of(peer * 8, 8), 8), :]
            deep = capacity // TILE
            right_pots = jnp.where(kind == 0, right_pots[0:deep, :], right_pots[deep : 2 * deep, :])
            left_pots = pots_home[pl.ds(pl.multiple_of(home_id * 8, 8), 8), :]
            right_side = jnp.concatenate(
                [
                    side_rows(right_pots[b : b + 1, :], live_moved - b * TILE, False)
                    for b in range(blocks)
                ],
                axis=1,
            )
            left_side = [
                side_rows(left_pots[i : i + 1, :], live_home - i * TILE, True)
                for i in range(count)
            ]
            sides.append((left_side, right_side))
            at = pl.multiple_of(home_id * capacity, TILE)
            lefts.append([home[pl.ds(at + i * TILE, TILE), :] for i in range(count)])
        work = [(k, i) for i in range(count) for k in range(len(pairs))]
        sums = [
            lax.dot_general(
                sides[k][0][i],
                sides[k][1],
                (((0,), (0,)), ((), ())),
                preferred_element_type=jnp.float32,
            )
            for k, i in work
        ]
        dots = [
            lax.dot_general(
                lefts[k][i], rights[k], (((1,), (1,)), ((), ())), preferred_element_type=jnp.float32
            )
            for k, i in work
        ]
        weights = []
        for dot, total_pot in zip(dots, sums):
            plan = jnp.exp2(dot * (scale * to_exp) + (total_pot * to_exp - to_exp))
            weights.append(
                (plan * (dot * (scale / epsilon) + (1.0 - 1.0 / epsilon))).astype(jnp.bfloat16)
            )
        pieces = [
            lax.dot_general(
                weight, lefts[k][i], (((0,), (0,)), ((), ())), preferred_element_type=jnp.float32
            )
            for weight, (k, i) in zip(weights, work)
        ]
        grads = [
            jnp.dot(weight, rights[k], preferred_element_type=jnp.float32)
            for weight, (k, i) in zip(weights, work)
        ]
        for k, pair in enumerate(pairs):
            at = pl.multiple_of(pair[2] * capacity, TILE)
            for i in range(count):
                acc[pl.ds(at + i * TILE, TILE), :] += (-scale) * grads[work.index((k, i))]
            piece = functools.reduce(
                jnp.add, [pieces[work.index((k, i))] for i in range(count)]
            ) * (-scale)
            for j in range(blocks * each):
                into = table[pair[5] + j, pair[0]]
                into = jnp.where(j * CHUNK < pair[3], into, total // CHUNK)
                ret[_rows(into), :] = piece[j * CHUNK : (j + 1) * CHUNK, :].astype(ret.dtype)

    deep = capacity // TILE
    for c in range(deep * deep):
        fill[c] = 0

    fill[deep * deep] = 0

    def sort(step, carry):
        for u in range(4):
            peer = step * 4 + u
            for kind in range(2):
                group = desc[8 + kind, peer] - phase * deep * deep
                ours = (group >= 0) & (group < deep * deep)
                group = jnp.where(ours, group, deep * deep)
                at = fill[group]
                items[group, at] = peer * 2 + kind
                fill[group] = at + 1
        return carry

    lax.fori_loop(0, desc.shape[1] // 4, sort, 0)
    for copy in copies:
        copy.wait()
    for b in range(1, deep + 1):
        for c in range(1, deep + 1):
            group = (b - 1) * deep + c - 1
            size = fill[group]

            def two(k, carry, b=b, c=c, group=group, size=size):
                some(b, c, [pair_of(group, 2 * k, size), pair_of(group, 2 * k + 1, size)])
                return carry

            lax.fori_loop(0, (size + 1) // 2, two, 0)

    back = [pltpu.make_async_copy(ret.at[pl.ds(0, near)], ret_near, sems.at[7])]
    if phase == 1:
        back.append(
            pltpu.make_async_copy(ret.at[pl.ds(near, far_rows)], ret_far, sems.at[8])
        )
    for copy in back:
        copy.start()
    for copy in back:
        copy.wait()


def compute(phase, desc, table, pots_in, pots_home, near, tgt_rows, src_rows, capacity, far_rows, extra):
    width = tgt_rows.shape[1]
    scale = width ** (-0.5)
    homes = 2 * tgt_rows.shape[0]
    shapes = [jax.ShapeDtypeStruct(near.shape, near.dtype)]
    if phase == 1:
        shapes.append(jax.ShapeDtypeStruct((far_rows, width), near.dtype))
    shapes.append(jax.ShapeDtypeStruct((homes, width), jnp.float32))
    rows = near.shape[0] + far_rows + CHUNK
    groups = (capacity // TILE) ** 2 + 1
    scratch = [
        pltpu.VMEM((rows, width), near.dtype),
        pltpu.VMEM((rows, width), near.dtype),
        pltpu.VMEM((homes, width), tgt_rows.dtype),
        pltpu.SMEM((groups, 2 * desc.shape[1]), jnp.int32),
        pltpu.SMEM((groups,), jnp.int32),
        pltpu.SemaphoreType.DMA((9,)),
    ]
    work = 4 * desc.shape[1] * capacity * capacity
    return pl.pallas_call(
        functools.partial(compute_kernel, capacity, scale, phase, far_rows, 7 + len(extra)),
        out_shape=tuple(shapes),
        in_specs=[_smem(), _smem(), _vmem(), _vmem()] + [_any()] * (3 + len(extra)),
        out_specs=tuple([_any()] * (len(shapes) - 1) + [_vmem()]),
        scratch_shapes=scratch,
        compiler_params=_params(),
        cost_estimate=pl.CostEstimate(
            flops=work * width, bytes_accessed=8 * homes * width, transcendentals=work // 8
        ),
        name="pairs%d" % phase,
    )(desc, table, pots_in, pots_home, near, tgt_rows, src_rows, *extra)


def pass_on_kernel(slot_chunks, table, tgt_any, src_any, got_any, out, pool, sems):
    half = tgt_any.shape[0]
    homes = 2 * half + CHUNK
    copies = [
        pltpu.make_async_copy(tgt_any, pool.at[pl.ds(0, half)], sems.at[0]),
        pltpu.make_async_copy(src_any, pool.at[pl.ds(half, half)], sems.at[1]),
        pltpu.make_async_copy(got_any, pool.at[pl.ds(homes, got_any.shape[0])], sems.at[2]),
    ]
    for copy in copies:
        copy.start()
    pool[pl.ds(2 * half, CHUNK), :] = jnp.zeros((CHUNK, pool.shape[1]), pool.dtype)
    for copy in copies:
        copy.wait()

    def slot(peer, carry):
        rows = [pool[_rows(table[p, peer]), :] for p in range(slot_chunks)]
        for p in range(slot_chunks):
            out[_rows(peer * slot_chunks + p), :] = rows[p]
        return carry

    lax.fori_loop(0, table.shape[1] // UNROLL, functools.partial(slots, slot), 0)


def pass_on(table, tgt_rows, src_rows, got, slot_chunks):
    peers = table.shape[1]
    width = tgt_rows.shape[1]
    return pl.pallas_call(
        functools.partial(pass_on_kernel, slot_chunks),
        out_shape=jax.ShapeDtypeStruct((peers * slot_chunks * CHUNK, width), tgt_rows.dtype),
        in_specs=[_smem(), _any(), _any(), _any()],
        out_specs=_vmem(),
        scratch_shapes=[
            pltpu.VMEM((2 * tgt_rows.shape[0] + CHUNK + got.shape[0], width), tgt_rows.dtype),
            pltpu.SemaphoreType.DMA((3,)),
        ],
        compiler_params=_params(),
        name="pass_on",
    )(table, tgt_rows, src_rows, got)


def pass_back_kernel(slot_chunks, homes, table, got, ret_any, out_any, out, sems):
    rows = ret_any.shape[0]
    first = pltpu.make_async_copy(ret_any, out.at[pl.ds(0, rows)], sems.at[0])
    first.start()
    first.wait()

    def slot(peer, carry):
        ats = [table[p, peer] - (homes + 1) for p in range(slot_chunks)]
        parts = [got[_rows(peer * slot_chunks + p), :] for p in range(slot_chunks)]
        for at, part in zip(ats, parts):
            out[_rows(jnp.where(at < 0, rows // CHUNK, at)), :] = part
        return carry

    lax.fori_loop(0, table.shape[1] // UNROLL, functools.partial(slots, slot), 0)
    second = pltpu.make_async_copy(out.at[pl.ds(0, rows)], out_any, sems.at[1])
    second.start()
    second.wait()


def pass_back(table, got, ret, homes, slot_chunks):
    rows, width = ret.shape
    return pl.pallas_call(
        functools.partial(pass_back_kernel, slot_chunks, homes),
        out_shape=jax.ShapeDtypeStruct(ret.shape, ret.dtype),
        in_specs=[_smem(), _vmem(), _any()],
        out_specs=_any(),
        scratch_shapes=[
            pltpu.VMEM((rows + CHUNK, width), ret.dtype),
            pltpu.SemaphoreType.DMA((2,)),
        ],
        compiler_params=_params(),
        name="pass_back",
    )(table, got, ret)


def fold_kernel(slot_chunks, bases, table, got, *refs):
    accs, outs, (even, odd, base, sems) = refs[:bases], refs[bases:-4], refs[-4:]
    homes = accs[0].shape[0]
    width = accs[0].shape[1]
    first = pltpu.make_async_copy(accs[0], base, sems.at[0])
    first.start()
    for k in range(1, bases):
        sums = (even, odd)[k - 1].at[pl.ds(0, homes)]
        pltpu.make_async_copy(accs[k], sums, sems.at[9 + k]).start()
    for sums in (even, odd):
        sums[pl.ds(homes, CHUNK), :] = jnp.zeros((CHUNK, width), jnp.float32)

    def clear(i, carry):
        at = pl.ds(pl.multiple_of(i * 8 * CHUNK, 8 * CHUNK), 8 * CHUNK)
        even[at, :] = jnp.zeros((8 * CHUNK, even.shape[1]), jnp.float32)
        odd[at, :] = jnp.zeros((8 * CHUNK, odd.shape[1]), jnp.float32)
        return carry

    if bases == 1:
        lax.fori_loop(0, homes // (8 * CHUNK), clear, 0)
    for k in range(1, bases):
        sums = (even, odd)[k - 1].at[pl.ds(0, homes)]
        pltpu.make_async_copy(accs[k], sums, sems.at[9 + k]).wait()

    def slot(peer, carry):
        ats = [
            _rows(jnp.minimum(table[p, peer], homes // CHUNK)) for p in range(slot_chunks)
        ]
        parts = [
            got[_rows(peer * slot_chunks + p), :].astype(jnp.float32) for p in range(slot_chunks)
        ]
        for p in range(0, slot_chunks, 2):
            one = even[ats[p], :] + parts[p]
            two = odd[ats[p + 1], :] + parts[p + 1]
            even[ats[p], :] = one
            odd[ats[p + 1], :] = two
        return carry

    lax.fori_loop(0, table.shape[1] // UNROLL, functools.partial(slots, slot), 0)
    first.wait()
    pieces = 8
    share = homes // pieces
    per_out = pieces // len(outs)
    copies = []
    for k in range(pieces):

        def join(i, carry, k=k):
            at = pl.ds(pl.multiple_of(k * share + i * 8 * CHUNK, 8 * CHUNK), 8 * CHUNK)
            base[at, :] = base[at, :] + (even[at, :] + odd[at, :])
            return carry

        lax.fori_loop(0, share // (8 * CHUNK), join, 0)
        out = outs[k // per_out]
        into = out.at[pl.ds((k % per_out) * share, share)]
        copies.append(
            pltpu.make_async_copy(base.at[pl.ds(k * share, share)], into, sems.at[k + 1])
        )
        copies[-1].start()
    for copy in copies:
        copy.wait()


def fold(table, got, accs, slot_chunks, parts):
    homes, width = accs[0].shape
    result = jax.ShapeDtypeStruct((homes // parts, width), jnp.float32)
    return pl.pallas_call(
        functools.partial(fold_kernel, slot_chunks, len(accs)),
        out_shape=(result,) * parts,
        in_specs=[_smem(), _vmem()] + [_any()] * len(accs),
        out_specs=(_any(),) * parts,
        scratch_shapes=[
            pltpu.VMEM((homes + CHUNK, width), jnp.float32),
            pltpu.VMEM((homes + CHUNK, width), jnp.float32),
            pltpu.VMEM((homes, width), jnp.float32),
            pltpu.SemaphoreType.DMA((12,)),
        ],
        compiler_params=_params(),
        cost_estimate=pl.CostEstimate(
            flops=homes * width, bytes_accessed=8 * homes * width, transcendentals=0
        ),
        name="fold%d" % parts,
    )(table, got, *accs)


def exchange(blocks, devices):
    shaped = blocks.reshape(devices, -1, blocks.shape[-1])
    got = lax.all_to_all(shaped, AXES, split_axis=0, concat_axis=0, tiled=True)
    return got.reshape(blocks.shape)


def sched_kernel(
    r1,
    r2,
    planes,
    clusters,
    depth,
    me_ref,
    code_ref,
    sizes_ref,
    header_ref,
    t1,
    t2,
    t3,
    desc,
    rest,
    moves,
):
    n = code_ref.shape[0]
    me = me_ref[0]
    last = n - 1
    chunks = clusters * depth
    row = lax.broadcasted_iota(jnp.int32, (n, n), 0)
    col = lax.broadcasted_iota(jnp.int32, (n, n), 1)
    direct = float(r1 + r2)
    code = code_ref[...]
    used = (code & 1).astype(jnp.float32)
    picked = (code // 2) & (clusters - 1)
    local = code // (2 * clusters)
    filler = jnp.zeros((n, n - clusters), jnp.float32)
    by_tgt = jnp.concatenate([sizes_ref[...], filler], axis=1).T
    every = header_ref[:, 6, :] * float(CHUNK) + header_ref[:, 7, :]
    by_src = every.T
    tgt_live = jnp.zeros((n, n), jnp.float32)
    src_live = jnp.zeros((n, n), jnp.float32)
    picked_t = picked.astype(jnp.float32).T
    for c in range(clusters):
        tgt_live = jnp.where(local == c, by_tgt[c : c + 1, :], tgt_live)
        src_live = jnp.where(picked_t == float(c), by_src[c : c + 1, :], src_live)
    src_live = src_live.T

    def ceil_chunks(rows):
        return jnp.floor((rows + (CHUNK - 1.0)) * (1.0 / CHUNK))

    tc = ceil_chunks(tgt_live) * used
    sc = ceil_chunks(src_live) * used
    tct, sct = tc.T, sc.T

    def cost(count, price):
        return price * (
            count + jnp.maximum(count - r1, 0.0) + jnp.maximum(count - direct, 0.0)
        )

    def choose(price):
        back = price.T
        src_tgt = cost(sc + tct, price)
        src_src = cost(sc, price) + cost(sct, back)
        tgt_tgt = cost(tct, price) + cost(tc, back)
        tgt_src = cost(tc + sct, back)
        best = jnp.minimum(jnp.minimum(src_tgt, src_src), jnp.minimum(tgt_tgt, tgt_src))
        src_first = (src_tgt == best) | (src_src == best)
        first = jnp.where(src_first, 0.0, 1.0)
        second = jnp.where(
            src_tgt == best,
            1.0,
            jnp.where(src_src == best, 0.0, jnp.where(tgt_tgt == best, 1.0, 0.0)),
        )
        tgt_moves = jnp.where(row < col, first, second.T)
        tm = tc * tgt_moves
        return tgt_moves, tm, tm.T + sc * (1.0 - tgt_moves)

    def update(_, price):
        load = choose(price)[2]
        sent = jnp.sum(load, axis=1, keepdims=True)
        got = jnp.sum(load, axis=0, keepdims=True)
        mean = jnp.maximum(jnp.sum(got, axis=1, keepdims=True) / n, 1.0)
        return price + STEP * (sent / mean - 1.0) + STEP * (got / mean - 1.0)

    prices = lax.fori_loop(0, ROUNDS, update, jnp.ones_like(tc))
    tgt_moves, tm, load = choose(prices)
    tmt = tm.T
    d1 = jnp.minimum(load, float(r1))
    d2 = jnp.minimum(load - d1, float(r2))
    d12 = d1 + d2
    slack1 = r1 - d1
    slack2 = r2 - d2
    bit = 1
    while bit < n:
        slack1 = jnp.where((row & bit) > 0, pltpu.roll(slack1, n - bit, 1), slack1)
        slack2 = jnp.where((col & bit) > 0, pltpu.roll(slack2, n - bit, 0), slack2)
        bit *= 2
    excess = load - d12
    group = 8

    def more(state):
        return (state[0] < planes) & (state[1] > 0.0)

    def step(state):
        at, _, excess, slack1, slack2 = state
        for k in range(group):
            x = jnp.minimum(jnp.minimum(excess, slack1), slack2)
            moves[at + k] = x
            excess = excess - x
            slack1 = pltpu.roll(slack1 - x, n - 1, 1)
            slack2 = pltpu.roll(slack2 - x, n - 1, 0)
        return at + group, jnp.sum(excess), excess, slack1, slack2

    count, left, _, _, _ = lax.while_loop(
        more, step, (jnp.int32(0), jnp.sum(excess), excess, slack1, slack2)
    )

    def mine(value):
        return jnp.sum(jnp.where(row == me, value, 0.0), axis=0, keepdims=True)

    d1r, d2r, d12r = mine(d1), mine(d2), mine(d12)
    d1c, d2c, d12c = mine(d1.T), mine(d2.T), mine(d12.T)
    tn = mine(tmt)
    local_t = local.astype(jnp.float32).T
    home_row = clusters + mine(picked.astype(jnp.float32))
    home_col = mine(local_t)
    tb = home_col * depth
    sb = home_row * depth - tn
    negate = jnp.where(row == ((n - col) & last), 1.0, 0.0).astype(jnp.bfloat16)
    p1n = jnp.dot(
        jnp.broadcast_to(d1c, (16, n)).astype(jnp.bfloat16),
        negate,
        preferred_element_type=jnp.float32,
    )[0:1, :]
    homes = 2.0 * chunks
    first_n = float(n * r1)
    total = float(n * (r1 + r2))
    lane = lax.broadcasted_iota(jnp.int32, (1, n), 1)
    lane_f = lane.astype(jnp.float32)

    def iota_f(rows):
        return lax.broadcasted_iota(jnp.int32, (rows, n), 0).astype(jnp.float32)

    p1, p2, p3 = iota_f(t1.shape[0]), iota_f(t2.shape[0]), iota_f(t3.shape[0])

    def home_of(q, tn, tb, sb):
        return jnp.where(q < tn, tb + q, sb + q)

    v1 = jnp.where(p1 < d1r, home_of(p1, tn, tb, sb), homes)
    v2 = jnp.where(p2 < d2r, home_of(p2 + d1r, tn, tb, sb), homes)
    v3 = jnp.where(
        p3 < d1c,
        lane_f * r1 + p3,
        jnp.where(p3 < d12c, first_n + lane_f * r2 + p3 - d1c, total),
    )
    pick = jnp.where(
        lax.broadcasted_iota(jnp.int32, (16, n), 1) == me, 1.0, 0.0
    ).astype(jnp.bfloat16)

    spread = (row + col - me) & last

    def extract(r, state):
        v1, v2, v3, qa, p1a, qb, p2b, p1n, p2c = state
        x = moves[r]
        xa = moves[r, pl.ds(me, 1), :]
        xb = lax.dot_general(
            pick, x.astype(jnp.bfloat16), (((1,), (1,)), ((), ())),
            preferred_element_type=jnp.float32,
        )[0:1, :]
        xc = jnp.sum(jnp.where(spread == ((n - r) & last), x, 0.0), axis=0, keepdims=True)
        ahead = (me + r) & last
        back = (n - ahead) & last
        stacked = jnp.concatenate([xa, qa, tn, tb, sb, xa, xa, xa], axis=0)
        turned = pltpu.roll(stacked, ahead, 1)
        xa_c, qa_c = turned[0:1, :], turned[1:2, :]
        at = p1 - p1a
        v1 = jnp.where(
            (at >= 0.0) & (at < xa_c),
            home_of(qa_c + at, turned[2:3, :], turned[3:4, :], turned[4:5, :]),
            v1,
        )
        p1a = p1a + xa_c
        qa = qa + xa
        forth = (me - r) & last
        p1b = pltpu.roll(jnp.broadcast_to(p1n, (8, n)), forth, 1)[0:1, :]
        at = p2 - p2c
        origin = ((me - lane - r) & last).astype(jnp.float32)
        v2 = jnp.where((at >= 0.0) & (at < xc), homes + 1.0 + origin * r1 + p1b + at, v2)
        p2c = p2c + xc
        p1n = p1n + pltpu.roll(jnp.broadcast_to(xc, (8, n)), (n - forth) & last, 1)[0:1, :]
        p2a = pltpu.roll(jnp.broadcast_to(p2b, (8, n)), back, 1)[0:1, :]
        via = ((lane + me + r) & last).astype(jnp.float32)
        at = p3 - qb
        v3 = jnp.where((at >= 0.0) & (at < xb), first_n + via * r2 + p2a + at, v3)
        p2b = p2b + pltpu.roll(jnp.broadcast_to(xb, (8, n)), ahead, 1)[0:1, :]
        qb = qb + xb
        return v1, v2, v3, qa, p1a, qb, p2b, p1n, p2c

    def several(k, state):
        for u in range(group // 2):
            state = extract(k * (group // 2) + u, state)
        return state

    v1, v2, v3 = lax.fori_loop(
        0, count // (group // 2), several, (v1, v2, v3, d12r, d1r, d12c, d2c, p1n, d2r)
    )[:3]
    t1[...] = v1.astype(jnp.int32)
    t2[...] = v2.astype(jnp.int32)
    t3[...] = v3.astype(jnp.int32)
    moves_here = mine(used * tgt_moves) > 0.0
    moves_there = mine((used * (1.0 - tgt_moves)).T) > 0.0
    tgt_end = mine(tm)
    src_rows = mine(src_live.T)
    src_end = tgt_end + ceil_chunks(src_rows)
    early = ((lane & 1) * 2).astype(jnp.float32)
    deep = depth * CHUNK // TILE

    def ceil_tiles(rows):
        return jnp.floor((rows + (TILE - 1.0)) * (1.0 / TILE))

    def group_of(active, end, moved, home):
        phase = jnp.where(end > r1, 1.0, early)
        group = (phase * deep + ceil_tiles(moved) - 1.0) * deep + ceil_tiles(home) - 1.0
        return jnp.where(active, group, -1.0)

    tgt_rows, own_rows, back_rows = mine(tgt_live), mine(src_live), mine(tgt_live.T)
    fields = [
        jnp.where(moves_here, home_row, -1.0),
        tgt_rows,
        own_rows,
        jnp.zeros_like(early),
        jnp.where(moves_there, home_col, -1.0),
        src_rows,
        back_rows,
        tgt_end,
        group_of(moves_here, tgt_end, tgt_rows, own_rows),
        group_of(moves_there, src_end, src_rows, back_rows),
    ]
    for k, field in enumerate(fields):
        desc[k : k + 1, :] = field.astype(jnp.int32)
    rest[...] = jnp.broadcast_to(left, rest.shape)


def header_kernel(clusters, me_ref, code_ref, sizes_ref, tgt_ref, src_ref, out):
    n = code_ref.shape[0]
    me = me_ref[0]
    code = code_ref[...]
    row = lax.broadcasted_iota(jnp.int32, (n, n), 0)

    def mine(value):
        return jnp.sum(jnp.where(row == me, value, 0.0), axis=0, keepdims=True)

    picked = mine(((code // 2) & (clusters - 1)).astype(jnp.float32))
    local = mine((code // (2 * clusters)).astype(jnp.float32).T)
    cluster = lax.broadcasted_iota(jnp.int32, (clusters, n), 0).astype(jnp.float32)
    width = tgt_ref.shape[1]
    at = 0
    for wanted, ref in ((local, tgt_ref), (picked, src_ref)):
        chosen = jnp.where(cluster == wanted, 1.0, 0.0).astype(jnp.bfloat16)
        rows = lax.dot_general(
            chosen, ref[...], (((0,), (0,)), ((), ())), preferred_element_type=jnp.float32
        )
        out[:, at : at + width] = rows.astype(out.dtype)
        at += width
    high = jnp.floor(sizes_ref[...] * (1.0 / CHUNK))
    low = sizes_ref[...] - high * CHUNK
    for part in (high, low):
        out[:, at : at + TILE] = jnp.broadcast_to(part, (n, TILE)).astype(out.dtype)
        at += TILE


def make_header(me, code, sizes, tgt_potential, src_potential):
    n = code.shape[0]
    clusters, capacity = tgt_potential.shape
    return pl.pallas_call(
        functools.partial(header_kernel, clusters),
        out_shape=jax.ShapeDtypeStruct((n, 2 * capacity + 2 * TILE), tgt_potential.dtype),
        in_specs=[_smem(), _vmem(), _vmem(), _vmem(), _vmem()],
        out_specs=_vmem(),
        compiler_params=_params(),
        name="header",
    )(me, code, sizes, tgt_potential, src_potential)


def schedule(me, code, sizes, header, r1, r2, planes, depth):
    n, clusters = sizes.shape

    def ints(rows):
        return jax.ShapeDtypeStruct((rows, n), jnp.int32)

    return pl.pallas_call(
        functools.partial(sched_kernel, r1, r2, planes, clusters, depth),
        out_shape=(
            ints((r1 + 7) // 8 * 8),
            ints((r2 + 7) // 8 * 8),
            ints(2 * depth),
            ints(10),
            jax.ShapeDtypeStruct((1, n), jnp.float32),
        ),
        in_specs=[_smem(), _vmem(), _vmem(), _vmem()],
        out_specs=(_vmem(),) * 5,
        scratch_shapes=[pltpu.VMEM((planes, n, n), jnp.float32)],
        compiler_params=_params(),
        name="plan",
    )(me, code, sizes, header)


def whole_blocks(
    src_embed, tgt_embed, src_potential, header, src_sizes, tgt_sizes, mine, theirs
):
    devices = mine.shape[0]
    clusters, capacity, width = src_embed.shape
    scale = width ** (-0.5)
    blocks = jnp.take(tgt_embed, theirs // (2 * clusters), axis=0)
    blocks = lax.all_to_all(blocks, AXES, split_axis=0, concat_axis=0, tiled=True)
    row_ids = jnp.arange(capacity, dtype=jnp.int32)

    def one(peer, carry):
        src_grad, parts = carry
        c = (mine[peer] // 2) % clusters
        t = peer * clusters + mine[peer] // (2 * clusters)
        src_block, tgt_block = src_embed[c], blocks[peer]
        right = header[peer, : capacity // TILE].reshape(capacity)
        dots = jnp.dot(src_block, tgt_block.T, preferred_element_type=jnp.float32) * scale
        plan = jnp.exp(
            (src_potential[c].astype(jnp.float32)[:, None] + right[None, :] - (1.0 - dots))
            / epsilon
        )
        live = (row_ids[:, None] < src_sizes[c]) & (row_ids[None, :] < tgt_sizes[t])
        live = live & (mine[peer] % 2 > 0)
        weight = jnp.where(live, plan * (1.0 - (1.0 - dots) / epsilon), 0.0).astype(jnp.bfloat16)
        grad = -jnp.dot(weight, tgt_block, preferred_element_type=jnp.float32) * scale
        part = -jnp.dot(weight.T, src_block, preferred_element_type=jnp.float32) * scale
        return src_grad.at[c].add(grad), parts.at[peer].set(part.astype(jnp.bfloat16))

    src_grad, parts = lax.fori_loop(
        0, devices, one, (jnp.zeros(src_embed.shape, jnp.float32), jnp.zeros_like(blocks))
    )
    parts = lax.all_to_all(parts, AXES, split_axis=0, concat_axis=0, tiled=True)

    def back(peer, tgt_grad):
        return tgt_grad.at[theirs[peer] // (2 * clusters)].add(
            jnp.where(theirs[peer] % 2 > 0, parts[peer].astype(jnp.float32), 0.0)
        )

    tgt_grad = lax.fori_loop(0, devices, back, jnp.zeros(tgt_embed.shape, jnp.float32))
    return src_grad, tgt_grad


def shards(
    src_embed, tgt_embed, src_potential, tgt_potential, src_sizes, tgt_sizes, pair_counts, pairs
):
    devices = lax.axis_size(AXES)
    me = lax.axis_index(AXES)
    clusters, capacity, width = src_embed.shape
    fanout = pairs.shape[1]
    chunks = capacity // CHUNK
    blocks = capacity // TILE
    peer_ids = jnp.arange(devices, dtype=jnp.int32)
    cluster_ids = jnp.arange(clusters, dtype=jnp.int32)
    fan_ids = jnp.arange(fanout, dtype=jnp.int32)
    listed = pairs.T.reshape(fanout, devices, clusters)
    counts = pair_counts.reshape(devices, clusters)
    code = (fan_ids[:, None, None] < counts[None]).astype(jnp.int32) * (
        1 + 2 * cluster_ids[None, None, :] + 2 * clusters * (listed % clusters)
    )
    matrix = jnp.sum(
        jnp.where((listed // clusters)[..., None] == peer_ids, code[..., None], 0), axis=(0, 2)
    )
    place = me.reshape(1).astype(jnp.int32)
    own_sizes = jnp.pad(src_sizes, (0, TILE - clusters)).reshape(1, TILE).astype(jnp.float32)
    header = make_header(place, matrix, own_sizes, tgt_potential, src_potential)
    header = header.reshape(devices, 2 * blocks + 2, TILE)
    header = lax.all_to_all(header, AXES, split_axis=0, concat_axis=0, tiled=True)
    header = header.astype(jnp.float32)
    first, second, third, desc, rest = schedule(
        place,
        matrix,
        tgt_sizes.reshape(devices, clusters).astype(jnp.float32),
        header,
        NEAR,
        FAR,
        PLANES,
        chunks,
    )
    homes = 2 * clusters
    pots_home = jnp.concatenate([tgt_potential, src_potential], axis=0).reshape(
        homes, blocks, TILE
    )
    pots_home = (
        jnp.pad(pots_home, ((0, 0), (0, 8 - blocks), (0, 0)))
        .astype(jnp.float32)
        .reshape(homes * 8, TILE)
    )

    def packed(_):
        tgt_rows = tgt_embed.reshape(clusters * capacity, width)
        src_rows = src_embed.reshape(clusters * capacity, width)
        near = exchange(pack(first, tgt_rows, src_rows, NEAR), devices)
        far = exchange(pass_on(second, tgt_rows, src_rows, near, FAR), devices)

        def pairs_of(phase, *extra):
            return compute(
                phase,
                desc,
                third,
                header.reshape(devices * 8, TILE),
                pots_home,
                near,
                tgt_rows,
                src_rows,
                capacity,
                devices * FAR * CHUNK,
                extra,
            )

        ret, acc_first = pairs_of(0)
        ret, ret_far, acc_second = pairs_of(1, far, ret)
        back_far = exchange(ret_far, devices)
        ret, acc_third = pairs_of(2, ret)
        ret = pass_back(second, back_far, ret, homes * chunks, FAR)
        back_near = exchange(ret, devices)
        (acc,) = fold(second, back_far, (acc_first, acc_second, acc_third), FAR, 1)
        tgt_grad, src_grad = fold(first, back_near, (acc,), NEAR, 2)
        return src_grad.reshape(src_embed.shape), tgt_grad.reshape(tgt_embed.shape)

    def unpacked(_):
        mine = lax.dynamic_index_in_dim(matrix, me, 0, keepdims=False)
        theirs = lax.dynamic_index_in_dim(matrix, me, 1, keepdims=False)
        return whole_blocks(
            src_embed, tgt_embed, src_potential, header, src_sizes, tgt_sizes, mine, theirs
        )

    return lax.cond(rest[0, 0] == 0.0, packed, unpacked, 0)


def solution(mesh):
    placed = (
        P(AXES, None, None),
        P(AXES, None, None),
        P(AXES, None),
        P(AXES, None),
        P(AXES),
        P(),
        P(),
        P(),
    )
    return jax.shard_map(
        shards,
        mesh=mesh,
        in_specs=placed,
        out_specs=(P(AXES, None, None), P(AXES, None, None)),
        check_vma=False,
    )
```

```python
import functools
import math

import jax
import jax.numpy as jnp
from jax import lax
from jax.experimental import pallas as pl
from jax.experimental.pallas import tpu as pltpu
from jax.sharding import PartitionSpec as P

AXES = ("gx", "gy")
CHUNK = 16
TILE = 128
VMEM_BYTES = 60 * 1024 * 1024
DEAD = -1e30
NEAR = 8
FAR = 4
PLANES = 128
ROUNDS = 4
STEP = 0.3
UNROLL = 1
epsilon = 0.5


def _params():
    return pltpu.CompilerParams(vmem_limit_bytes=VMEM_BYTES)


def _any():
    return pl.BlockSpec(memory_space=pl.ANY)


def _vmem():
    return pl.BlockSpec(memory_space=pltpu.VMEM)


def _smem():
    return pl.BlockSpec(memory_space=pltpu.SMEM)


def _rows(chunk):
    return pl.ds(pl.multiple_of(chunk * CHUNK, CHUNK), CHUNK)


def slots(one, step, carry):
    for u in range(UNROLL):
        carry = one(step * UNROLL + u, carry)
    return carry


def pack_kernel(slot_chunks, table, tgt_any, src_any, out, home, sems):
    half = tgt_any.shape[0]
    first = pltpu.make_async_copy(tgt_any, home.at[pl.ds(0, half)], sems.at[0])
    second = pltpu.make_async_copy(src_any, home.at[pl.ds(half, half)], sems.at[1])
    first.start()
    second.start()
    home[pl.ds(2 * half, CHUNK), :] = jnp.zeros((CHUNK, home.shape[1]), home.dtype)
    first.wait()
    second.wait()

    def slot(peer, carry):
        rows = [home[_rows(table[p, peer]), :] for p in range(slot_chunks)]
        for p in range(slot_chunks):
            out[_rows(peer * slot_chunks + p), :] = rows[p]
        return carry

    lax.fori_loop(0, table.shape[1] // UNROLL, functools.partial(slots, slot), 0)


def pack(table, tgt_rows, src_rows, slot_chunks):
    peers = table.shape[1]
    width = tgt_rows.shape[1]
    total = peers * slot_chunks * CHUNK
    return pl.pallas_call(
        functools.partial(pack_kernel, slot_chunks),
        out_shape=jax.ShapeDtypeStruct((total, width), tgt_rows.dtype),
        in_specs=[_smem(), _any(), _any()],
        out_specs=_vmem(),
        scratch_shapes=[
            pltpu.VMEM((2 * tgt_rows.shape[0] + CHUNK, width), tgt_rows.dtype),
            pltpu.SemaphoreType.DMA((2,)),
        ],
        compiler_params=_params(),
        name="pack",
    )(table, tgt_rows, src_rows)


def side_rows(potential, live, first):
    shape = (CHUNK, potential.shape[1])
    row = lax.broadcasted_iota(jnp.int32, shape, 0)
    lane = lax.broadcasted_iota(jnp.int32, shape, 1)
    dead = jnp.where(lane < live, 0.0, DEAD)
    pot = jnp.broadcast_to(potential, shape)
    own = 0 if first else 1
    other = 1 - own
    mine = 2 if first else 3
    rows = jnp.where(row == own, pot, jnp.where(row == mine, dead, 1.0))
    rows = jnp.where(row < 4, rows, 0.0)
    return rows.astype(jnp.bfloat16)


def compute_kernel(capacity, scale, phase, far_rows, refs_in, *refs):
    desc, table, pots_in, pots_home, near_any, tgt_any, src_any = refs[:7]
    extra = refs[7:refs_in]
    if phase == 1:
        far_any, ret_before = extra
        ret_near, ret_far, acc = refs[refs_in : refs_in + 3]
    else:
        ret_near, acc = refs[refs_in : refs_in + 2]
    recv, ret, home, items, fill, sems = refs[-6:]
    width = home.shape[1]
    half = tgt_any.shape[0]
    near = near_any.shape[0]
    total = near + far_rows
    copies = [
        pltpu.make_async_copy(tgt_any, home.at[pl.ds(0, half)], sems.at[0]),
        pltpu.make_async_copy(src_any, home.at[pl.ds(half, half)], sems.at[1]),
        pltpu.make_async_copy(near_any, recv.at[pl.ds(0, near)], sems.at[2]),
    ]
    if phase == 1:
        copies += [
            pltpu.make_async_copy(far_any, recv.at[pl.ds(near, far_rows)], sems.at[3]),
            pltpu.make_async_copy(ret_before, ret.at[pl.ds(0, near)], sems.at[4]),
        ]
    if phase == 2:
        (ret_before,) = extra
        copies += [pltpu.make_async_copy(ret_before, ret.at[pl.ds(0, near)], sems.at[4])]
    for copy in copies:
        copy.start()
    recv[pl.ds(total, CHUNK), :] = jnp.zeros((CHUNK, width), recv.dtype)


    def clear(i, carry):
        at = pl.multiple_of(i * capacity, capacity)
        acc[pl.ds(at, capacity), :] = jnp.zeros((capacity, width), jnp.float32)
        return carry

    lax.fori_loop(0, acc.shape[0] // capacity, clear, 0)
    log2e = math.log2(math.e)
    to_exp = log2e / epsilon

    each = TILE // CHUNK

    def pair_of(group, at, size):
        item = items[group, jnp.minimum(at, size - 1)]
        real = at < size
        peer, kind = item // 2, item % 2
        field = kind * 4
        return (
            peer,
            kind,
            desc[field, peer],
            jnp.where(real, desc[field + 1, peer], 0),
            jnp.where(real, desc[field + 2, peer], 0),
            desc[field + 3, peer],
        )

    def some(blocks, count, pairs):
        rights, sides, lefts = [], [], []
        for peer, kind, home_id, live_moved, live_home, start in pairs:
            rights.append(
                jnp.concatenate(
                    [recv[_rows(table[start + j, peer]), :] for j in range(blocks * each)], axis=0
                )
            )
            right_pots = pots_in[pl.ds(pl.multiple_of(peer * 8, 8), 8), :]
            deep = capacity // TILE
            right_pots = jnp.where(kind == 0, right_pots[0:deep, :], right_pots[deep : 2 * deep, :])
            left_pots = pots_home[pl.ds(pl.multiple_of(home_id * 8, 8), 8), :]
            right_side = jnp.concatenate(
                [
                    side_rows(right_pots[b : b + 1, :], live_moved - b * TILE, False)
                    for b in range(blocks)
                ],
                axis=1,
            )
            left_side = [
                side_rows(left_pots[i : i + 1, :], live_home - i * TILE, True)
                for i in range(count)
            ]
            sides.append((left_side, right_side))
            at = pl.multiple_of(home_id * capacity, TILE)
            lefts.append([home[pl.ds(at + i * TILE, TILE), :] for i in range(count)])
        work = [(k, i) for i in range(count) for k in range(len(pairs))]
        sums = [
            lax.dot_general(
                sides[k][0][i],
                sides[k][1],
                (((0,), (0,)), ((), ())),
                preferred_element_type=jnp.float32,
            )
            for k, i in work
        ]
        dots = [
            lax.dot_general(
                lefts[k][i], rights[k], (((1,), (1,)), ((), ())), preferred_element_type=jnp.float32
            )
            for k, i in work
        ]
        weights = []
        for dot, total_pot in zip(dots, sums):
            plan = jnp.exp2(dot * (scale * to_exp) + (total_pot * to_exp - to_exp))
            weights.append(
                (plan * (dot * (scale / epsilon) + (1.0 - 1.0 / epsilon))).astype(jnp.bfloat16)
            )
        pieces = [
            lax.dot_general(
                weight, lefts[k][i], (((0,), (0,)), ((), ())), preferred_element_type=jnp.float32
            )
            for weight, (k, i) in zip(weights, work)
        ]
        grads = [
            jnp.dot(weight, rights[k], preferred_element_type=jnp.float32)
            for weight, (k, i) in zip(weights, work)
        ]
        for k, pair in enumerate(pairs):
            at = pl.multiple_of(pair[2] * capacity, TILE)
            for i in range(count):
                acc[pl.ds(at + i * TILE, TILE), :] += (-scale) * grads[work.index((k, i))]
            piece = functools.reduce(
                jnp.add, [pieces[work.index((k, i))] for i in range(count)]
            ) * (-scale)
            for j in range(blocks * each):
                into = table[pair[5] + j, pair[0]]
                into = jnp.where(j * CHUNK < pair[3], into, total // CHUNK)
                ret[_rows(into), :] = piece[j * CHUNK : (j + 1) * CHUNK, :].astype(ret.dtype)

    deep = capacity // TILE
    for c in range(deep * deep):
        fill[c] = 0

    fill[deep * deep] = 0

    def sort(step, carry):
        for u in range(4):
            peer = step * 4 + u
            for kind in range(2):
                group = desc[8 + kind, peer] - phase * deep * deep
                ours = (group >= 0) & (group < deep * deep)
                group = jnp.where(ours, group, deep * deep)
                at = fill[group]
                items[group, at] = peer * 2 + kind
                fill[group] = at + 1
        return carry

    lax.fori_loop(0, desc.shape[1] // 4, sort, 0)
    for copy in copies:
        copy.wait()
    for b in range(1, deep + 1):
        for c in range(1, deep + 1):
            group = (b - 1) * deep + c - 1
            size = fill[group]

            def two(k, carry, b=b, c=c, group=group, size=size):
                some(b, c, [pair_of(group, 2 * k, size), pair_of(group, 2 * k + 1, size)])
                return carry

            lax.fori_loop(0, (size + 1) // 2, two, 0)

    back = [pltpu.make_async_copy(ret.at[pl.ds(0, near)], ret_near, sems.at[7])]
    if phase == 1:
        back.append(
            pltpu.make_async_copy(ret.at[pl.ds(near, far_rows)], ret_far, sems.at[8])
        )
    for copy in back:
        copy.start()
    for copy in back:
        copy.wait()


def compute(phase, desc, table, pots_in, pots_home, near, tgt_rows, src_rows, capacity, far_rows, extra):
    width = tgt_rows.shape[1]
    scale = width ** (-0.5)
    homes = 2 * tgt_rows.shape[0]
    shapes = [jax.ShapeDtypeStruct(near.shape, near.dtype)]
    if phase == 1:
        shapes.append(jax.ShapeDtypeStruct((far_rows, width), near.dtype))
    shapes.append(jax.ShapeDtypeStruct((homes, width), jnp.float32))
    rows = near.shape[0] + far_rows + CHUNK
    groups = (capacity // TILE) ** 2 + 1
    scratch = [
        pltpu.VMEM((rows, width), near.dtype),
        pltpu.VMEM((rows, width), near.dtype),
        pltpu.VMEM((homes, width), tgt_rows.dtype),
        pltpu.SMEM((groups, 2 * desc.shape[1]), jnp.int32),
        pltpu.SMEM((groups,), jnp.int32),
        pltpu.SemaphoreType.DMA((9,)),
    ]
    work = 4 * desc.shape[1] * capacity * capacity
    return pl.pallas_call(
        functools.partial(compute_kernel, capacity, scale, phase, far_rows, 7 + len(extra)),
        out_shape=tuple(shapes),
        in_specs=[_smem(), _smem(), _vmem(), _vmem()] + [_any()] * (3 + len(extra)),
        out_specs=tuple([_any()] * (len(shapes) - 1) + [_vmem()]),
        scratch_shapes=scratch,
        compiler_params=_params(),
        cost_estimate=pl.CostEstimate(
            flops=work * width, bytes_accessed=8 * homes * width, transcendentals=work // 8
        ),
        name="pairs%d" % phase,
    )(desc, table, pots_in, pots_home, near, tgt_rows, src_rows, *extra)


def pass_on_kernel(slot_chunks, table, tgt_any, src_any, got_any, out, pool, sems):
    half = tgt_any.shape[0]
    homes = 2 * half + CHUNK
    copies = [
        pltpu.make_async_copy(tgt_any, pool.at[pl.ds(0, half)], sems.at[0]),
        pltpu.make_async_copy(src_any, pool.at[pl.ds(half, half)], sems.at[1]),
        pltpu.make_async_copy(got_any, pool.at[pl.ds(homes, got_any.shape[0])], sems.at[2]),
    ]
    for copy in copies:
        copy.start()
    pool[pl.ds(2 * half, CHUNK), :] = jnp.zeros((CHUNK, pool.shape[1]), pool.dtype)
    for copy in copies:
        copy.wait()

    def slot(peer, carry):
        rows = [pool[_rows(table[p, peer]), :] for p in range(slot_chunks)]
        for p in range(slot_chunks):
            out[_rows(peer * slot_chunks + p), :] = rows[p]
        return carry

    lax.fori_loop(0, table.shape[1] // UNROLL, functools.partial(slots, slot), 0)


def pass_on(table, tgt_rows, src_rows, got, slot_chunks):
    peers = table.shape[1]
    width = tgt_rows.shape[1]
    return pl.pallas_call(
        functools.partial(pass_on_kernel, slot_chunks),
        out_shape=jax.ShapeDtypeStruct((peers * slot_chunks * CHUNK, width), tgt_rows.dtype),
        in_specs=[_smem(), _any(), _any(), _any()],
        out_specs=_vmem(),
        scratch_shapes=[
            pltpu.VMEM((2 * tgt_rows.shape[0] + CHUNK + got.shape[0], width), tgt_rows.dtype),
            pltpu.SemaphoreType.DMA((3,)),
        ],
        compiler_params=_params(),
        name="pass_on",
    )(table, tgt_rows, src_rows, got)


def pass_back_kernel(slot_chunks, homes, table, got, ret_any, out_any, out, sems):
    rows = ret_any.shape[0]
    first = pltpu.make_async_copy(ret_any, out.at[pl.ds(0, rows)], sems.at[0])
    first.start()
    first.wait()

    def slot(peer, carry):
        ats = [table[p, peer] - (homes + 1) for p in range(slot_chunks)]
        parts = [got[_rows(peer * slot_chunks + p), :] for p in range(slot_chunks)]
        for at, part in zip(ats, parts):
            out[_rows(jnp.where(at < 0, rows // CHUNK, at)), :] = part
        return carry

    lax.fori_loop(0, table.shape[1] // UNROLL, functools.partial(slots, slot), 0)
    second = pltpu.make_async_copy(out.at[pl.ds(0, rows)], out_any, sems.at[1])
    second.start()
    second.wait()


def pass_back(table, got, ret, homes, slot_chunks):
    rows, width = ret.shape
    return pl.pallas_call(
        functools.partial(pass_back_kernel, slot_chunks, homes),
        out_shape=jax.ShapeDtypeStruct(ret.shape, ret.dtype),
        in_specs=[_smem(), _vmem(), _any()],
        out_specs=_any(),
        scratch_shapes=[
            pltpu.VMEM((rows + CHUNK, width), ret.dtype),
            pltpu.SemaphoreType.DMA((2,)),
        ],
        compiler_params=_params(),
        name="pass_back",
    )(table, got, ret)


def fold_kernel(slot_chunks, bases, table, got, *refs):
    accs, outs, (even, odd, base, sems) = refs[:bases], refs[bases:-4], refs[-4:]
    homes = accs[0].shape[0]
    width = accs[0].shape[1]
    first = pltpu.make_async_copy(accs[0], base, sems.at[0])
    first.start()
    for k in range(1, bases):
        sums = (even, odd)[k - 1].at[pl.ds(0, homes)]
        pltpu.make_async_copy(accs[k], sums, sems.at[9 + k]).start()
    for sums in (even, odd):
        sums[pl.ds(homes, CHUNK), :] = jnp.zeros((CHUNK, width), jnp.float32)

    def clear(i, carry):
        at = pl.ds(pl.multiple_of(i * 8 * CHUNK, 8 * CHUNK), 8 * CHUNK)
        even[at, :] = jnp.zeros((8 * CHUNK, even.shape[1]), jnp.float32)
        odd[at, :] = jnp.zeros((8 * CHUNK, odd.shape[1]), jnp.float32)
        return carry

    if bases == 1:
        lax.fori_loop(0, homes // (8 * CHUNK), clear, 0)
    for k in range(1, bases):
        sums = (even, odd)[k - 1].at[pl.ds(0, homes)]
        pltpu.make_async_copy(accs[k], sums, sems.at[9 + k]).wait()

    def slot(peer, carry):
        ats = [
            _rows(jnp.minimum(table[p, peer], homes // CHUNK)) for p in range(slot_chunks)
        ]
        parts = [
            got[_rows(peer * slot_chunks + p), :].astype(jnp.float32) for p in range(slot_chunks)
        ]
        for p in range(0, slot_chunks, 2):
            one = even[ats[p], :] + parts[p]
            two = odd[ats[p + 1], :] + parts[p + 1]
            even[ats[p], :] = one
            odd[ats[p + 1], :] = two
        return carry

    lax.fori_loop(0, table.shape[1] // UNROLL, functools.partial(slots, slot), 0)
    first.wait()
    pieces = 8
    share = homes // pieces
    per_out = pieces // len(outs)
    copies = []
    for k in range(pieces):

        def join(i, carry, k=k):
            at = pl.ds(pl.multiple_of(k * share + i * 8 * CHUNK, 8 * CHUNK), 8 * CHUNK)
            base[at, :] = base[at, :] + (even[at, :] + odd[at, :])
            return carry

        lax.fori_loop(0, share // (8 * CHUNK), join, 0)
        out = outs[k // per_out]
        into = out.at[pl.ds((k % per_out) * share, share)]
        copies.append(
            pltpu.make_async_copy(base.at[pl.ds(k * share, share)], into, sems.at[k + 1])
        )
        copies[-1].start()
    for copy in copies:
        copy.wait()


def fold(table, got, accs, slot_chunks, parts):
    homes, width = accs[0].shape
    result = jax.ShapeDtypeStruct((homes // parts, width), jnp.float32)
    return pl.pallas_call(
        functools.partial(fold_kernel, slot_chunks, len(accs)),
        out_shape=(result,) * parts,
        in_specs=[_smem(), _vmem()] + [_any()] * len(accs),
        out_specs=(_any(),) * parts,
        scratch_shapes=[
            pltpu.VMEM((homes + CHUNK, width), jnp.float32),
            pltpu.VMEM((homes + CHUNK, width), jnp.float32),
            pltpu.VMEM((homes, width), jnp.float32),
            pltpu.SemaphoreType.DMA((12,)),
        ],
        compiler_params=_params(),
        cost_estimate=pl.CostEstimate(
            flops=homes * width, bytes_accessed=8 * homes * width, transcendentals=0
        ),
        name="fold%d" % parts,
    )(table, got, *accs)


def exchange(blocks, devices):
    shaped = blocks.reshape(devices, -1, blocks.shape[-1])
    got = lax.all_to_all(shaped, AXES, split_axis=0, concat_axis=0, tiled=True)
    return got.reshape(blocks.shape)


def sched_kernel(
    r1,
    r2,
    planes,
    clusters,
    depth,
    me_ref,
    code_ref,
    sizes_ref,
    header_ref,
    t1,
    t2,
    t3,
    desc,
    rest,
    moves,
):
    n = code_ref.shape[0]
    me = me_ref[0]
    last = n - 1
    chunks = clusters * depth
    row = lax.broadcasted_iota(jnp.int32, (n, n), 0)
    col = lax.broadcasted_iota(jnp.int32, (n, n), 1)
    direct = float(r1 + r2)
    code = code_ref[...]
    used = (code & 1).astype(jnp.float32)
    picked = (code // 2) & (clusters - 1)
    local = code // (2 * clusters)
    filler = jnp.zeros((n, n - clusters), jnp.float32)
    by_tgt = jnp.concatenate([sizes_ref[...], filler], axis=1).T
    every = header_ref[:, 6, :] * float(CHUNK) + header_ref[:, 7, :]
    by_src = every.T
    tgt_live = jnp.zeros((n, n), jnp.float32)
    src_live = jnp.zeros((n, n), jnp.float32)
    picked_t = picked.astype(jnp.float32).T
    for c in range(clusters):
        tgt_live = jnp.where(local == c, by_tgt[c : c + 1, :], tgt_live)
        src_live = jnp.where(picked_t == float(c), by_src[c : c + 1, :], src_live)
    src_live = src_live.T

    def ceil_chunks(rows):
        return jnp.floor((rows + (CHUNK - 1.0)) * (1.0 / CHUNK))

    tc = ceil_chunks(tgt_live) * used
    sc = ceil_chunks(src_live) * used
    tct, sct = tc.T, sc.T

    def cost(count, price):
        return price * (
            count + jnp.maximum(count - r1, 0.0) + jnp.maximum(count - direct, 0.0)
        )

    def choose(price):
        back = price.T
        src_tgt = cost(sc + tct, price)
        src_src = cost(sc, price) + cost(sct, back)
        tgt_tgt = cost(tct, price) + cost(tc, back)
        tgt_src = cost(tc + sct, back)
        best = jnp.minimum(jnp.minimum(src_tgt, src_src), jnp.minimum(tgt_tgt, tgt_src))
        src_first = (src_tgt == best) | (src_src == best)
        first = jnp.where(src_first, 0.0, 1.0)
        second = jnp.where(
            src_tgt == best,
            1.0,
            jnp.where(src_src == best, 0.0, jnp.where(tgt_tgt == best, 1.0, 0.0)),
        )
        tgt_moves = jnp.where(row < col, first, second.T)
        tm = tc * tgt_moves
        return tgt_moves, tm, tm.T + sc * (1.0 - tgt_moves)

    def update(_, price):
        load = choose(price)[2]
        sent = jnp.sum(load, axis=1, keepdims=True)
        got = jnp.sum(load, axis=0, keepdims=True)
        mean = jnp.maximum(jnp.sum(got, axis=1, keepdims=True) / n, 1.0)
        return price + STEP * (sent / mean - 1.0) + STEP * (got / mean - 1.0)

    prices = lax.fori_loop(0, ROUNDS, update, jnp.ones_like(tc))
    tgt_moves, tm, load = choose(prices)
    tmt = tm.T
    d1 = jnp.minimum(load, float(r1))
    d2 = jnp.minimum(load - d1, float(r2))
    d12 = d1 + d2
    slack1 = r1 - d1
    slack2 = r2 - d2
    bit = 1
    while bit < n:
        slack1 = jnp.where((row & bit) > 0, pltpu.roll(slack1, n - bit, 1), slack1)
        slack2 = jnp.where((col & bit) > 0, pltpu.roll(slack2, n - bit, 0), slack2)
        bit *= 2
    excess = load - d12
    group = 8

    def more(state):
        return (state[0] < planes) & (state[1] > 0.0)

    def step(state):
        at, _, excess, slack1, slack2 = state
        for k in range(group):
            x = jnp.minimum(jnp.minimum(excess, slack1), slack2)
            moves[at + k] = x
            excess = excess - x
            slack1 = pltpu.roll(slack1 - x, n - 1, 1)
            slack2 = pltpu.roll(slack2 - x, n - 1, 0)
        return at + group, jnp.sum(excess), excess, slack1, slack2

    count, left, _, _, _ = lax.while_loop(
        more, step, (jnp.int32(0), jnp.sum(excess), excess, slack1, slack2)
    )

    def mine(value):
        return jnp.sum(jnp.where(row == me, value, 0.0), axis=0, keepdims=True)

    d1r, d2r, d12r = mine(d1), mine(d2), mine(d12)
    d1c, d2c, d12c = mine(d1.T), mine(d2.T), mine(d12.T)
    tn = mine(tmt)
    local_t = local.astype(jnp.float32).T
    home_row = clusters + mine(picked.astype(jnp.float32))
    home_col = mine(local_t)
    tb = home_col * depth
    sb = home_row * depth - tn
    negate = jnp.where(row == ((n - col) & last), 1.0, 0.0).astype(jnp.bfloat16)
    p1n = jnp.dot(
        jnp.broadcast_to(d1c, (16, n)).astype(jnp.bfloat16),
        negate,
        preferred_element_type=jnp.float32,
    )[0:1, :]
    homes = 2.0 * chunks
    first_n = float(n * r1)
    total = float(n * (r1 + r2))
    lane = lax.broadcasted_iota(jnp.int32, (1, n), 1)
    lane_f = lane.astype(jnp.float32)

    def iota_f(rows):
        return lax.broadcasted_iota(jnp.int32, (rows, n), 0).astype(jnp.float32)

    p1, p2, p3 = iota_f(t1.shape[0]), iota_f(t2.shape[0]), iota_f(t3.shape[0])

    def home_of(q, tn, tb, sb):
        return jnp.where(q < tn, tb + q, sb + q)

    v1 = jnp.where(p1 < d1r, home_of(p1, tn, tb, sb), homes)
    v2 = jnp.where(p2 < d2r, home_of(p2 + d1r, tn, tb, sb), homes)
    v3 = jnp.where(
        p3 < d1c,
        lane_f * r1 + p3,
        jnp.where(p3 < d12c, first_n + lane_f * r2 + p3 - d1c, total),
    )
    pick = jnp.where(
        lax.broadcasted_iota(jnp.int32, (16, n), 1) == me, 1.0, 0.0
    ).astype(jnp.bfloat16)

    spread = (row + col - me) & last

    def extract(r, state):
        v1, v2, v3, qa, p1a, qb, p2b, p1n, p2c = state
        x = moves[r]
        xa = moves[r, pl.ds(me, 1), :]
        xb = lax.dot_general(
            pick, x.astype(jnp.bfloat16), (((1,), (1,)), ((), ())),
            preferred_element_type=jnp.float32,
        )[0:1, :]
        xc = jnp.sum(jnp.where(spread == ((n - r) & last), x, 0.0), axis=0, keepdims=True)
        ahead = (me + r) & last
        back = (n - ahead) & last
        stacked = jnp.concatenate([xa, qa, tn, tb, sb, xa, xa, xa], axis=0)
        turned = pltpu.roll(stacked, ahead, 1)
        xa_c, qa_c = turned[0:1, :], turned[1:2, :]
        at = p1 - p1a
        v1 = jnp.where(
            (at >= 0.0) & (at < xa_c),
            home_of(qa_c + at, turned[2:3, :], turned[3:4, :], turned[4:5, :]),
            v1,
        )
        p1a = p1a + xa_c
        qa = qa + xa
        forth = (me - r) & last
        p1b = pltpu.roll(jnp.broadcast_to(p1n, (8, n)), forth, 1)[0:1, :]
        at = p2 - p2c
        origin = ((me - lane - r) & last).astype(jnp.float32)
        v2 = jnp.where((at >= 0.0) & (at < xc), homes + 1.0 + origin * r1 + p1b + at, v2)
        p2c = p2c + xc
        p1n = p1n + pltpu.roll(jnp.broadcast_to(xc, (8, n)), (n - forth) & last, 1)[0:1, :]
        p2a = pltpu.roll(jnp.broadcast_to(p2b, (8, n)), back, 1)[0:1, :]
        via = ((lane + me + r) & last).astype(jnp.float32)
        at = p3 - qb
        v3 = jnp.where((at >= 0.0) & (at < xb), first_n + via * r2 + p2a + at, v3)
        p2b = p2b + pltpu.roll(jnp.broadcast_to(xb, (8, n)), ahead, 1)[0:1, :]
        qb = qb + xb
        return v1, v2, v3, qa, p1a, qb, p2b, p1n, p2c

    def several(k, state):
        for u in range(group // 2):
            state = extract(k * (group // 2) + u, state)
        return state

    v1, v2, v3 = lax.fori_loop(
        0, count // (group // 2), several, (v1, v2, v3, d12r, d1r, d12c, d2c, p1n, d2r)
    )[:3]
    t1[...] = v1.astype(jnp.int32)
    t2[...] = v2.astype(jnp.int32)
    t3[...] = v3.astype(jnp.int32)
    moves_here = mine(used * tgt_moves) > 0.0
    moves_there = mine((used * (1.0 - tgt_moves)).T) > 0.0
    tgt_end = mine(tm)
    src_rows = mine(src_live.T)
    src_end = tgt_end + ceil_chunks(src_rows)
    early = ((lane & 1) * 2).astype(jnp.float32)
    deep = depth * CHUNK // TILE

    def ceil_tiles(rows):
        return jnp.floor((rows + (TILE - 1.0)) * (1.0 / TILE))

    def group_of(active, end, moved, home):
        phase = jnp.where(end > r1, 1.0, early)
        group = (phase * deep + ceil_tiles(moved) - 1.0) * deep + ceil_tiles(home) - 1.0
        return jnp.where(active, group, -1.0)

    tgt_rows, own_rows, back_rows = mine(tgt_live), mine(src_live), mine(tgt_live.T)
    fields = [
        jnp.where(moves_here, home_row, -1.0),
        tgt_rows,
        own_rows,
        jnp.zeros_like(early),
        jnp.where(moves_there, home_col, -1.0),
        src_rows,
        back_rows,
        tgt_end,
        group_of(moves_here, tgt_end, tgt_rows, own_rows),
        group_of(moves_there, src_end, src_rows, back_rows),
    ]
    for k, field in enumerate(fields):
        desc[k : k + 1, :] = field.astype(jnp.int32)
    rest[...] = jnp.broadcast_to(left, rest.shape)


def header_kernel(me_ref, listed_ref, counts_ref, sizes_ref, tgt_ref, src_ref, out, matrix):
    fanout, n, clusters = listed_ref.shape
    me = me_ref[0]
    row = lax.broadcasted_iota(jnp.int32, (n, n), 0)
    row_f = row.astype(jnp.float32)
    filler = jnp.zeros((n, n - clusters), jnp.float32)

    def turn(values):
        return jnp.concatenate([values.astype(jnp.float32), filler], axis=1).T

    counts = turn(counts_ref[...])
    found = jnp.zeros((n, n), jnp.float32)
    for k in range(fanout):
        listed = turn(listed_ref[k])
        owner = jnp.floor(listed * (1.0 / clusters))
        entry = 1.0 + 2.0 * row_f + (2.0 * clusters) * (listed - owner * clusters)
        entry = jnp.where(counts > float(k), entry, 0.0)
        for c in range(clusters):
            found = found + jnp.where(row_f == owner[c : c + 1, :], entry[c : c + 1, :], 0.0)
    code = found.T.astype(jnp.int32)
    matrix[...] = code

    def mine(value):
        return jnp.sum(jnp.where(row == me, value, 0.0), axis=0, keepdims=True)

    picked = mine(((code // 2) & (clusters - 1)).astype(jnp.float32))
    local = mine((code // (2 * clusters)).astype(jnp.float32).T)
    cluster = lax.broadcasted_iota(jnp.int32, (clusters, n), 0).astype(jnp.float32)
    width = tgt_ref.shape[1]
    at = 0
    for wanted, ref in ((local, tgt_ref), (picked, src_ref)):
        chosen = jnp.where(cluster == wanted, 1.0, 0.0).astype(jnp.bfloat16)
        rows = lax.dot_general(
            chosen, ref[...], (((0,), (0,)), ((), ())), preferred_element_type=jnp.float32
        )
        out[:, at : at + width] = rows.astype(out.dtype)
        at += width
    high = jnp.floor(sizes_ref[...] * (1.0 / CHUNK))
    low = sizes_ref[...] - high * CHUNK
    for part in (high, low):
        out[:, at : at + TILE] = jnp.broadcast_to(part, (n, TILE)).astype(out.dtype)
        at += TILE


def make_header(me, listed, counts, sizes, tgt_potential, src_potential):
    n = listed.shape[1]
    capacity = tgt_potential.shape[1]
    return pl.pallas_call(
        header_kernel,
        out_shape=(
            jax.ShapeDtypeStruct((n, 2 * capacity + 2 * TILE), tgt_potential.dtype),
            jax.ShapeDtypeStruct((n, n), jnp.int32),
        ),
        in_specs=[_smem(), _vmem(), _vmem(), _vmem(), _vmem(), _vmem()],
        out_specs=(_vmem(), _vmem()),
        compiler_params=_params(),
        name="header",
    )(me, listed, counts, sizes, tgt_potential, src_potential)


def schedule(me, code, sizes, header, r1, r2, planes, depth):
    n, clusters = sizes.shape

    def ints(rows):
        return jax.ShapeDtypeStruct((rows, n), jnp.int32)

    return pl.pallas_call(
        functools.partial(sched_kernel, r1, r2, planes, clusters, depth),
        out_shape=(
            ints((r1 + 7) // 8 * 8),
            ints((r2 + 7) // 8 * 8),
            ints(2 * depth),
            ints(10),
            jax.ShapeDtypeStruct((1, n), jnp.float32),
        ),
        in_specs=[_smem(), _vmem(), _vmem(), _vmem()],
        out_specs=(_vmem(),) * 5,
        scratch_shapes=[pltpu.VMEM((planes, n, n), jnp.float32)],
        compiler_params=_params(),
        name="plan",
    )(me, code, sizes, header)


def whole_blocks(
    src_embed, tgt_embed, src_potential, header, src_sizes, tgt_sizes, mine, theirs
):
    devices = mine.shape[0]
    clusters, capacity, width = src_embed.shape
    scale = width ** (-0.5)
    blocks = jnp.take(tgt_embed, theirs // (2 * clusters), axis=0)
    blocks = lax.all_to_all(blocks, AXES, split_axis=0, concat_axis=0, tiled=True)
    row_ids = jnp.arange(capacity, dtype=jnp.int32)

    def one(peer, carry):
        src_grad, parts = carry
        c = (mine[peer] // 2) % clusters
        t = peer * clusters + mine[peer] // (2 * clusters)
        src_block, tgt_block = src_embed[c], blocks[peer]
        right = header[peer, : capacity // TILE].reshape(capacity)
        dots = jnp.dot(src_block, tgt_block.T, preferred_element_type=jnp.float32) * scale
        plan = jnp.exp(
            (src_potential[c].astype(jnp.float32)[:, None] + right[None, :] - (1.0 - dots))
            / epsilon
        )
        live = (row_ids[:, None] < src_sizes[c]) & (row_ids[None, :] < tgt_sizes[t])
        live = live & (mine[peer] % 2 > 0)
        weight = jnp.where(live, plan * (1.0 - (1.0 - dots) / epsilon), 0.0).astype(jnp.bfloat16)
        grad = -jnp.dot(weight, tgt_block, preferred_element_type=jnp.float32) * scale
        part = -jnp.dot(weight.T, src_block, preferred_element_type=jnp.float32) * scale
        return src_grad.at[c].add(grad), parts.at[peer].set(part.astype(jnp.bfloat16))

    src_grad, parts = lax.fori_loop(
        0, devices, one, (jnp.zeros(src_embed.shape, jnp.float32), jnp.zeros_like(blocks))
    )
    parts = lax.all_to_all(parts, AXES, split_axis=0, concat_axis=0, tiled=True)

    def back(peer, tgt_grad):
        return tgt_grad.at[theirs[peer] // (2 * clusters)].add(
            jnp.where(theirs[peer] % 2 > 0, parts[peer].astype(jnp.float32), 0.0)
        )

    tgt_grad = lax.fori_loop(0, devices, back, jnp.zeros(tgt_embed.shape, jnp.float32))
    return src_grad, tgt_grad


def shards(
    src_embed, tgt_embed, src_potential, tgt_potential, src_sizes, tgt_sizes, pair_counts, pairs
):
    devices = lax.axis_size(AXES)
    me = lax.axis_index(AXES)
    clusters, capacity, width = src_embed.shape
    fanout = pairs.shape[1]
    chunks = capacity // CHUNK
    blocks = capacity // TILE
    listed = pairs.T.reshape(fanout, devices, clusters)
    counts = pair_counts.reshape(devices, clusters)
    place = me.reshape(1).astype(jnp.int32)
    own_sizes = jnp.pad(src_sizes, (0, TILE - clusters)).reshape(1, TILE).astype(jnp.float32)
    header, matrix = make_header(
        place, listed, counts, own_sizes, tgt_potential, src_potential
    )
    header = header.reshape(devices, 2 * blocks + 2, TILE)
    header = lax.all_to_all(header, AXES, split_axis=0, concat_axis=0, tiled=True)
    header = header.astype(jnp.float32)
    first, second, third, desc, rest = schedule(
        place,
        matrix,
        tgt_sizes.reshape(devices, clusters).astype(jnp.float32),
        header,
        NEAR,
        FAR,
        PLANES,
        chunks,
    )
    homes = 2 * clusters
    pots_home = jnp.concatenate([tgt_potential, src_potential], axis=0).reshape(
        homes, blocks, TILE
    )
    pots_home = (
        jnp.pad(pots_home, ((0, 0), (0, 8 - blocks), (0, 0)))
        .astype(jnp.float32)
        .reshape(homes * 8, TILE)
    )

    def packed(_):
        tgt_rows = tgt_embed.reshape(clusters * capacity, width)
        src_rows = src_embed.reshape(clusters * capacity, width)
        near = exchange(pack(first, tgt_rows, src_rows, NEAR), devices)
        far = exchange(pass_on(second, tgt_rows, src_rows, near, FAR), devices)

        def pairs_of(phase, *extra):
            return compute(
                phase,
                desc,
                third,
                header.reshape(devices * 8, TILE),
                pots_home,
                near,
                tgt_rows,
                src_rows,
                capacity,
                devices * FAR * CHUNK,
                extra,
            )

        ret, acc_first = pairs_of(0)
        ret, ret_far, acc_second = pairs_of(1, far, ret)
        back_far = exchange(ret_far, devices)
        ret, acc_third = pairs_of(2, ret)
        ret = pass_back(second, back_far, ret, homes * chunks, FAR)
        back_near = exchange(ret, devices)
        (acc,) = fold(second, back_far, (acc_first, acc_second, acc_third), FAR, 1)
        tgt_grad, src_grad = fold(first, back_near, (acc,), NEAR, 2)
        return src_grad.reshape(src_embed.shape), tgt_grad.reshape(tgt_embed.shape)

    def unpacked(_):
        mine = lax.dynamic_index_in_dim(matrix, me, 0, keepdims=False)
        theirs = lax.dynamic_index_in_dim(matrix, me, 1, keepdims=False)
        return whole_blocks(
            src_embed, tgt_embed, src_potential, header, src_sizes, tgt_sizes, mine, theirs
        )

    return lax.cond(rest[0, 0] == 0.0, packed, unpacked, 0)


def solution(mesh):
    placed = (
        P(AXES, None, None),
        P(AXES, None, None),
        P(AXES, None),
        P(AXES, None),
        P(AXES),
        P(),
        P(),
        P(),
    )
    return jax.shard_map(
        shards,
        mesh=mesh,
        in_specs=placed,
        out_specs=(P(AXES, None, None), P(AXES, None, None)),
        check_vma=False,
    )
```

```python
import functools
import math

import jax
import jax.numpy as jnp
from jax import lax
from jax.experimental import pallas as pl
from jax.experimental.pallas import tpu as pltpu
from jax.sharding import PartitionSpec as P

AXES = ("gx", "gy")
CHUNK = 16
TILE = 128
VMEM_BYTES = 60 * 1024 * 1024
DEAD = -1e30
NEAR = 8
FAR = 4
PLANES = 128
ROUNDS = 4
STEP = 0.3
UNROLL = 1
epsilon = 0.5


def _params():
    return pltpu.CompilerParams(vmem_limit_bytes=VMEM_BYTES)


def _any():
    return pl.BlockSpec(memory_space=pl.ANY)


def _vmem():
    return pl.BlockSpec(memory_space=pltpu.VMEM)


def _smem():
    return pl.BlockSpec(memory_space=pltpu.SMEM)


def _rows(chunk):
    return pl.ds(pl.multiple_of(chunk * CHUNK, CHUNK), CHUNK)


def slots(one, step, carry):
    for u in range(UNROLL):
        carry = one(step * UNROLL + u, carry)
    return carry


def pack_kernel(slot_chunks, table, tgt_any, src_any, out, home, sems):
    half = tgt_any.shape[0]
    first = pltpu.make_async_copy(tgt_any, home.at[pl.ds(0, half)], sems.at[0])
    second = pltpu.make_async_copy(src_any, home.at[pl.ds(half, half)], sems.at[1])
    first.start()
    second.start()
    home[pl.ds(2 * half, CHUNK), :] = jnp.zeros((CHUNK, home.shape[1]), home.dtype)
    first.wait()
    second.wait()

    def slot(peer, carry):
        for p in range(slot_chunks):
            out[_rows(peer * slot_chunks + p), :] = home[_rows(table[p, peer]), :]
        return carry

    lax.fori_loop(0, table.shape[1] // UNROLL, functools.partial(slots, slot), 0)


def pack(table, tgt_rows, src_rows, slot_chunks):
    peers = table.shape[1]
    width = tgt_rows.shape[1]
    total = peers * slot_chunks * CHUNK
    return pl.pallas_call(
        functools.partial(pack_kernel, slot_chunks),
        out_shape=jax.ShapeDtypeStruct((total, width), tgt_rows.dtype),
        in_specs=[_smem(), _any(), _any()],
        out_specs=_vmem(),
        scratch_shapes=[
            pltpu.VMEM((2 * tgt_rows.shape[0] + CHUNK, width), tgt_rows.dtype),
            pltpu.SemaphoreType.DMA((2,)),
        ],
        compiler_params=_params(),
        name="pack",
    )(table, tgt_rows, src_rows)


def side_rows(potential, live, first):
    shape = (CHUNK, potential.shape[1])
    row = lax.broadcasted_iota(jnp.int32, shape, 0)
    lane = lax.broadcasted_iota(jnp.int32, shape, 1)
    dead = jnp.where(lane < live, 0.0, DEAD)
    pot = jnp.broadcast_to(potential, shape)
    own = 0 if first else 1
    other = 1 - own
    mine = 2 if first else 3
    rows = jnp.where(row == own, pot, jnp.where(row == mine, dead, 1.0))
    rows = jnp.where(row < 4, rows, 0.0)
    return rows.astype(jnp.bfloat16)


def compute_kernel(capacity, scale, phase, far_rows, refs_in, *refs):
    desc, table, pots_in, pots_home, near_any, tgt_any, src_any = refs[:7]
    extra = refs[7:refs_in]
    if phase == 1:
        far_any, ret_before = extra
        ret_near, ret_far, acc = refs[refs_in : refs_in + 3]
    else:
        ret_near, acc = refs[refs_in : refs_in + 2]
    recv, ret, home, items, fill, sems = refs[-6:]
    width = home.shape[1]
    half = tgt_any.shape[0]
    near = near_any.shape[0]
    total = near + far_rows
    copies = [
        pltpu.make_async_copy(tgt_any, home.at[pl.ds(0, half)], sems.at[0]),
        pltpu.make_async_copy(src_any, home.at[pl.ds(half, half)], sems.at[1]),
        pltpu.make_async_copy(near_any, recv.at[pl.ds(0, near)], sems.at[2]),
    ]
    if phase == 1:
        copies += [
            pltpu.make_async_copy(far_any, recv.at[pl.ds(near, far_rows)], sems.at[3]),
            pltpu.make_async_copy(ret_before, ret.at[pl.ds(0, near)], sems.at[4]),
        ]
    if phase == 2:
        (ret_before,) = extra
        copies += [pltpu.make_async_copy(ret_before, ret.at[pl.ds(0, near)], sems.at[4])]
    for copy in copies:
        copy.start()
    recv[pl.ds(total, CHUNK), :] = jnp.zeros((CHUNK, width), recv.dtype)


    def clear(i, carry):
        at = pl.multiple_of(i * capacity, capacity)
        acc[pl.ds(at, capacity), :] = jnp.zeros((capacity, width), jnp.float32)
        return carry

    lax.fori_loop(0, acc.shape[0] // capacity, clear, 0)
    log2e = math.log2(math.e)
    to_exp = log2e / epsilon

    each = TILE // CHUNK

    def pair_of(group, at, size):
        item = items[group, jnp.minimum(at, size - 1)]
        real = at < size
        peer, kind = item // 2, item % 2
        field = kind * 4
        return (
            peer,
            kind,
            desc[field, peer],
            jnp.where(real, desc[field + 1, peer], 0),
            jnp.where(real, desc[field + 2, peer], 0),
            desc[field + 3, peer],
        )

    def some(blocks, count, pairs):
        rights, sides, lefts = [], [], []
        for peer, kind, home_id, live_moved, live_home, start in pairs:
            rights.append(
                jnp.concatenate(
                    [recv[_rows(table[start + j, peer]), :] for j in range(blocks * each)], axis=0
                )
            )
            right_pots = pots_in[pl.ds(pl.multiple_of(peer * 8, 8), 8), :]
            deep = capacity // TILE
            right_pots = jnp.where(kind == 0, right_pots[0:deep, :], right_pots[deep : 2 * deep, :])
            left_pots = pots_home[pl.ds(pl.multiple_of(home_id * 8, 8), 8), :]
            right_side = jnp.concatenate(
                [
                    side_rows(right_pots[b : b + 1, :], live_moved - b * TILE, False)
                    for b in range(blocks)
                ],
                axis=1,
            )
            left_side = [
                side_rows(left_pots[i : i + 1, :], live_home - i * TILE, True)
                for i in range(count)
            ]
            sides.append((left_side, right_side))
            at = pl.multiple_of(home_id * capacity, TILE)
            lefts.append([home[pl.ds(at + i * TILE, TILE), :] for i in range(count)])
        work = [(k, i) for i in range(count) for k in range(len(pairs))]
        sums = [
            lax.dot_general(
                sides[k][0][i],
                sides[k][1],
                (((0,), (0,)), ((), ())),
                preferred_element_type=jnp.float32,
            )
            for k, i in work
        ]
        dots = [
            lax.dot_general(
                lefts[k][i], rights[k], (((1,), (1,)), ((), ())), preferred_element_type=jnp.float32
            )
            for k, i in work
        ]
        weights = []
        for dot, total_pot in zip(dots, sums):
            plan = jnp.exp2(dot * (scale * to_exp) + (total_pot * to_exp - to_exp))
            weights.append(
                (plan * (dot * (scale / epsilon) + (1.0 - 1.0 / epsilon))).astype(jnp.bfloat16)
            )
        pieces = [
            lax.dot_general(
                weight, lefts[k][i], (((0,), (0,)), ((), ())), preferred_element_type=jnp.float32
            )
            for weight, (k, i) in zip(weights, work)
        ]
        grads = [
            jnp.dot(weight, rights[k], preferred_element_type=jnp.float32)
            for weight, (k, i) in zip(weights, work)
        ]
        for k, pair in enumerate(pairs):
            at = pl.multiple_of(pair[2] * capacity, TILE)
            for i in range(count):
                acc[pl.ds(at + i * TILE, TILE), :] += (-scale) * grads[work.index((k, i))]
            piece = functools.reduce(
                jnp.add, [pieces[work.index((k, i))] for i in range(count)]
            ) * (-scale)
            for j in range(blocks * each):
                into = table[pair[5] + j, pair[0]]
                into = jnp.where(j * CHUNK < pair[3], into, total // CHUNK)
                ret[_rows(into), :] = piece[j * CHUNK : (j + 1) * CHUNK, :].astype(ret.dtype)

    deep = capacity // TILE
    for c in range(deep * deep):
        fill[c] = 0

    fill[deep * deep] = 0

    def sort(step, carry):
        for u in range(4):
            peer = step * 4 + u
            for kind in range(2):
                group = desc[8 + kind, peer] - phase * deep * deep
                ours = (group >= 0) & (group < deep * deep)
                group = jnp.where(ours, group, deep * deep)
                at = fill[group]
                items[group, at] = peer * 2 + kind
                fill[group] = at + 1
        return carry

    lax.fori_loop(0, desc.shape[1] // 4, sort, 0)
    for copy in copies:
        copy.wait()
    for b in range(1, deep + 1):
        for c in range(1, deep + 1):
            group = (b - 1) * deep + c - 1
            size = fill[group]

            def two(k, carry, b=b, c=c, group=group, size=size):
                some(b, c, [pair_of(group, 2 * k, size), pair_of(group, 2 * k + 1, size)])
                return carry

            lax.fori_loop(0, (size + 1) // 2, two, 0)

    back = [pltpu.make_async_copy(ret.at[pl.ds(0, near)], ret_near, sems.at[7])]
    if phase == 1:
        back.append(
            pltpu.make_async_copy(ret.at[pl.ds(near, far_rows)], ret_far, sems.at[8])
        )
    for copy in back:
        copy.start()
    for copy in back:
        copy.wait()


def compute(phase, desc, table, pots_in, pots_home, near, tgt_rows, src_rows, capacity, far_rows, extra):
    width = tgt_rows.shape[1]
    scale = width ** (-0.5)
    homes = 2 * tgt_rows.shape[0]
    shapes = [jax.ShapeDtypeStruct(near.shape, near.dtype)]
    if phase == 1:
        shapes.append(jax.ShapeDtypeStruct((far_rows, width), near.dtype))
    shapes.append(jax.ShapeDtypeStruct((homes, width), jnp.float32))
    rows = near.shape[0] + far_rows + CHUNK
    groups = (capacity // TILE) ** 2 + 1
    scratch = [
        pltpu.VMEM((rows, width), near.dtype),
        pltpu.VMEM((rows, width), near.dtype),
        pltpu.VMEM((homes, width), tgt_rows.dtype),
        pltpu.SMEM((groups, 2 * desc.shape[1]), jnp.int32),
        pltpu.SMEM((groups,), jnp.int32),
        pltpu.SemaphoreType.DMA((9,)),
    ]
    work = 4 * desc.shape[1] * capacity * capacity
    return pl.pallas_call(
        functools.partial(compute_kernel, capacity, scale, phase, far_rows, 7 + len(extra)),
        out_shape=tuple(shapes),
        in_specs=[_smem(), _smem(), _vmem(), _vmem()] + [_any()] * (3 + len(extra)),
        out_specs=tuple([_any()] * (len(shapes) - 1) + [_vmem()]),
        scratch_shapes=scratch,
        compiler_params=_params(),
        cost_estimate=pl.CostEstimate(
            flops=work * width, bytes_accessed=8 * homes * width, transcendentals=work // 8
        ),
        name="pairs%d" % phase,
    )(desc, table, pots_in, pots_home, near, tgt_rows, src_rows, *extra)


def pass_on_kernel(slot_chunks, table, tgt_any, src_any, got_any, out, pool, sems):
    half = tgt_any.shape[0]
    homes = 2 * half + CHUNK
    copies = [
        pltpu.make_async_copy(tgt_any, pool.at[pl.ds(0, half)], sems.at[0]),
        pltpu.make_async_copy(src_any, pool.at[pl.ds(half, half)], sems.at[1]),
        pltpu.make_async_copy(got_any, pool.at[pl.ds(homes, got_any.shape[0])], sems.at[2]),
    ]
    for copy in copies:
        copy.start()
    pool[pl.ds(2 * half, CHUNK), :] = jnp.zeros((CHUNK, pool.shape[1]), pool.dtype)
    for copy in copies:
        copy.wait()

    def slot(peer, carry):
        for p in range(slot_chunks):
            out[_rows(peer * slot_chunks + p), :] = pool[_rows(table[p, peer]), :]
        return carry

    lax.fori_loop(0, table.shape[1] // UNROLL, functools.partial(slots, slot), 0)


def pass_on(table, tgt_rows, src_rows, got, slot_chunks):
    peers = table.shape[1]
    width = tgt_rows.shape[1]
    return pl.pallas_call(
        functools.partial(pass_on_kernel, slot_chunks),
        out_shape=jax.ShapeDtypeStruct((peers * slot_chunks * CHUNK, width), tgt_rows.dtype),
        in_specs=[_smem(), _any(), _any(), _any()],
        out_specs=_vmem(),
        scratch_shapes=[
            pltpu.VMEM((2 * tgt_rows.shape[0] + CHUNK + got.shape[0], width), tgt_rows.dtype),
            pltpu.SemaphoreType.DMA((3,)),
        ],
        compiler_params=_params(),
        name="pass_on",
    )(table, tgt_rows, src_rows, got)


def pass_back_kernel(slot_chunks, homes, table, got, ret_any, out_any, out, sems):
    rows = ret_any.shape[0]
    first = pltpu.make_async_copy(ret_any, out.at[pl.ds(0, rows)], sems.at[0])
    first.start()
    first.wait()

    def slot(peer, carry):
        ats = [table[p, peer] - (homes + 1) for p in range(slot_chunks)]
        parts = [got[_rows(peer * slot_chunks + p), :] for p in range(slot_chunks)]
        for at, part in zip(ats, parts):
            out[_rows(jnp.where(at < 0, rows // CHUNK, at)), :] = part
        return carry

    lax.fori_loop(0, table.shape[1] // UNROLL, functools.partial(slots, slot), 0)
    second = pltpu.make_async_copy(out.at[pl.ds(0, rows)], out_any, sems.at[1])
    second.start()
    second.wait()


def pass_back(table, got, ret, homes, slot_chunks):
    rows, width = ret.shape
    return pl.pallas_call(
        functools.partial(pass_back_kernel, slot_chunks, homes),
        out_shape=jax.ShapeDtypeStruct(ret.shape, ret.dtype),
        in_specs=[_smem(), _vmem(), _any()],
        out_specs=_any(),
        scratch_shapes=[
            pltpu.VMEM((rows + CHUNK, width), ret.dtype),
            pltpu.SemaphoreType.DMA((2,)),
        ],
        compiler_params=_params(),
        name="pass_back",
    )(table, got, ret)


def fold_kernel(slot_chunks, bases, table, got, *refs):
    accs, outs, (even, odd, base, sems) = refs[:bases], refs[bases:-4], refs[-4:]
    homes = accs[0].shape[0]
    width = accs[0].shape[1]
    first = pltpu.make_async_copy(accs[0], base, sems.at[0])
    first.start()
    for k in range(1, bases):
        sums = (even, odd)[k - 1].at[pl.ds(0, homes)]
        pltpu.make_async_copy(accs[k], sums, sems.at[17 + k]).start()
    for sums in (even, odd):
        sums[pl.ds(homes, CHUNK), :] = jnp.zeros((CHUNK, width), jnp.float32)

    def clear(i, carry):
        at = pl.ds(pl.multiple_of(i * 8 * CHUNK, 8 * CHUNK), 8 * CHUNK)
        even[at, :] = jnp.zeros((8 * CHUNK, even.shape[1]), jnp.float32)
        odd[at, :] = jnp.zeros((8 * CHUNK, odd.shape[1]), jnp.float32)
        return carry

    if bases == 1:
        lax.fori_loop(0, homes // (8 * CHUNK), clear, 0)
    for k in range(1, bases):
        sums = (even, odd)[k - 1].at[pl.ds(0, homes)]
        pltpu.make_async_copy(accs[k], sums, sems.at[17 + k]).wait()

    def slot(peer, carry):
        ats = [
            _rows(jnp.minimum(table[p, peer], homes // CHUNK)) for p in range(slot_chunks)
        ]
        parts = [
            got[_rows(peer * slot_chunks + p), :].astype(jnp.float32) for p in range(slot_chunks)
        ]
        for p in range(0, slot_chunks, 2):
            one = even[ats[p], :] + parts[p]
            two = odd[ats[p + 1], :] + parts[p + 1]
            even[ats[p], :] = one
            odd[ats[p + 1], :] = two
        return carry

    lax.fori_loop(0, table.shape[1] // UNROLL, functools.partial(slots, slot), 0)
    first.wait()
    pieces = 16
    share = homes // pieces
    per_out = pieces // len(outs)
    copies = []
    for k in range(pieces):

        def join(i, carry, k=k):
            at = pl.ds(pl.multiple_of(k * share + i * 8 * CHUNK, 8 * CHUNK), 8 * CHUNK)
            base[at, :] = base[at, :] + (even[at, :] + odd[at, :])
            return carry

        lax.fori_loop(0, share // (8 * CHUNK), join, 0)
        out = outs[k // per_out]
        into = out.at[pl.ds((k % per_out) * share, share)]
        copies.append(
            pltpu.make_async_copy(base.at[pl.ds(k * share, share)], into, sems.at[k + 1])
        )
        copies[-1].start()
    for copy in copies:
        copy.wait()


def fold(table, got, accs, slot_chunks, parts):
    homes, width = accs[0].shape
    result = jax.ShapeDtypeStruct((homes // parts, width), jnp.float32)
    return pl.pallas_call(
        functools.partial(fold_kernel, slot_chunks, len(accs)),
        out_shape=(result,) * parts,
        in_specs=[_smem(), _vmem()] + [_any()] * len(accs),
        out_specs=(_any(),) * parts,
        scratch_shapes=[
            pltpu.VMEM((homes + CHUNK, width), jnp.float32),
            pltpu.VMEM((homes + CHUNK, width), jnp.float32),
            pltpu.VMEM((homes, width), jnp.float32),
            pltpu.SemaphoreType.DMA((20,)),
        ],
        compiler_params=_params(),
        cost_estimate=pl.CostEstimate(
            flops=homes * width, bytes_accessed=8 * homes * width, transcendentals=0
        ),
        name="fold%d" % parts,
    )(table, got, *accs)


def exchange(blocks, devices):
    shaped = blocks.reshape(devices, -1, blocks.shape[-1])
    got = lax.all_to_all(shaped, AXES, split_axis=0, concat_axis=0, tiled=True)
    return got.reshape(blocks.shape)


def sched_kernel(
    r1,
    r2,
    planes,
    clusters,
    depth,
    me_ref,
    code_ref,
    sizes_ref,
    header_ref,
    t1,
    t2,
    t3,
    desc,
    rest,
    moves,
):
    n = code_ref.shape[0]
    me = me_ref[0]
    last = n - 1
    chunks = clusters * depth
    row = lax.broadcasted_iota(jnp.int32, (n, n), 0)
    col = lax.broadcasted_iota(jnp.int32, (n, n), 1)
    direct = float(r1 + r2)
    code = code_ref[...]
    used = (code & 1).astype(jnp.float32)
    picked = (code // 2) & (clusters - 1)
    local = code // (2 * clusters)
    filler = jnp.zeros((n, n - clusters), jnp.float32)
    by_tgt = jnp.concatenate([sizes_ref[...], filler], axis=1).T
    every = header_ref[:, 6, :] * float(CHUNK) + header_ref[:, 7, :]
    by_src = every.T
    tgt_live = jnp.zeros((n, n), jnp.float32)
    src_live = jnp.zeros((n, n), jnp.float32)
    picked_t = picked.astype(jnp.float32).T
    for c in range(clusters):
        tgt_live = jnp.where(local == c, by_tgt[c : c + 1, :], tgt_live)
        src_live = jnp.where(picked_t == float(c), by_src[c : c + 1, :], src_live)
    src_live = src_live.T

    def ceil_chunks(rows):
        return jnp.floor((rows + (CHUNK - 1.0)) * (1.0 / CHUNK))

    tc = ceil_chunks(tgt_live) * used
    sc = ceil_chunks(src_live) * used
    tct, sct = tc.T, sc.T

    def cost(count, price):
        return price * (
            count + jnp.maximum(count - r1, 0.0) + jnp.maximum(count - direct, 0.0)
        )

    def choose(price):
        back = price.T
        src_tgt = cost(sc + tct, price)
        src_src = cost(sc, price) + cost(sct, back)
        tgt_tgt = cost(tct, price) + cost(tc, back)
        tgt_src = cost(tc + sct, back)
        best = jnp.minimum(jnp.minimum(src_tgt, src_src), jnp.minimum(tgt_tgt, tgt_src))
        src_first = (src_tgt == best) | (src_src == best)
        first = jnp.where(src_first, 0.0, 1.0)
        second = jnp.where(
            src_tgt == best,
            1.0,
            jnp.where(src_src == best, 0.0, jnp.where(tgt_tgt == best, 1.0, 0.0)),
        )
        tgt_moves = jnp.where(row < col, first, second.T)
        tm = tc * tgt_moves
        return tgt_moves, tm, tm.T + sc * (1.0 - tgt_moves)

    def update(_, price):
        load = choose(price)[2]
        sent = jnp.sum(load, axis=1, keepdims=True)
        got = jnp.sum(load, axis=0, keepdims=True)
        mean = jnp.maximum(jnp.sum(got, axis=1, keepdims=True) / n, 1.0)
        return price + STEP * (sent / mean - 1.0) + STEP * (got / mean - 1.0)

    prices = lax.fori_loop(0, ROUNDS, update, jnp.ones_like(tc))
    tgt_moves, tm, load = choose(prices)
    tmt = tm.T
    d1 = jnp.minimum(load, float(r1))
    d2 = jnp.minimum(load - d1, float(r2))
    d12 = d1 + d2
    slack1 = r1 - d1
    slack2 = r2 - d2
    bit = 1
    while bit < n:
        slack1 = jnp.where((row & bit) > 0, pltpu.roll(slack1, n - bit, 1), slack1)
        slack2 = jnp.where((col & bit) > 0, pltpu.roll(slack2, n - bit, 0), slack2)
        bit *= 2
    excess = load - d12
    group = 8

    def more(state):
        return (state[0] < planes) & (state[1] > 0.0)

    def step(state):
        at, _, excess, slack1, slack2 = state
        for k in range(group):
            x = jnp.minimum(jnp.minimum(excess, slack1), slack2)
            moves[at + k] = x
            excess = excess - x
            slack1 = pltpu.roll(slack1 - x, n - 1, 1)
            slack2 = pltpu.roll(slack2 - x, n - 1, 0)
        return at + group, jnp.sum(excess), excess, slack1, slack2

    count, left, _, _, _ = lax.while_loop(
        more, step, (jnp.int32(0), jnp.sum(excess), excess, slack1, slack2)
    )

    def mine(value):
        return jnp.sum(jnp.where(row == me, value, 0.0), axis=0, keepdims=True)

    d1r, d2r, d12r = mine(d1), mine(d2), mine(d12)
    d1c, d2c, d12c = mine(d1.T), mine(d2.T), mine(d12.T)
    tn = mine(tmt)
    local_t = local.astype(jnp.float32).T
    home_row = clusters + mine(picked.astype(jnp.float32))
    home_col = mine(local_t)
    tb = home_col * depth
    sb = home_row * depth - tn
    negate = jnp.where(row == ((n - col) & last), 1.0, 0.0).astype(jnp.bfloat16)
    p1n = jnp.dot(
        jnp.broadcast_to(d1c, (16, n)).astype(jnp.bfloat16),
        negate,
        preferred_element_type=jnp.float32,
    )[0:1, :]
    homes = 2.0 * chunks
    first_n = float(n * r1)
    total = float(n * (r1 + r2))
    lane = lax.broadcasted_iota(jnp.int32, (1, n), 1)
    lane_f = lane.astype(jnp.float32)

    def iota_f(rows):
        return lax.broadcasted_iota(jnp.int32, (rows, n), 0).astype(jnp.float32)

    p1, p2, p3 = iota_f(t1.shape[0]), iota_f(t2.shape[0]), iota_f(t3.shape[0])

    def home_of(q, tn, tb, sb):
        return jnp.where(q < tn, tb + q, sb + q)

    v1 = jnp.where(p1 < d1r, home_of(p1, tn, tb, sb), homes)
    v2 = jnp.where(p2 < d2r, home_of(p2 + d1r, tn, tb, sb), homes)
    v3 = jnp.where(
        p3 < d1c,
        lane_f * r1 + p3,
        jnp.where(p3 < d12c, first_n + lane_f * r2 + p3 - d1c, total),
    )
    pick = jnp.where(
        lax.broadcasted_iota(jnp.int32, (16, n), 1) == me, 1.0, 0.0
    ).astype(jnp.bfloat16)

    spread = (row + col - me) & last

    def extract(r, state):
        v1, v2, v3, qa, p1a, qb, p2b, p1n, p2c = state
        x = moves[r]
        xa = moves[r, pl.ds(me, 1), :]
        xb = lax.dot_general(
            pick, x.astype(jnp.bfloat16), (((1,), (1,)), ((), ())),
            preferred_element_type=jnp.float32,
        )[0:1, :]
        xc = jnp.sum(jnp.where(spread == ((n - r) & last), x, 0.0), axis=0, keepdims=True)
        ahead = (me + r) & last
        back = (n - ahead) & last
        stacked = jnp.concatenate([xa, qa, tn, tb, sb, xa, xa, xa], axis=0)
        turned = pltpu.roll(stacked, ahead, 1)
        xa_c, qa_c = turned[0:1, :], turned[1:2, :]
        at = p1 - p1a
        v1 = jnp.where(
            (at >= 0.0) & (at < xa_c),
            home_of(qa_c + at, turned[2:3, :], turned[3:4, :], turned[4:5, :]),
            v1,
        )
        p1a = p1a + xa_c
        qa = qa + xa
        forth = (me - r) & last
        p1b = pltpu.roll(jnp.broadcast_to(p1n, (8, n)), forth, 1)[0:1, :]
        at = p2 - p2c
        origin = ((me - lane - r) & last).astype(jnp.float32)
        v2 = jnp.where((at >= 0.0) & (at < xc), homes + 1.0 + origin * r1 + p1b + at, v2)
        p2c = p2c + xc
        p1n = p1n + pltpu.roll(jnp.broadcast_to(xc, (8, n)), (n - forth) & last, 1)[0:1, :]
        p2a = pltpu.roll(jnp.broadcast_to(p2b, (8, n)), back, 1)[0:1, :]
        via = ((lane + me + r) & last).astype(jnp.float32)
        at = p3 - qb
        v3 = jnp.where((at >= 0.0) & (at < xb), first_n + via * r2 + p2a + at, v3)
        p2b = p2b + pltpu.roll(jnp.broadcast_to(xb, (8, n)), ahead, 1)[0:1, :]
        qb = qb + xb
        return v1, v2, v3, qa, p1a, qb, p2b, p1n, p2c

    def several(k, state):
        for u in range(group // 2):
            state = extract(k * (group // 2) + u, state)
        return state

    v1, v2, v3 = lax.fori_loop(
        0, count // (group // 2), several, (v1, v2, v3, d12r, d1r, d12c, d2c, p1n, d2r)
    )[:3]
    t1[...] = v1.astype(jnp.int32)
    t2[...] = v2.astype(jnp.int32)
    t3[...] = v3.astype(jnp.int32)
    moves_here = mine(used * tgt_moves) > 0.0
    moves_there = mine((used * (1.0 - tgt_moves)).T) > 0.0
    tgt_end = mine(tm)
    src_rows = mine(src_live.T)
    src_end = tgt_end + ceil_chunks(src_rows)
    early = ((lane & 1) * 2).astype(jnp.float32)
    deep = depth * CHUNK // TILE

    def ceil_tiles(rows):
        return jnp.floor((rows + (TILE - 1.0)) * (1.0 / TILE))

    def group_of(active, end, moved, home):
        phase = jnp.where(end > r1, 1.0, early)
        group = (phase * deep + ceil_tiles(moved) - 1.0) * deep + ceil_tiles(home) - 1.0
        return jnp.where(active, group, -1.0)

    tgt_rows, own_rows, back_rows = mine(tgt_live), mine(src_live), mine(tgt_live.T)
    fields = [
        jnp.where(moves_here, home_row, -1.0),
        tgt_rows,
        own_rows,
        jnp.zeros_like(early),
        jnp.where(moves_there, home_col, -1.0),
        src_rows,
        back_rows,
        tgt_end,
        group_of(moves_here, tgt_end, tgt_rows, own_rows),
        group_of(moves_there, src_end, src_rows, back_rows),
    ]
    for k, field in enumerate(fields):
        desc[k : k + 1, :] = field.astype(jnp.int32)
    rest[...] = jnp.broadcast_to(left, rest.shape)


def header_kernel(me_ref, listed_ref, counts_ref, sizes_ref, tgt_ref, src_ref, out, matrix):
    fanout, n, clusters = listed_ref.shape
    me = me_ref[0]
    row = lax.broadcasted_iota(jnp.int32, (n, n), 0)
    row_f = row.astype(jnp.float32)
    filler = jnp.zeros((n, n - clusters), jnp.float32)

    def turn(values):
        return jnp.concatenate([values.astype(jnp.float32), filler], axis=1).T

    counts = turn(counts_ref[...])
    found = jnp.zeros((n, n), jnp.float32)
    for k in range(fanout):
        listed = turn(listed_ref[k])
        owner = jnp.floor(listed * (1.0 / clusters))
        entry = 1.0 + 2.0 * row_f + (2.0 * clusters) * (listed - owner * clusters)
        entry = jnp.where(counts > float(k), entry, 0.0)
        for c in range(clusters):
            found = found + jnp.where(row_f == owner[c : c + 1, :], entry[c : c + 1, :], 0.0)
    code = found.T.astype(jnp.int32)
    matrix[...] = code

    def mine(value):
        return jnp.sum(jnp.where(row == me, value, 0.0), axis=0, keepdims=True)

    picked = mine(((code // 2) & (clusters - 1)).astype(jnp.float32))
    local = mine((code // (2 * clusters)).astype(jnp.float32).T)
    cluster = lax.broadcasted_iota(jnp.int32, (clusters, n), 0).astype(jnp.float32)
    width = tgt_ref.shape[1]
    at = 0
    for wanted, ref in ((local, tgt_ref), (picked, src_ref)):
        chosen = jnp.where(cluster == wanted, 1.0, 0.0).astype(jnp.bfloat16)
        rows = lax.dot_general(
            chosen, ref[...], (((0,), (0,)), ((), ())), preferred_element_type=jnp.float32
        )
        out[:, at : at + width] = rows.astype(out.dtype)
        at += width
    high = jnp.floor(sizes_ref[...] * (1.0 / CHUNK))
    low = sizes_ref[...] - high * CHUNK
    for part in (high, low):
        out[:, at : at + TILE] = jnp.broadcast_to(part, (n, TILE)).astype(out.dtype)
        at += TILE


def make_header(me, listed, counts, sizes, tgt_potential, src_potential):
    n = listed.shape[1]
    capacity = tgt_potential.shape[1]
    return pl.pallas_call(
        header_kernel,
        out_shape=(
            jax.ShapeDtypeStruct((n, 2 * capacity + 2 * TILE), tgt_potential.dtype),
            jax.ShapeDtypeStruct((n, n), jnp.int32),
        ),
        in_specs=[_smem(), _vmem(), _vmem(), _vmem(), _vmem(), _vmem()],
        out_specs=(_vmem(), _vmem()),
        compiler_params=_params(),
        name="header",
    )(me, listed, counts, sizes, tgt_potential, src_potential)


def schedule(me, code, sizes, header, r1, r2, planes, depth):
    n, clusters = sizes.shape

    def ints(rows):
        return jax.ShapeDtypeStruct((rows, n), jnp.int32)

    return pl.pallas_call(
        functools.partial(sched_kernel, r1, r2, planes, clusters, depth),
        out_shape=(
            ints((r1 + 7) // 8 * 8),
            ints((r2 + 7) // 8 * 8),
            ints(2 * depth),
            ints(10),
            jax.ShapeDtypeStruct((1, n), jnp.float32),
        ),
        in_specs=[_smem(), _vmem(), _vmem(), _vmem()],
        out_specs=(_vmem(),) * 5,
        scratch_shapes=[pltpu.VMEM((planes, n, n), jnp.float32)],
        compiler_params=_params(),
        name="plan",
    )(me, code, sizes, header)


def whole_blocks(
    src_embed, tgt_embed, src_potential, header, src_sizes, tgt_sizes, mine, theirs
):
    devices = mine.shape[0]
    clusters, capacity, width = src_embed.shape
    scale = width ** (-0.5)
    blocks = jnp.take(tgt_embed, theirs // (2 * clusters), axis=0)
    blocks = lax.all_to_all(blocks, AXES, split_axis=0, concat_axis=0, tiled=True)
    row_ids = jnp.arange(capacity, dtype=jnp.int32)

    def one(peer, carry):
        src_grad, parts = carry
        c = (mine[peer] // 2) % clusters
        t = peer * clusters + mine[peer] // (2 * clusters)
        src_block, tgt_block = src_embed[c], blocks[peer]
        right = header[peer, : capacity // TILE].reshape(capacity)
        dots = jnp.dot(src_block, tgt_block.T, preferred_element_type=jnp.float32) * scale
        plan = jnp.exp(
            (src_potential[c].astype(jnp.float32)[:, None] + right[None, :] - (1.0 - dots))
            / epsilon
        )
        live = (row_ids[:, None] < src_sizes[c]) & (row_ids[None, :] < tgt_sizes[t])
        live = live & (mine[peer] % 2 > 0)
        weight = jnp.where(live, plan * (1.0 - (1.0 - dots) / epsilon), 0.0).astype(jnp.bfloat16)
        grad = -jnp.dot(weight, tgt_block, preferred_element_type=jnp.float32) * scale
        part = -jnp.dot(weight.T, src_block, preferred_element_type=jnp.float32) * scale
        return src_grad.at[c].add(grad), parts.at[peer].set(part.astype(jnp.bfloat16))

    src_grad, parts = lax.fori_loop(
        0, devices, one, (jnp.zeros(src_embed.shape, jnp.float32), jnp.zeros_like(blocks))
    )
    parts = lax.all_to_all(parts, AXES, split_axis=0, concat_axis=0, tiled=True)

    def back(peer, tgt_grad):
        return tgt_grad.at[theirs[peer] // (2 * clusters)].add(
            jnp.where(theirs[peer] % 2 > 0, parts[peer].astype(jnp.float32), 0.0)
        )

    tgt_grad = lax.fori_loop(0, devices, back, jnp.zeros(tgt_embed.shape, jnp.float32))
    return src_grad, tgt_grad


def shards(
    src_embed, tgt_embed, src_potential, tgt_potential, src_sizes, tgt_sizes, pair_counts, pairs
):
    devices = lax.axis_size(AXES)
    me = lax.axis_index(AXES)
    clusters, capacity, width = src_embed.shape
    fanout = pairs.shape[1]
    chunks = capacity // CHUNK
    blocks = capacity // TILE
    listed = pairs.T.reshape(fanout, devices, clusters)
    counts = pair_counts.reshape(devices, clusters)
    place = me.reshape(1).astype(jnp.int32)
    own_sizes = jnp.pad(src_sizes, (0, TILE - clusters)).reshape(1, TILE).astype(jnp.float32)
    header, matrix = make_header(
        place, listed, counts, own_sizes, tgt_potential, src_potential
    )
    header = header.reshape(devices, 2 * blocks + 2, TILE)
    header = lax.all_to_all(header, AXES, split_axis=0, concat_axis=0, tiled=True)
    header = header.astype(jnp.float32)
    first, second, third, desc, rest = schedule(
        place,
        matrix,
        tgt_sizes.reshape(devices, clusters).astype(jnp.float32),
        header,
        NEAR,
        FAR,
        PLANES,
        chunks,
    )
    homes = 2 * clusters
    pots_home = jnp.concatenate([tgt_potential, src_potential], axis=0).reshape(
        homes, blocks, TILE
    )
    pots_home = (
        jnp.pad(pots_home, ((0, 0), (0, 8 - blocks), (0, 0)))
        .astype(jnp.float32)
        .reshape(homes * 8, TILE)
    )

    def packed(_):
        tgt_rows = tgt_embed.reshape(clusters * capacity, width)
        src_rows = src_embed.reshape(clusters * capacity, width)
        near = exchange(pack(first, tgt_rows, src_rows, NEAR), devices)
        far = exchange(pass_on(second, tgt_rows, src_rows, near, FAR), devices)

        def pairs_of(phase, *extra):
            return compute(
                phase,
                desc,
                third,
                header.reshape(devices * 8, TILE),
                pots_home,
                near,
                tgt_rows,
                src_rows,
                capacity,
                devices * FAR * CHUNK,
                extra,
            )

        ret, acc_first = pairs_of(0)
        ret, ret_far, acc_second = pairs_of(1, far, ret)
        back_far = exchange(ret_far, devices)
        ret, acc_third = pairs_of(2, ret)
        ret = pass_back(second, back_far, ret, homes * chunks, FAR)
        back_near = exchange(ret, devices)
        (acc,) = fold(second, back_far, (acc_first, acc_second, acc_third), FAR, 1)
        tgt_grad, src_grad = fold(first, back_near, (acc,), NEAR, 2)
        return src_grad.reshape(src_embed.shape), tgt_grad.reshape(tgt_embed.shape)

    def unpacked(_):
        mine = lax.dynamic_index_in_dim(matrix, me, 0, keepdims=False)
        theirs = lax.dynamic_index_in_dim(matrix, me, 1, keepdims=False)
        return whole_blocks(
            src_embed, tgt_embed, src_potential, header, src_sizes, tgt_sizes, mine, theirs
        )

    return lax.cond(rest[0, 0] == 0.0, packed, unpacked, 0)


def solution(mesh):
    placed = (
        P(AXES, None, None),
        P(AXES, None, None),
        P(AXES, None),
        P(AXES, None),
        P(AXES),
        P(),
        P(),
        P(),
    )
    return jax.shard_map(
        shards,
        mesh=mesh,
        in_specs=placed,
        out_specs=(P(AXES, None, None), P(AXES, None, None)),
        check_vma=False,
    )
```
